512 devices in a mesh: ocx: 16 (over z), ocy: 4 (over x), ml: 8 (over y, core).
Axes of the slice: x: 4, y: 4, z: 16, core: 2. Of those that a mesh axis runs over, the one named last changes fastest.
Arguments:
- tracer: float32 [75, 64, 4096], P(None, 'ocx', ('ocy', 'ml')), may hold values from -4 to 4
- east_velocity: float32 [75, 64, 4096], P(None, 'ocx', ('ocy', 'ml')), may hold values from -0.15 to 0.15
- north_velocity: float32 [75, 64, 4096], P(None, 'ocx', ('ocy', 'ml')), may hold values from -0.15 to 0.15
- target_increment: bfloat16 [75, 64, 4096], P(None, 'ocx', ('ocy', 'ml')), may hold values from -21 to 21
- depth_levels: int32 [64, 4096], P('ocx', ('ocy', 'ml')), may hold values from 0 to 75, as said below
- relay_slots: int32 [16, 32, 32, 12], P('ocx', ('ocy', 'ml')), may hold values from 0 to 512, as said below
- closure_w1: bfloat16 [225, 1024], replicated, may hold values from -0.375 to 0.375
- closure_b1: float32 [1024], replicated, may hold values from -3 to 3
- closure_w2: bfloat16 [1024, 75], replicated, may hold values from -0.1875 to 0.1875
- closure_b2: float32 [75], replicated, may hold values from -3 to 3
Outputs:
- tracer_out: float32 [75, 64, 4096], P(None, 'ocx', ('ocy', 'ml'))
- misfit_out: bfloat16 [75, 64, 4096], P(None, 'ocx', ('ocy', 'ml'))
- grad_w1: float32 [225, 1024], replicated
- grad_b1: float32 [1024], replicated
- grad_w2: float32 [1024, 75], replicated
- grad_b2: float32 [75], replicated
The draws below stay inside these ranges and needn't reach their ends.
Inputs may be any that keep to these rules, and one draw needn't show every extreme that they name: A column has depth_levels > 0 exactly when relay_slots names it. relay_slots[a, b, r, q] names a column of tile (a, b), the cells with longitude a * 4 to a * 4 + 3 and latitude b * 128 to b * 128 + 127, numbered i * 128 + j inside the tile, whose closure is computed by shard r of the tiles with the same a; the value 4 * 128 marks an unused entry. No column is named twice. For every a, one shard r receives 12 named columns from every tile b.
All inputs are finite; a program needn't handle non-finite values.
Results may differ from the reference program's by a relative error of at most 0.0044.
Values may be sent and summed in bfloat16 or wider, within the bound.
A program may use at most 64 MiB of HBM per device.

```python
import jax
import jax.numpy as jnp
from jax import lax

LEV = 75
HID = 1024
STEPS = 3
CX = 4
CY = 128
NX = 64
GROUP = 32
NY = 4096
CAP = 12
COLUMNS = 262144


def relay_layout(key):
    tiles_x = NX // CX
    cells = CX * CY
    n_tiles = tiles_x * GROUP
    key_perm, key_count, key_target, key_level = jax.random.split(key, 4)
    shuffled = jax.vmap(lambda subkey: jax.random.permutation(subkey, cells - 1))(jax.random.split(key_perm, n_tiles)).astype(jnp.int32) + 1
    order_cols = jnp.concatenate([jnp.zeros((n_tiles, 1), jnp.int32), shuffled], axis=1)
    wet_count = jax.random.randint(key_count, (n_tiles,), cells // 4, 3 * cells // 4 + 1).astype(jnp.int32)
    full_shard = jnp.repeat(jax.random.randint(key_target, (tiles_x,), 0, GROUP).astype(jnp.int32), GROUP)
    member = jnp.tile(jnp.arange(GROUP, dtype=jnp.int32), tiles_x)
    shards = jnp.arange(GROUP, dtype=jnp.int32)[None, :]
    order_rank = jnp.mod(shards - full_shard[:, None] - 1, GROUP)
    rank = jnp.mod(order_rank + member[:, None], GROUP - 1)
    remain = wet_count - CAP
    base = remain // (GROUP - 1)
    extra = remain % (GROUP - 1)
    counts = jnp.where(shards == full_shard[:, None], CAP, base[:, None] + (rank < extra[:, None]).astype(jnp.int32))
    offsets = jnp.cumsum(counts, axis=1) - counts
    entry = jnp.arange(CAP, dtype=jnp.int32)[None, None, :]
    where_pos = jnp.minimum(offsets[:, :, None] + entry, cells - 1).reshape(n_tiles, GROUP * CAP)
    picked = jnp.take_along_axis(order_cols, where_pos, axis=1).reshape(n_tiles, GROUP, CAP)
    slots = jnp.where(entry < counts[:, :, None], picked, cells).astype(jnp.int32)
    drawn_levels = jax.random.randint(key_level, (n_tiles, cells), 1, LEV + 1).astype(jnp.int32)
    position = jnp.arange(cells, dtype=jnp.int32)[None, :]
    drawn_levels = jnp.where(position == 0, LEV, jnp.where(position == 1, 1, drawn_levels))
    by_position = jnp.where(position < wet_count[:, None], drawn_levels, 0).astype(jnp.int32)
    depth_tiles = jax.vmap(lambda order_row, value_row: jnp.zeros((cells,), jnp.int32).at[order_row].set(value_row))(order_cols, by_position)
    depth_grid = depth_tiles.reshape(tiles_x, GROUP, CX, CY).transpose(0, 2, 1, 3).reshape(NX, NY)
    return (slots.reshape(tiles_x, GROUP, GROUP, CAP), depth_grid)


def draw_depth_levels(key, part):
    return relay_layout(key)[1]


def draw_relay_slots(key, part):
    return relay_layout(key)[0]


def smooth_target(key, gain_lo, gain_hi, noise):
    key_gain, key_rough = jax.random.split(key, 2)
    level_gain = jax.random.uniform(key_gain, (LEV, 1, 1), jnp.float32, gain_lo, gain_hi)
    place = (jnp.arange(NX, dtype=jnp.float32) + 0.5) / NX
    swing = jnp.cos(2.0 * jnp.pi * place)[None, :, None]
    rough = jax.random.uniform(key_rough, (LEV, NX, NY), jnp.float32, -1.0, 1.0) * noise
    return 16.0 * level_gain * swing + rough


def draw_target_increment(key, part):
    key = jax.random.fold_in(key, 7)
    key_a, key_b = jax.random.split(key)
    values = smooth_target(key_a, 0.6, 1.2, 0.0) + jnp.clip(jax.random.normal(key_b, (LEV, NX, NY), jnp.float32) * 0.5, -1.5, 1.5)
    return values.astype(jnp.bfloat16)


def shard_levels(stream_key, extent, cuts, low, largest):
    loudness, own = 1.0, jax.random.fold_in(stream_key, 6)
    for dim, shards_of in cuts:
        draws = jnp.exp(jax.random.uniform(jax.random.fold_in(own, dim), (shards_of,), jnp.float32, low / len(cuts), largest / len(cuts)))
        loudness = loudness * jnp.repeat(draws, extent[dim] // shards_of).reshape([-1 if axis == dim else 1 for axis in range(len(extent))])
    return loudness


def bell_draw(stream_key, shape, scale, bound, cuts=(), kind=jnp.bfloat16):
    entries = scale * jax.random.normal(stream_key, shape, jnp.float32)
    if cuts:
        entries = entries * shard_levels(stream_key, shape, cuts, -0.22, 0.18)
    return jnp.clip(entries, -bound, bound).astype(kind)


def setup_inputs(seed: int = 0) -> dict:
    arg_keys = jax.random.split(jax.random.key(seed), 11)
    tracer = bell_draw(arg_keys[0], (LEV, NX, NY), 1.0, 4.0, ((1, 16), (2, 32)), jnp.float32)
    east_velocity = bell_draw(arg_keys[1], (LEV, NX, NY), 0.06, 0.15, ((1, 16), (2, 32)), jnp.float32)
    north_velocity = bell_draw(arg_keys[2], (LEV, NX, NY), 0.06, 0.15, ((1, 16), (2, 32)), jnp.float32)
    target_increment = draw_target_increment(jax.random.fold_in(arg_keys[10], 71), 0)
    depth_levels = draw_depth_levels(jax.random.fold_in(arg_keys[10], 71), 0)
    relay_slots = draw_relay_slots(jax.random.fold_in(arg_keys[10], 71), 0)
    closure_w1 = bell_draw(arg_keys[6], (3 * LEV, HID), (3 * LEV) ** -0.5, 0.375)
    closure_b1 = bell_draw(arg_keys[7], (HID,), 0.5, 3.0, (), jnp.float32)
    closure_w2 = bell_draw(arg_keys[8], (HID, LEV), HID ** -0.5, 0.1875)
    closure_b2 = bell_draw(arg_keys[9], (LEV,), 0.5, 3.0, (), jnp.float32)
    return {"tracer": tracer, "east_velocity": east_velocity, "north_velocity": north_velocity, "target_increment": target_increment, "depth_levels": depth_levels, "relay_slots": relay_slots, "closure_w1": closure_w1, "closure_b1": closure_b1, "closure_w2": closure_w2, "closure_b2": closure_b2}


KAPPA = 0.1


def transport(tracer_now, east_velocity, north_velocity, depth_levels):
    level_ids = jnp.arange(LEV, dtype=jnp.int32)[:, None, None]
    east_open = level_ids < jnp.minimum(depth_levels, jnp.roll(depth_levels, -1, axis=0))[None]
    lat_index = jnp.arange(NY, dtype=jnp.int32)
    north_open = (level_ids < jnp.minimum(depth_levels, jnp.roll(depth_levels, -1, axis=1))[None]) & (lat_index < NY - 1)[None, None, :]
    for number in range(STEPS):
        east_cell = jnp.roll(tracer_now, -1, axis=1)
        east_flux = jnp.where(east_open, jnp.maximum(east_velocity, 0.0) * tracer_now + jnp.minimum(east_velocity, 0.0) * east_cell - KAPPA * (east_cell - tracer_now), 0.0)
        north_cell = jnp.roll(tracer_now, -1, axis=2)
        north_flux = jnp.where(north_open, jnp.maximum(north_velocity, 0.0) * tracer_now + jnp.minimum(north_velocity, 0.0) * north_cell - KAPPA * (north_cell - tracer_now), 0.0)
        tracer_now = tracer_now + jnp.roll(east_flux, 1, axis=1) - east_flux + jnp.roll(north_flux, 1, axis=2) - north_flux
    return tracer_now


def closure(row_data, depth_rows, closure_w1, closure_b1, closure_w2, closure_b2, columns):
    levels_n = closure_w2.shape[1]
    inputs = row_data[:, :3 * levels_n]
    wanted = row_data[:, 3 * levels_n:].astype(jnp.float32)
    level_ids = jnp.arange(levels_n, dtype=jnp.float32)
    level_mask = (level_ids[None, :] < depth_rows.astype(jnp.float32)[:, None]).astype(jnp.float32)
    before = jnp.dot(inputs, closure_w1, preferred_element_type=jnp.float32) + closure_b1
    stash = lax.optimization_barrier(before.astype(jnp.bfloat16)).astype(jnp.float32)
    gate_sig = jax.nn.sigmoid(stash)
    hidden = (stash * gate_sig).astype(jnp.bfloat16)
    output = jnp.dot(hidden, closure_w2, preferred_element_type=jnp.float32) + closure_b2
    tendency = (output * level_mask).astype(jnp.bfloat16)
    misfit = tendency.astype(jnp.float32) - wanted
    d_output = (misfit / columns).astype(jnp.bfloat16)
    grad_w2 = jnp.dot(hidden.T, d_output, preferred_element_type=jnp.float32)
    grad_b2 = jnp.sum(d_output.astype(jnp.float32), axis=0)
    d_hidden = jnp.dot(d_output, closure_w2.T, preferred_element_type=jnp.float32)
    d_before = (d_hidden * gate_sig * (1.0 + stash * (1.0 - gate_sig))).astype(jnp.bfloat16)
    grad_w1 = jnp.dot(inputs.T, d_before, preferred_element_type=jnp.float32)
    grad_b1 = jnp.sum(d_before.astype(jnp.float32), axis=0)
    return tendency, (grad_w1, grad_b1, grad_w2, grad_b2)


def reference(tracer, east_velocity, north_velocity, target_increment, depth_levels, relay_slots, closure_w1, closure_b1, closure_w2, closure_b2):
    final = transport(tracer, east_velocity, north_velocity, depth_levels)
    tiles_x = NX // CX
    cells = CX * CY
    n_tiles = tiles_x * GROUP
    level_ids = jnp.arange(LEV, dtype=jnp.int32)[:, None, None]
    wet = level_ids < depth_levels[None]
    target_wet = jnp.where(wet, target_increment.astype(jnp.float32), 0.0)
    features = jnp.concatenate([jnp.where(wet, final, 0.0), jnp.where(wet, east_velocity, 0.0), jnp.where(wet, north_velocity, 0.0), target_wet], axis=0).astype(jnp.bfloat16)
    tiled = features.reshape(4 * LEV, tiles_x, CX, GROUP, CY).transpose(1, 3, 2, 4, 0).reshape(n_tiles, cells, 4 * LEV)
    depth_tiles = depth_levels.reshape(tiles_x, CX, GROUP, CY).transpose(0, 2, 1, 3).reshape(n_tiles, cells)
    slot_tiles = relay_slots.reshape(n_tiles, GROUP * CAP).astype(jnp.int32)

    def per_tile(running, pieces):
        tile_rows, tile_depth, tile_slots = pieces
        padded = jnp.concatenate([tile_rows, jnp.zeros((1, 4 * LEV), jnp.bfloat16)], axis=0)
        depth_pad = jnp.concatenate([tile_depth.astype(jnp.float32), jnp.zeros((1,), jnp.float32)])
        tendency, grads = closure(padded[tile_slots], depth_pad[tile_slots].astype(jnp.bfloat16), closure_w1, closure_b1, closure_w2, closure_b2, COLUMNS)
        placed = jnp.zeros((cells + 1, LEV), jnp.bfloat16).at[tile_slots].set(tendency)[:cells]
        return tuple(earlier + update for earlier, update in zip(running, grads)), placed

    start = (jnp.zeros((3 * LEV, HID), jnp.float32), jnp.zeros((HID,), jnp.float32), jnp.zeros((HID, LEV), jnp.float32), jnp.zeros((LEV,), jnp.float32))
    totals, placed = lax.scan(per_tile, start, (tiled, depth_tiles, slot_tiles))
    tendency_grid = placed.reshape(tiles_x, GROUP, CX, CY, LEV).transpose(4, 0, 2, 1, 3).reshape(LEV, NX, NY).astype(jnp.float32)
    misfit_out = (tendency_grid - target_wet).astype(jnp.bfloat16)
    return final + tendency_grid, misfit_out, totals[0], totals[1], totals[2], totals[3]
```

```python
import jax
import jax.numpy as jnp
from jax import lax
from jax.experimental import pallas as pl
from jax.experimental.pallas import tpu as pltpu
from jax.sharding import PartitionSpec as P

MESH = pl.DeviceIdType.MESH
KAPPA = 0.1
STEPS = 3
LEV = 75
PAD = 80
CX = 4
CY = 128
CELLS = CX * CY
HID = 1024
ROWS = 240
TILES = 32
NZ = 16
COLUMNS = 262144
BLK = 256
F32 = jnp.float32
BF16 = jnp.bfloat16
VMEM_LIMIT = 40 * 1024 * 1024


def place(p):
    return p // 8, p % 8


def faces(opened, speed):
    near = jnp.where(opened, jnp.maximum(speed, 0.0) + KAPPA, 0.0)
    far = jnp.where(opened, jnp.minimum(speed, 0.0) - KAPPA, 0.0)
    return near, far


def transport_kernel(
    tracer_ref, east_ref, north_ref, depth_ref, out_ref,
    cells, side, pack_n, pack_s, halo_w, halo_e, halo_s, halo_n, halo_u,
    send_sems, recv_sems,
):
    z, x, m = lax.axis_index("ocx"), lax.axis_index("ocy"), lax.axis_index("ml")
    p = x * 8 + m
    to_e = (lax.rem(z + 1, NZ), x, m)
    to_w = (lax.rem(z + NZ - 1, NZ), x, m)
    to_n = (z, *place(lax.rem(p + 1, TILES)))
    to_s = (z, *place(lax.rem(p + TILES - 1, TILES)))
    barrier = pltpu.get_barrier_semaphore()
    for target in (to_e, to_w, to_n, to_s):
        pl.semaphore_signal(barrier, inc=1, device_id=target, device_id_type=MESH)

    level = lax.broadcasted_iota(jnp.int32, (PAD, CY), 0).astype(F32)
    lane = lax.broadcasted_iota(jnp.int32, (PAD, CY), 1)
    tail = lax.broadcasted_iota(jnp.int32, (PAD - LEV, CY), 0)
    depth = [depth_ref[i : i + 1, :].astype(F32) for i in range(CX)]
    for i in range(CX):
        cells[0, i, 0:LEV, :] = tracer_ref[:, i, :]
        cells[0, i, LEV:PAD, :] = jnp.where(tail == 0, depth[i], 0.0)
    for i in range(CX):
        side[i, 0:LEV, :] = north_ref[:, i, :]
        side[i, LEV:PAD, :] = jnp.zeros((PAD - LEV, CY), F32)
    side[CX, 0:LEV, :] = east_ref[:, CX - 1, :]
    side[CX, LEV:PAD, :] = jnp.zeros((PAD - LEV, CY), F32)
    pl.semaphore_wait(barrier, 4)

    def remote(src, dst, number, target):
        copy = pltpu.make_async_remote_copy(
            src_ref=src, dst_ref=dst, send_sem=send_sems.at[number], recv_sem=recv_sems.at[number],
            device_id=target, device_id_type=MESH,
        )
        copy.start()
        return copy

    copies = [remote(side.at[CX], halo_u, 12, to_e)]
    coef = None
    for step in range(STEPS):
        rows = [cells[step, i] for i in range(CX)]
        now = [
            remote(cells.at[step, CX - 1], halo_w.at[step], 4 * step, to_e),
            remote(cells.at[step, 0], halo_e.at[step], 4 * step + 1, to_w),
        ]
        up = jnp.zeros((PAD, CY), F32)
        down = jnp.zeros((PAD, CY), F32)
        for i in range(CX):
            up = jnp.where(lane == i, pltpu.roll(rows[i], i + 1, 1), up)
            down = jnp.where(lane == i, pltpu.roll(rows[i], i, 1) if i else rows[i], down)
            if step == 0:
                up = jnp.where(lane == CX + i, pltpu.roll(side[i], CX + i + 1, 1), up)
        pack_n[step] = up
        pack_s[step] = down
        now += [
            remote(pack_n.at[step], halo_s.at[step], 4 * step + 2, to_n),
            remote(pack_s.at[step], halo_n.at[step], 4 * step + 3, to_s),
        ]
        for copy in now:
            copy.wait_recv()
        copies += now
        west, east = halo_w[step], halo_e[step]
        south_pack, north_pack = halo_s[step], halo_n[step]
        south_in = [pltpu.roll(south_pack, (CY - i) % CY, 1) if i else south_pack for i in range(CX)]
        north_in = [pltpu.roll(north_pack, CY - 1 - i, 1) for i in range(CX)]
        if step == 0:
            copies[0].wait_recv()
            deep = [west[LEV : LEV + 1, :]] + depth + [east[LEV : LEV + 1, :]]
            east_faces = []
            for i in range(CX + 1):
                speed = halo_u[...] if i == 0 else None
                if i:
                    speed = jnp.concatenate(
                        [east_ref[:, i - 1, :], jnp.zeros((PAD - LEV, CY), F32)], axis=0
                    ) if i < CX else side[CX]
                east_faces.append(faces(level < jnp.minimum(deep[i], deep[i + 1]), speed))
            coef = []
            for i in range(CX):
                here = jnp.broadcast_to(depth[i], (PAD, CY))
                there = jnp.where(
                    lane == CY - 1,
                    jnp.broadcast_to(north_in[i][LEV : LEV + 1, :], (PAD, CY)),
                    pltpu.roll(here, CY - 1, 1),
                )
                shut_n = jnp.logical_and(lane == CY - 1, p == TILES - 1)
                near_n, far_n = faces(
                    jnp.logical_and(level < jnp.minimum(here, there), jnp.logical_not(shut_n)), side[i]
                )
                below = jnp.broadcast_to(south_in[i][LEV : LEV + 1, :], (PAD, CY))
                near_b, far_b = faces(
                    jnp.logical_and(level < jnp.minimum(here, below), p != 0),
                    pltpu.roll(south_pack, CY - CX - i, 1),
                )
                near_s = jnp.where(lane == 0, near_b, pltpu.roll(near_n, 1, 1))
                far_s = jnp.where(lane == 0, far_b, pltpu.roll(far_n, 1, 1))
                near_w, far_w = east_faces[i]
                near_e, far_e = east_faces[i + 1]
                coef.append((1.0 + far_w - near_e + far_s - near_n, near_w, far_e, near_s, far_n))
        wide = [west] + rows + [east]
        for i in range(CX):
            keep, near_w, far_e, near_s, far_n = coef[i]
            south = jnp.where(lane == 0, south_in[i], pltpu.roll(rows[i], 1, 1))
            north = jnp.where(lane == CY - 1, north_in[i], pltpu.roll(rows[i], CY - 1, 1))
            value = (
                keep * rows[i] + near_w * wide[i] - far_e * wide[i + 2] + near_s * south - far_n * north
            )
            if step == STEPS - 1:
                out_ref[i] = value
            else:
                cells[step + 1, i] = value
    for copy in copies:
        copy.wait_send()


def transport(tracer, east, north, depth):
    vmem = pl.BlockSpec(memory_space=pltpu.VMEM)
    halo = pltpu.VMEM((STEPS, PAD, CY), F32)
    return pl.pallas_call(
        transport_kernel,
        out_shape=jax.ShapeDtypeStruct((CX, PAD, CY), F32),
        in_specs=[vmem] * 4,
        out_specs=vmem,
        scratch_shapes=[
            pltpu.VMEM((STEPS, CX, PAD, CY), F32),
            pltpu.VMEM((CX + 1, PAD, CY), F32),
            halo, halo, halo, halo, halo, halo,
            pltpu.VMEM((PAD, CY), F32),
            pltpu.SemaphoreType.DMA((13,)),
            pltpu.SemaphoreType.DMA((13,)),
        ],
        compiler_params=pltpu.CompilerParams(
            collective_id=0, has_side_effects=True, vmem_limit_bytes=VMEM_LIMIT
        ),
        name="transport",
    )(tracer, east, north, depth)


def dot(a, b, dims):
    return lax.dot_general(a, b, (dims, ((), ())), preferred_element_type=F32)


def closure_kernel(
    moved_ref, east_ref, north_ref, target_ref, depth_ref, w1_ref, b1_ref, w2_ref, b2_ref,
    tracer_out, misfit_out, chunks,
    feat, weights, hidden, slope, total, wanted,
):
    level = lax.broadcasted_iota(jnp.int32, (LEV, CY), 0).astype(F32)
    masks = []
    want = target_ref[...].astype(F32)
    wanted[...] = want
    for i in range(CX):
        at = slice(CY * i, CY * (i + 1))
        mask = level < depth_ref[i : i + 1, :].astype(F32)
        masks.append(mask)
        feat[0:LEV, at] = jnp.where(mask, moved_ref[i, 0:LEV, :], 0.0)
        feat[LEV : 2 * LEV, at] = jnp.where(mask, east_ref[:, i, :], 0.0)
        feat[2 * LEV : 3 * LEV, at] = jnp.where(mask, north_ref[:, i, :], 0.0)
    last = lax.broadcasted_iota(jnp.int32, (ROWS - 3 * LEV, CELLS), 0)
    feat[3 * LEV : ROWS, :] = jnp.where(last < 2, 1.0, 0.0)
    inputs = feat[...].astype(BF16)

    edge = 3 * LEV // 16 * 16
    weights[0:edge, :] = w1_ref[0:edge, :]
    bias = b1_ref[...]
    coarse = bias.astype(BF16).astype(F32)
    row = lax.broadcasted_iota(jnp.int32, (ROWS - edge, HID), 0) + edge
    final = jnp.where(row == 3 * LEV - 1, w1_ref[3 * LEV - 1 : 3 * LEV, :].astype(F32), 0.0)
    final = jnp.where(row == 3 * LEV, coarse, final)
    final = jnp.where(row == 3 * LEV + 1, bias - coarse, final)
    weights[edge:ROWS, :] = final.astype(BF16)

    acc = None
    for b in range(HID // BLK):
        at = slice(b * BLK, (b + 1) * BLK)
        before = dot(weights[:, at], inputs, ((0,), (0,)))
        stash = before.astype(BF16).astype(F32)
        gate = 0.5 * jnp.tanh(0.5 * stash) + 0.5
        act = (stash * gate).astype(BF16)
        hidden[at, :] = act
        slope[at, :] = gate * (1.0 + stash * (1.0 - gate))
        part = dot(w2_ref[at, :], act, ((0,), (0,)))
        acc = part if acc is None else acc + part
    eye = lax.broadcasted_iota(jnp.int32, (LEV, LEV), 0) == lax.broadcasted_iota(jnp.int32, (LEV, LEV), 1)
    bias2 = jnp.sum(jnp.where(eye, b2_ref[...], 0.0), axis=1, keepdims=True)
    output = acc + bias2
    total[...] = jnp.zeros((PAD, CELLS), F32)
    for i in range(CX):
        at = slice(CY * i, CY * (i + 1))
        tendency = jnp.where(masks[i], output[:, at], 0.0).astype(BF16).astype(F32)
        goal = jnp.where(masks[i], wanted[:, i, :], 0.0)
        misfit = tendency - goal
        total[0:LEV, at] = misfit * (1.0 / COLUMNS)
        tracer_out[:, i, :] = moved_ref[i, 0:LEV, :] + tendency
        wanted[:, i, :] = misfit
    misfit_out[...] = wanted[...].astype(BF16)
    d_out = total[...].astype(BF16)
    ones = jnp.ones((16, CELLS), BF16)
    bias_grad = dot(ones, d_out, ((1,), (1,)))
    spread = lax.broadcasted_iota(jnp.int32, (PAD, CY), 0) == LEV
    for b in range(HID // BLK):
        at = slice(b * BLK, (b + 1) * BLK)
        d_hidden = dot(w2_ref[at, :], d_out[0:LEV, :], ((1,), (0,)))
        d_before = (d_hidden * slope[at, :]).astype(BF16)
        g1 = dot(inputs, d_before, ((1,), (1,)))
        g2 = dot(d_out, hidden[at, :], ((1,), (1,)))
        for t in range(BLK // CY):
            lanes = slice(t * CY, (t + 1) * CY)
            first = 4 * (b * (BLK // CY) + t)
            for g in range(3):
                chunks[first + g] = g1[PAD * g : PAD * (g + 1), lanes].astype(BF16)
            last_part = g2[:, lanes]
            if first == 0:
                row = jnp.concatenate([bias_grad[0:1, :], jnp.zeros((1, CY - PAD), F32)], axis=1)
                last_part = jnp.where(spread, row, last_part)
            chunks[first + 3] = last_part.astype(BF16)


def closure(moved, east, north, target, depth, w1, b1, w2, b2):
    vmem = pl.BlockSpec(memory_space=pltpu.VMEM)
    return pl.pallas_call(
        closure_kernel,
        out_shape=(
            jax.ShapeDtypeStruct((LEV, CX, CY), F32),
            jax.ShapeDtypeStruct((LEV, CX, CY), BF16),
            jax.ShapeDtypeStruct((TILES, PAD, CY), BF16),
        ),
        in_specs=[vmem] * 9,
        out_specs=(vmem,) * 3,
        scratch_shapes=[
            pltpu.VMEM((ROWS, CELLS), F32),
            pltpu.VMEM((ROWS, HID), BF16),
            pltpu.VMEM((HID, CELLS), BF16),
            pltpu.VMEM((HID, CELLS), F32),
            pltpu.VMEM((PAD, CELLS), F32),
            pltpu.VMEM((LEV, CX, CY), F32),
        ],
        compiler_params=pltpu.CompilerParams(vmem_limit_bytes=VMEM_LIMIT),
        name="closure",
    )(moved, east, north, target, depth, w1, b1.reshape(1, HID), w2, b2.reshape(1, LEV))


def reduce_kernel(
    chunks, out_ref, landed, strips, strips_in, mine, strips_all, chunk, send_sems, recv_sems
):
    z, x, m = lax.axis_index("ocx"), lax.axis_index("ocy"), lax.axis_index("ml")
    p = x * 8 + m
    barrier = pltpu.get_barrier_semaphore()

    def member(k):
        q = lax.rem(p + k, TILES)
        return q, (z, *place(q))

    def ring(k):
        w = lax.rem(z + k, NZ)
        return w, (w, x, m)

    def greet(k, carry):
        pl.semaphore_signal(barrier, inc=1, device_id=member(k)[1], device_id_type=MESH)
        return carry

    def greet_ring(k, carry):
        pl.semaphore_signal(barrier, inc=1, device_id=ring(k)[1], device_id_type=MESH)
        return carry

    lax.fori_loop(1, TILES, greet, 0)
    lax.fori_loop(1, NZ, greet_ring, 0)
    pl.semaphore_wait(barrier, TILES + NZ - 2)

    def remote(src, dst, number, target):
        return pltpu.make_async_remote_copy(
            src_ref=src, dst_ref=dst, send_sem=send_sems.at[number], recv_sem=recv_sems.at[number],
            device_id=target, device_id_type=MESH,
        )

    def scatter(k, carry):
        q, target = member(k)
        remote(chunks.at[q], landed.at[k - 1], 0, target).start()
        return carry

    lax.fori_loop(1, TILES, scatter, 0)
    remote(landed, landed, 0, ring(1)[1]).wait_recv()
    total = chunks[p].astype(F32)
    total = lax.fori_loop(0, TILES - 1, lambda k, s: s + landed[k].astype(F32), total)
    mine[...] = total
    part = PAD // NZ
    for k in range(NZ):
        strips[k] = mine[part * k : part * (k + 1), :]

    def scatter_ring(k, carry):
        w, target = ring(k)
        remote(strips.at[w], strips_in.at[k - 1], 1, target).start()
        return carry

    lax.fori_loop(1, NZ, scatter_ring, 0)
    remote(strips_in, strips_in, 1, ring(1)[1]).wait_recv()
    strip = strips[z]
    for k in range(NZ - 1):
        strip = strip + strips_in[k]
    strips_all[NZ - 1] = strip

    def gather_ring(k, carry):
        _, target = ring(k)
        remote(strips_all.at[NZ - 1], strips_all.at[k - 1], 2, target).start()
        return carry

    lax.fori_loop(1, NZ, gather_ring, 0)
    arrived = strips_all.at[0 : NZ - 1]
    remote(arrived, arrived, 2, ring(1)[1]).wait_recv()
    for k in range(NZ):
        place_in = lax.rem(z - k + NZ - 1 + NZ, NZ)
        mine[part * k : part * (k + 1), :] = strips_all[place_in]
    chunk[...] = mine[...].astype(BF16)
    out_ref[p] = chunk[...]

    def gather(k, carry):
        _, target = member(k)
        remote(chunk, out_ref.at[p], 3, target).start()
        return carry

    lax.fori_loop(1, TILES, gather, 0)
    remote(landed, landed, 3, ring(1)[1]).wait_recv()
    remote(landed, landed, 0, ring(1)[1]).wait_send()
    remote(strips_in, strips_in, 1, ring(1)[1]).wait_send()
    remote(arrived, arrived, 2, ring(1)[1]).wait_send()
    remote(landed, landed, 3, ring(1)[1]).wait_send()


def reduce(chunks):
    vmem = pl.BlockSpec(memory_space=pltpu.VMEM)
    part = PAD // NZ
    return pl.pallas_call(
        reduce_kernel,
        out_shape=jax.ShapeDtypeStruct((TILES, PAD, CY), BF16),
        in_specs=[vmem],
        out_specs=vmem,
        scratch_shapes=[
            pltpu.VMEM((TILES - 1, PAD, CY), BF16),
            pltpu.VMEM((NZ, part, CY), F32),
            pltpu.VMEM((NZ - 1, part, CY), F32),
            pltpu.VMEM((PAD, CY), F32),
            pltpu.VMEM((NZ, part, CY), F32),
            pltpu.VMEM((PAD, CY), BF16),
            pltpu.SemaphoreType.DMA((4,)),
            pltpu.SemaphoreType.DMA((4,)),
        ],
        compiler_params=pltpu.CompilerParams(
            collective_id=1, has_side_effects=True, vmem_limit_bytes=VMEM_LIMIT
        ),
        name="reduce",
    )(chunks)


def unpack_kernel(chunks, w1_ref, b1_ref, w2_ref, b2_ref):
    for t in range(HID // CY):
        lanes = slice(t * CY, (t + 1) * CY)
        for g in range(2):
            w1_ref[PAD * g : PAD * (g + 1), lanes] = chunks[4 * t + g].astype(F32)
        third = chunks[4 * t + 2].astype(F32)
        rest = 3 * LEV - 2 * PAD
        w1_ref[2 * PAD : 3 * LEV, lanes] = third[0:rest, :]
        b1_ref[:, lanes] = third[rest : rest + 1, :]
        fourth = chunks[4 * t + 3].astype(F32)
        w2_ref[lanes, :] = jnp.transpose(fourth)[:, 0:LEV]
        if t == 0:
            b2_ref[...] = fourth[LEV : LEV + 1, 0:LEV]


def unpack(chunks):
    vmem = pl.BlockSpec(memory_space=pltpu.VMEM)
    return pl.pallas_call(
        unpack_kernel,
        out_shape=(
            jax.ShapeDtypeStruct((3 * LEV, HID), F32),
            jax.ShapeDtypeStruct((1, HID), F32),
            jax.ShapeDtypeStruct((HID, LEV), F32),
            jax.ShapeDtypeStruct((1, LEV), F32),
        ),
        in_specs=[vmem],
        out_specs=(vmem,) * 4,
        compiler_params=pltpu.CompilerParams(vmem_limit_bytes=VMEM_LIMIT),
        name="unpack",
    )(chunks)


def on_device(tracer, east, north, target, depth, slots, w1, b1, w2, b2):
    moved = transport(tracer, east, north, depth)
    tracer_out, misfit_out, chunks = closure(moved, east, north, target, depth, w1, b1, w2, b2)
    grad_w1, grad_b1, grad_w2, grad_b2 = unpack(reduce(chunks))
    return tracer_out, misfit_out, grad_w1, grad_b1.reshape(HID), grad_w2, grad_b2.reshape(LEV)


def solution(mesh):
    grid = P(None, "ocx", ("ocy", "ml"))
    return jax.shard_map(
        on_device,
        mesh=mesh,
        in_specs=(grid, grid, grid, grid, P("ocx", ("ocy", "ml")), P("ocx", ("ocy", "ml"), None, None), P(), P(), P(), P()),
        out_specs=(grid, grid, P(), P(), P(), P()),
        check_vma=False,
    )
```

```python
import jax
import jax.numpy as jnp
from jax import lax
from jax.experimental import pallas as pl
from jax.experimental.pallas import tpu as pltpu
from jax.sharding import PartitionSpec as P

MESH = pl.DeviceIdType.MESH
KAPPA = 0.1
STEPS = 3
LEV = 75
PAD = 80
CX = 4
CY = 128
CELLS = CX * CY
HID = 1024
ROWS = 240
TILES = 32
NZ = 16
CHIPS = 16
COLUMNS = 262144
BLK = 256
F32 = jnp.float32
BF16 = jnp.bfloat16
VMEM_LIMIT = 40 * 1024 * 1024


def place(p):
    return p // 8, p % 8


def faces(opened, speed):
    near = jnp.where(opened, jnp.maximum(speed, 0.0) + KAPPA, 0.0)
    far = jnp.where(opened, jnp.minimum(speed, 0.0) - KAPPA, 0.0)
    return near, far


def transport_kernel(
    tracer_ref, east_ref, north_ref, depth_ref, out_ref,
    cells, side, pack_n, pack_s, halo_w, halo_e, halo_s, halo_n, halo_u,
    send_sems, recv_sems,
):
    z, x, m = lax.axis_index("ocx"), lax.axis_index("ocy"), lax.axis_index("ml")
    p = x * 8 + m
    to_e = (lax.rem(z + 1, NZ), x, m)
    to_w = (lax.rem(z + NZ - 1, NZ), x, m)
    to_n = (z, *place(lax.rem(p + 1, TILES)))
    to_s = (z, *place(lax.rem(p + TILES - 1, TILES)))
    barrier = pltpu.get_barrier_semaphore()
    for target in (to_e, to_w, to_n, to_s):
        pl.semaphore_signal(barrier, inc=1, device_id=target, device_id_type=MESH)

    level = lax.broadcasted_iota(jnp.int32, (PAD, CY), 0).astype(F32)
    lane = lax.broadcasted_iota(jnp.int32, (PAD, CY), 1)
    tail = lax.broadcasted_iota(jnp.int32, (PAD - LEV, CY), 0)
    depth = [depth_ref[i : i + 1, :].astype(F32) for i in range(CX)]
    for i in range(CX):
        cells[0, i, 0:LEV, :] = tracer_ref[:, i, :]
        cells[0, i, LEV:PAD, :] = jnp.where(tail == 0, depth[i], 0.0)
    for i in range(CX):
        side[i, 0:LEV, :] = north_ref[:, i, :]
        side[i, LEV:PAD, :] = jnp.zeros((PAD - LEV, CY), F32)
    side[CX, 0:LEV, :] = east_ref[:, CX - 1, :]
    side[CX, LEV:PAD, :] = jnp.zeros((PAD - LEV, CY), F32)
    pl.semaphore_wait(barrier, 4)

    def remote(src, dst, number, target):
        copy = pltpu.make_async_remote_copy(
            src_ref=src, dst_ref=dst, send_sem=send_sems.at[number], recv_sem=recv_sems.at[number],
            device_id=target, device_id_type=MESH,
        )
        copy.start()
        return copy

    copies = [remote(side.at[CX], halo_u, 12, to_e)]
    coef = None
    for step in range(STEPS):
        rows = [cells[step, i] for i in range(CX)]
        now = [
            remote(cells.at[step, CX - 1], halo_w.at[step], 4 * step, to_e),
            remote(cells.at[step, 0], halo_e.at[step], 4 * step + 1, to_w),
        ]
        up = jnp.zeros((PAD, CY), F32)
        down = jnp.zeros((PAD, CY), F32)
        for i in range(CX):
            up = jnp.where(lane == i, pltpu.roll(rows[i], i + 1, 1), up)
            down = jnp.where(lane == i, pltpu.roll(rows[i], i, 1) if i else rows[i], down)
            if step == 0:
                up = jnp.where(lane == CX + i, pltpu.roll(side[i], CX + i + 1, 1), up)
        pack_n[step] = up
        pack_s[step] = down
        now += [
            remote(pack_n.at[step], halo_s.at[step], 4 * step + 2, to_n),
            remote(pack_s.at[step], halo_n.at[step], 4 * step + 3, to_s),
        ]
        for copy in now:
            copy.wait_recv()
        copies += now
        west, east = halo_w[step], halo_e[step]
        south_pack, north_pack = halo_s[step], halo_n[step]
        south_in = [pltpu.roll(south_pack, (CY - i) % CY, 1) if i else south_pack for i in range(CX)]
        north_in = [pltpu.roll(north_pack, CY - 1 - i, 1) for i in range(CX)]
        if step == 0:
            copies[0].wait_recv()
            deep = [west[LEV : LEV + 1, :]] + depth + [east[LEV : LEV + 1, :]]
            east_faces = []
            for i in range(CX + 1):
                speed = halo_u[...] if i == 0 else None
                if i:
                    speed = jnp.concatenate(
                        [east_ref[:, i - 1, :], jnp.zeros((PAD - LEV, CY), F32)], axis=0
                    ) if i < CX else side[CX]
                east_faces.append(faces(level < jnp.minimum(deep[i], deep[i + 1]), speed))
            coef = []
            for i in range(CX):
                here = jnp.broadcast_to(depth[i], (PAD, CY))
                there = jnp.where(
                    lane == CY - 1,
                    jnp.broadcast_to(north_in[i][LEV : LEV + 1, :], (PAD, CY)),
                    pltpu.roll(here, CY - 1, 1),
                )
                shut_n = jnp.logical_and(lane == CY - 1, p == TILES - 1)
                near_n, far_n = faces(
                    jnp.logical_and(level < jnp.minimum(here, there), jnp.logical_not(shut_n)), side[i]
                )
                below = jnp.broadcast_to(south_in[i][LEV : LEV + 1, :], (PAD, CY))
                near_b, far_b = faces(
                    jnp.logical_and(level < jnp.minimum(here, below), p != 0),
                    pltpu.roll(south_pack, CY - CX - i, 1),
                )
                near_s = jnp.where(lane == 0, near_b, pltpu.roll(near_n, 1, 1))
                far_s = jnp.where(lane == 0, far_b, pltpu.roll(far_n, 1, 1))
                near_w, far_w = east_faces[i]
                near_e, far_e = east_faces[i + 1]
                coef.append((1.0 + far_w - near_e + far_s - near_n, near_w, far_e, near_s, far_n))
        wide = [west] + rows + [east]
        for i in range(CX):
            keep, near_w, far_e, near_s, far_n = coef[i]
            south = jnp.where(lane == 0, south_in[i], pltpu.roll(rows[i], 1, 1))
            north = jnp.where(lane == CY - 1, north_in[i], pltpu.roll(rows[i], CY - 1, 1))
            value = (
                keep * rows[i] + near_w * wide[i] - far_e * wide[i + 2] + near_s * south - far_n * north
            )
            if step == STEPS - 1:
                out_ref[i] = value
            else:
                cells[step + 1, i] = value
    for copy in copies:
        copy.wait_send()


def transport(tracer, east, north, depth):
    vmem = pl.BlockSpec(memory_space=pltpu.VMEM)
    halo = pltpu.VMEM((STEPS, PAD, CY), F32)
    return pl.pallas_call(
        transport_kernel,
        out_shape=jax.ShapeDtypeStruct((CX, PAD, CY), F32),
        in_specs=[vmem] * 4,
        out_specs=vmem,
        scratch_shapes=[
            pltpu.VMEM((STEPS, CX, PAD, CY), F32),
            pltpu.VMEM((CX + 1, PAD, CY), F32),
            halo, halo, halo, halo, halo, halo,
            pltpu.VMEM((PAD, CY), F32),
            pltpu.SemaphoreType.DMA((13,)),
            pltpu.SemaphoreType.DMA((13,)),
        ],
        compiler_params=pltpu.CompilerParams(
            collective_id=0, has_side_effects=True, vmem_limit_bytes=VMEM_LIMIT
        ),
        name="transport",
    )(tracer, east, north, depth)


def dot(a, b, dims):
    return lax.dot_general(a, b, (dims, ((), ())), preferred_element_type=F32)


def closure_kernel(
    moved_ref, east_ref, north_ref, target_ref, depth_ref, w1_ref, b1_ref, w2_ref, b2_ref,
    tendency_out, misfit_out, gathered,
    feat, weights, hidden, slope, total, wanted, chunks, core_in, summed, sending, landed,
    mine, strips, strips_in, strips_all, chunk, core_send, core_recv, send_sems, recv_sems,
):
    z, x, m = lax.axis_index("ocx"), lax.axis_index("ocy"), lax.axis_index("ml")
    core = lax.rem(m, 2)
    chip = x * 4 + m // 2
    sibling = (z, x, m + 1 - 2 * core)
    barrier = pltpu.get_barrier_semaphore()

    def other_chip(k):
        c = lax.rem(chip + k, CHIPS)
        return c, (z, c // 4, (c % 4) * 2 + core)

    def ring(k):
        w = lax.rem(z + k, NZ)
        return w, (w, x, m)

    def far_first(j):
        half = (j + 1) // 2
        return NZ // 2 + half * (1 - 2 * lax.rem(j, 2))

    def signal(target):
        pl.semaphore_signal(barrier, inc=1, device_id=target, device_id_type=MESH)

    def greet_ring(j, carry):
        signal(ring(far_first(j))[1])
        return carry

    def greet_chips(k, carry):
        signal(other_chip(k)[1])
        return carry

    lax.fori_loop(0, NZ - 1, greet_ring, 0)
    lax.fori_loop(1, CHIPS, greet_chips, 0)
    signal(sibling)

    def remote(src, dst, send_sem, recv_sem, target):
        return pltpu.make_async_remote_copy(
            src_ref=src, dst_ref=dst, send_sem=send_sem, recv_sem=recv_sem,
            device_id=target, device_id_type=MESH,
        )

    def whole(ref, number):
        return remote(ref, ref, send_sems.at[number], recv_sems.at[number], sibling)

    level = lax.broadcasted_iota(jnp.int32, (LEV, CY), 0).astype(F32)
    masks = []
    want = target_ref[...].astype(F32)
    wanted[...] = want
    for i in range(CX):
        at = slice(CY * i, CY * (i + 1))
        mask = level < depth_ref[i : i + 1, :].astype(F32)
        masks.append(mask)
        feat[0:LEV, at] = jnp.where(mask, moved_ref[i, 0:LEV, :], 0.0)
        feat[LEV : 2 * LEV, at] = jnp.where(mask, east_ref[:, i, :], 0.0)
        feat[2 * LEV : 3 * LEV, at] = jnp.where(mask, north_ref[:, i, :], 0.0)
    last = lax.broadcasted_iota(jnp.int32, (ROWS - 3 * LEV, CELLS), 0)
    feat[3 * LEV : ROWS, :] = jnp.where(last < 2, 1.0, 0.0)
    inputs = feat[...].astype(BF16)

    edge = 3 * LEV // 16 * 16
    weights[0:edge, :] = w1_ref[0:edge, :]
    bias = b1_ref[...]
    coarse = bias.astype(BF16).astype(F32)
    row = lax.broadcasted_iota(jnp.int32, (ROWS - edge, HID), 0) + edge
    final = jnp.where(row == 3 * LEV - 1, w1_ref[3 * LEV - 1 : 3 * LEV, :].astype(F32), 0.0)
    final = jnp.where(row == 3 * LEV, coarse, final)
    final = jnp.where(row == 3 * LEV + 1, bias - coarse, final)
    weights[edge:ROWS, :] = final.astype(BF16)

    acc = None
    for b in range(HID // BLK):
        at = slice(b * BLK, (b + 1) * BLK)
        before = dot(weights[:, at], inputs, ((0,), (0,)))
        stash = before.astype(BF16).astype(F32)
        gate = 0.5 * jnp.tanh(0.5 * stash) + 0.5
        act = (stash * gate).astype(BF16)
        hidden[at, :] = act
        slope[at, :] = gate * (1.0 + stash * (1.0 - gate))
        part = dot(w2_ref[:, at], act, ((1,), (0,)))
        acc = part if acc is None else acc + part
    eye = lax.broadcasted_iota(jnp.int32, (LEV, LEV), 0) == lax.broadcasted_iota(jnp.int32, (LEV, LEV), 1)
    bias2 = jnp.sum(jnp.where(eye, b2_ref[...], 0.0), axis=1, keepdims=True)
    output = acc + bias2
    total[...] = jnp.zeros((PAD, CELLS), F32)
    for i in range(CX):
        at = slice(CY * i, CY * (i + 1))
        tendency = jnp.where(masks[i], output[:, at], 0.0).astype(BF16).astype(F32)
        goal = jnp.where(masks[i], wanted[:, i, :], 0.0)
        misfit = tendency - goal
        total[0:LEV, at] = misfit * (1.0 / COLUMNS)
        tendency_out[i, 0:LEV, :] = tendency
        misfit_out[i, 0:LEV, :] = misfit
    d_out = total[...].astype(BF16)
    ones = jnp.ones((16, CELLS), BF16)
    bias_grad = dot(ones, d_out, ((1,), (1,)))
    spread = lax.broadcasted_iota(jnp.int32, (PAD, CY), 0) == LEV
    per = BLK // CY
    to_sibling = []
    for b in range(HID // BLK):
        at = slice(b * BLK, (b + 1) * BLK)
        d_hidden = dot(w2_ref[:, at], d_out[0:LEV, :], ((0,), (0,)))
        d_before = (d_hidden * slope[at, :]).astype(BF16)
        g1 = dot(inputs, d_before, ((1,), (1,)))
        g2 = dot(d_out, hidden[at, :], ((1,), (1,)))
        for t in range(per):
            lanes = slice(t * CY, (t + 1) * CY)
            tile = b * per + t
            for g in range(3):
                chunks[g % 2, 2 * tile + g // 2] = g1[PAD * g : PAD * (g + 1), lanes]
            last_part = g2[:, lanes]
            if tile == 0:
                row = jnp.concatenate([bias_grad[0:1, :], jnp.zeros((1, CY - PAD), F32)], axis=1)
                last_part = jnp.where(spread, row, last_part)
            chunks[1, 2 * tile + 1] = last_part
        if b == 0:
            pl.semaphore_wait(barrier, NZ - 1 + CHIPS - 1 + 1)
        some = pl.ds(2 * per * b, 2 * per)
        copy = remote(chunks.at[1 - core, some], core_in.at[some], core_send.at[b], core_recv.at[b], sibling)
        copy.start()
        to_sibling.append(copy)
    row = lax.broadcasted_iota(jnp.int32, (PAD, CY), 0)
    bias_row = 3 * LEV - 2 * PAD + core * (LEV - (3 * LEV - 2 * PAD))
    for b in range(HID // BLK):
        to_sibling[b].wait_recv()
        some = pl.ds(2 * per * b, 2 * per)
        both = chunks[core, some] + core_in[some]
        for j in range(2 * per):
            value = both[j]
            sent = value
            if j % 2:
                low = value - value.astype(BF16).astype(F32)
                value = jnp.where(row == bias_row + 1, 0.0, value)
                sent = jnp.where(row == bias_row + 1, pltpu.roll(low, 1, 0), value)
            summed[2 * per * b + j] = value
            sending[2 * per * b + j] = sent.astype(BF16)

    def scatter(k, carry):
        c, target = other_chip(k)
        remote(sending.at[c], landed.at[k - 1], send_sems.at[0], recv_sems.at[0], target).start()
        return carry

    lax.fori_loop(1, CHIPS, scatter, 0)
    whole(landed, 0).wait_recv()
    amount = summed[chip]
    for k in range(CHIPS - 1):
        amount = amount + landed[k].astype(F32)
    mine[...] = amount
    part = PAD // NZ
    for k in range(NZ):
        strips[k] = mine[part * k : part * (k + 1), :]

    def scatter_ring(j, carry):
        k = far_first(j)
        w, target = ring(k)
        remote(strips.at[w], strips_in.at[k - 1], send_sems.at[1], recv_sems.at[1], target).start()
        return carry

    lax.fori_loop(0, NZ - 1, scatter_ring, 0)
    whole(strips_in, 1).wait_recv()
    strip = strips[z]
    for k in range(NZ - 1):
        strip = strip + strips_in[k]
    strips_all[NZ - 1] = strip

    def gather_ring(j, carry):
        k = far_first(j)
        _, target = ring(k)
        remote(
            strips_all.at[NZ - 1], strips_all.at[k - 1], send_sems.at[2], recv_sems.at[2], target
        ).start()
        return carry

    lax.fori_loop(0, NZ - 1, gather_ring, 0)
    arrived = strips_all.at[0 : NZ - 1]
    whole(arrived, 2).wait_recv()
    for k in range(NZ):
        place_in = lax.rem(z - k + NZ - 1 + NZ, NZ)
        mine[part * k : part * (k + 1), :] = strips_all[place_in]
    has_bias = lax.rem(chip, 2) == 1
    value = mine[...]
    both = jnp.where(jnp.logical_and(row == bias_row, has_bias), pltpu.roll(value, PAD - 1, 0), 0.0) + value
    low = both - both.astype(BF16).astype(F32)
    both = jnp.where(jnp.logical_and(row == bias_row + 1, has_bias), pltpu.roll(low, 1, 0), both)
    chunk[...] = both.astype(BF16)
    gathered[core, chip] = chunk[...]

    def gather(k, carry):
        _, target = other_chip(k)
        remote(chunk, gathered.at[core, chip], send_sems.at[3], recv_sems.at[3], target).start()
        return carry

    lax.fori_loop(1, CHIPS, gather, 0)
    whole(landed, 3).wait_recv()
    forward = remote(gathered.at[core], gathered.at[core], send_sems.at[4], recv_sems.at[4], sibling)
    forward.start()
    for copy in to_sibling:
        copy.wait_send()
    whole(landed, 0).wait_send()
    whole(strips_in, 1).wait_send()
    whole(arrived, 2).wait_send()
    whole(landed, 3).wait_send()
    forward.wait()


def closure(moved, east, north, target, depth, w1, b1, w2, b2):
    vmem = pl.BlockSpec(memory_space=pltpu.VMEM)
    part = PAD // NZ
    halves = HID // BLK
    return pl.pallas_call(
        closure_kernel,
        out_shape=(
            jax.ShapeDtypeStruct((CX, PAD, CY), F32),
            jax.ShapeDtypeStruct((CX, PAD, CY), F32),
            jax.ShapeDtypeStruct((2, CHIPS, PAD, CY), BF16),
        ),
        in_specs=[vmem] * 9,
        out_specs=(vmem,) * 3,
        scratch_shapes=[
            pltpu.VMEM((ROWS, CELLS), F32),
            pltpu.VMEM((ROWS, HID), BF16),
            pltpu.VMEM((HID, CELLS), BF16),
            pltpu.VMEM((HID, CELLS), F32),
            pltpu.VMEM((PAD, CELLS), F32),
            pltpu.VMEM((LEV, CX, CY), F32),
            pltpu.VMEM((2, CHIPS, PAD, CY), F32),
            pltpu.VMEM((CHIPS, PAD, CY), F32),
            pltpu.VMEM((CHIPS, PAD, CY), F32),
            pltpu.VMEM((CHIPS, PAD, CY), BF16),
            pltpu.VMEM((CHIPS - 1, PAD, CY), BF16),
            pltpu.VMEM((PAD, CY), F32),
            pltpu.VMEM((NZ, part, CY), F32),
            pltpu.VMEM((NZ - 1, part, CY), F32),
            pltpu.VMEM((NZ, part, CY), F32),
            pltpu.VMEM((PAD, CY), BF16),
            pltpu.SemaphoreType.DMA((halves,)),
            pltpu.SemaphoreType.DMA((halves,)),
            pltpu.SemaphoreType.DMA((5,)),
            pltpu.SemaphoreType.DMA((5,)),
        ],
        compiler_params=pltpu.CompilerParams(
            collective_id=1, has_side_effects=True, vmem_limit_bytes=VMEM_LIMIT
        ),
        name="closure",
    )(moved, east, north, target, depth, w1, b1.reshape(1, HID), w2.T, b2.reshape(1, LEV))


def unpack_kernel(moved, tendency, misfit, chunks, tracer_out, misfit_out, w1_ref, b1_ref, w2_ref, b2_ref, wide):
    for i in range(CX):
        tracer_out[:, i, :] = moved[i, 0:LEV, :] + tendency[i, 0:LEV, :]
        wide[:, i, :] = misfit[i, 0:LEV, :]
    misfit_out[...] = wide[...].astype(BF16)
    rest = 3 * LEV - 2 * PAD
    for t in range(HID // CY):
        lanes = slice(t * CY, (t + 1) * CY)
        for g in range(2):
            w1_ref[PAD * g : PAD * (g + 1), lanes] = chunks[g % 2, 2 * t + g // 2].astype(F32)
        third = chunks[0, 2 * t + 1].astype(F32)
        w1_ref[2 * PAD : 3 * LEV, lanes] = third[0:rest, :]
        b1_ref[:, lanes] = third[rest : rest + 1, :] + third[rest + 1 : rest + 2, :]
        fourth = chunks[1, 2 * t + 1].astype(F32)
        w2_ref[:, lanes] = fourth[0:LEV, :]
        if t == 0:
            b2_ref[...] = fourth[LEV : LEV + 1, 0:LEV] + fourth[LEV + 1 : LEV + 2, 0:LEV]


def unpack(moved, tendency, misfit, chunks):
    vmem = pl.BlockSpec(memory_space=pltpu.VMEM)
    return pl.pallas_call(
        unpack_kernel,
        out_shape=(
            jax.ShapeDtypeStruct((LEV, CX, CY), F32),
            jax.ShapeDtypeStruct((LEV, CX, CY), BF16),
            jax.ShapeDtypeStruct((3 * LEV, HID), F32),
            jax.ShapeDtypeStruct((1, HID), F32),
            jax.ShapeDtypeStruct((LEV, HID), F32),
            jax.ShapeDtypeStruct((1, LEV), F32),
        ),
        in_specs=[vmem] * 4,
        out_specs=(vmem,) * 6,
        scratch_shapes=[pltpu.VMEM((LEV, CX, CY), F32)],
        compiler_params=pltpu.CompilerParams(vmem_limit_bytes=VMEM_LIMIT),
        name="unpack",
    )(moved, tendency, misfit, chunks)


def on_device(tracer, east, north, target, depth, slots, w1, b1, w2, b2):
    moved = transport(tracer, east, north, depth)
    tendency, misfit, chunks = closure(moved, east, north, target, depth, w1, b1, w2, b2)
    tracer_out, misfit_out, grad_w1, grad_b1, grad_w2, grad_b2 = unpack(moved, tendency, misfit, chunks)
    return tracer_out, misfit_out, grad_w1, grad_b1.reshape(HID), grad_w2.T, grad_b2.reshape(LEV)


def solution(mesh):
    grid = P(None, "ocx", ("ocy", "ml"))
    return jax.shard_map(
        on_device,
        mesh=mesh,
        in_specs=(grid, grid, grid, grid, P("ocx", ("ocy", "ml")), P("ocx", ("ocy", "ml"), None, None), P(), P(), P(), P()),
        out_specs=(grid, grid, P(), P(), P(), P()),
        check_vma=False,
    )
```

```python
import jax
import jax.numpy as jnp
from jax import lax
from jax.experimental import pallas as pl
from jax.experimental.pallas import tpu as pltpu
from jax.sharding import PartitionSpec as P

MESH = pl.DeviceIdType.MESH
KAPPA = 0.1
STEPS = 3
LEV = 75
PAD = 80
CX = 4
CY = 128
CELLS = CX * CY
HID = 1024
ROWS = 240
TILES = 32
NZ = 16
CHIPS = 16
COLUMNS = 262144
BLK = 256
F32 = jnp.float32
BF16 = jnp.bfloat16
VMEM_LIMIT = 60 * 1024 * 1024


def place(p):
    return lax.div(p, 8), lax.rem(p, 8)


def faces(opened, speed):
    near = jnp.where(opened, jnp.maximum(speed, 0.0) + KAPPA, 0.0)
    far = jnp.where(opened, jnp.minimum(speed, 0.0) - KAPPA, 0.0)
    return near, far


def dot(a, b, dims):
    return lax.dot_general(a, b, (dims, ((), ())), preferred_element_type=F32)


def main_kernel(
    tracer_hbm, east_hbm, north_hbm, target_hbm, depth_hbm, w1_hbm, b1_hbm, w2_hbm, b2_hbm,
    fresh_out, misfit_out, gathered,
    tracer_ref, east_ref, north_ref, target_ref, depth_ref, w1_ref, b1_ref, w2_ref, b2_ref,
    cells, side, side_u, halo_out, halo_w, halo_e, halo_s, halo_n, halo_u,
    feat, weights, hidden, slope, total, wanted, chunks, core_in, summed, sending, landed,
    mine, strips, strips_in, strips_all, chunk,
    load_sems, halo_send, halo_recv, core_send, core_recv, send_sems, recv_sems, known,
):
    z, x, m = lax.axis_index("ocx"), lax.axis_index("ocy"), lax.axis_index("ml")
    core = lax.rem(m, 2)
    chip = x * 4 + lax.div(m, 2)
    p = x * 8 + m
    sibling = (z, x, m + 1 - 2 * core)

    def other_chip(k):
        c = lax.rem(chip + k, CHIPS)
        return c, (z, lax.div(c, 4), lax.rem(c, 4) * 2 + core)

    def ring(k):
        w = lax.rem(z + k, NZ)
        return w, (w, x, m)

    def far_first(j):
        half = lax.div(j + 1, 2)
        return NZ // 2 + half * (1 - 2 * lax.rem(j, 2))

    to_e, to_w = ring(1)[1], ring(NZ - 1)[1]
    to_n = (z, *place(lax.rem(p + 1, TILES)))
    to_s = (z, *place(lax.rem(p + TILES - 1, TILES)))

    pairs = (
        (depth_hbm, depth_ref), (tracer_hbm, tracer_ref), (north_hbm, north_ref), (east_hbm, east_ref),
        (target_hbm, target_ref), (w1_hbm, w1_ref), (b1_hbm, b1_ref), (w2_hbm, w2_ref), (b2_hbm, b2_ref),
    )
    loads = [pltpu.make_async_copy(src, dst, load_sems.at[i]) for i, (src, dst) in enumerate(pairs)]
    for load in loads:
        load.start()

    barrier = pltpu.get_barrier_semaphore()

    def signal(target):
        pl.semaphore_signal(barrier, inc=1, device_id=target, device_id_type=MESH)

    def greet_chips(k, carry):
        signal(other_chip(k)[1])
        return carry

    for target in (to_e, to_w, to_n, to_s):
        signal(target)
    lax.fori_loop(1, CHIPS, greet_chips, 0)
    signal(sibling)

    def spread_word(number, places):
        for k in (places, NZ - places):
            pl.semaphore_signal(known.at[number], inc=1, device_id=ring(k)[1], device_id_type=MESH)

    def remote(src, dst, send_sem, recv_sem, target):
        return pltpu.make_async_remote_copy(
            src_ref=src, dst_ref=dst, send_sem=send_sem, recv_sem=recv_sem,
            device_id=target, device_id_type=MESH,
        )

    def whole(ref, number):
        return remote(ref, ref, send_sems.at[number], recv_sems.at[number], sibling)

    def halo(src, dst, number, target):
        copy = remote(src, dst, halo_send.at[number], halo_recv.at[number], target)
        copy.start()
        return copy

    level = lax.broadcasted_iota(jnp.int32, (PAD, CY), 0).astype(F32)
    lane = lax.broadcasted_iota(jnp.int32, (PAD, CY), 1)
    tail = lax.broadcasted_iota(jnp.int32, (PAD - LEV, CY), 0)
    none = jnp.zeros((PAD - LEV, CY), F32)
    for load in loads[:4]:
        load.wait()
    depth = [depth_ref[i : i + 1, :].astype(F32) for i in range(CX)]
    masks = [level[0:LEV, :] < depth[i] for i in range(CX)]
    for i in range(CX):
        at = slice(CY * i, CY * (i + 1))
        cells[0, i, 0:LEV, :] = tracer_ref[:, i, :]
        cells[0, i, LEV:PAD, :] = jnp.where(tail == 0, depth[i], 0.0)
        north_i, east_i = north_ref[:, i, :], east_ref[:, i, :]
        side[i, 0:LEV, :] = north_i
        side[i, LEV:PAD, :] = none
        side[CX + i, 0:LEV, :] = east_i
        side[CX + i, LEV:PAD, :] = none
        feat[LEV : 2 * LEV, at] = jnp.where(masks[i], east_i, 0.0)
        feat[2 * LEV : 3 * LEV, at] = jnp.where(masks[i], north_i, 0.0)
    last = lax.broadcasted_iota(jnp.int32, (ROWS - 3 * LEV, CELLS), 0)
    feat[3 * LEV : ROWS, :] = jnp.where(last < 2, 1.0, 0.0)
    side_u[...] = side[2 * CX - 1].astype(BF16)

    for load in loads[4:]:
        load.wait()
    wanted[...] = target_ref[...].astype(F32)
    edge = 3 * LEV // 16 * 16
    weights[0:edge, :] = w1_ref[0:edge, :]
    bias = b1_ref[...]
    coarse = bias.astype(BF16).astype(F32)
    row = lax.broadcasted_iota(jnp.int32, (ROWS - edge, HID), 0) + edge
    final = jnp.where(row == 3 * LEV - 1, w1_ref[3 * LEV - 1 : 3 * LEV, :].astype(F32), 0.0)
    final = jnp.where(row == 3 * LEV, coarse, final)
    final = jnp.where(row == 3 * LEV + 1, bias - coarse, final)
    weights[edge:ROWS, :] = final.astype(BF16)

    pl.semaphore_wait(barrier, 4 + CHIPS - 1 + 1)
    spread_word(0, 1)

    copies = [halo(side_u, halo_u, 4 * STEPS, to_e)]
    coef = None
    for step in range(STEPS):
        rows = [cells[step, i] for i in range(CX)]
        halo_out[step, 0] = rows[CX - 1].astype(BF16)
        halo_out[step, 1] = rows[0].astype(BF16)
        now = [
            halo(halo_out.at[step, 0], halo_w.at[step], 4 * step, to_e),
            halo(halo_out.at[step, 1], halo_e.at[step], 4 * step + 1, to_w),
        ]
        up = jnp.zeros((PAD, CY), F32)
        down = jnp.zeros((PAD, CY), F32)
        for i in range(CX):
            up = jnp.where(lane == i, pltpu.roll(rows[i], i + 1, 1), up)
            down = jnp.where(lane == i, pltpu.roll(rows[i], i, 1) if i else rows[i], down)
            if step == 0:
                up = jnp.where(lane == CX + i, pltpu.roll(side[i], CX + i + 1, 1), up)
        halo_out[step, 2] = up.astype(BF16)
        halo_out[step, 3] = down.astype(BF16)
        now += [
            halo(halo_out.at[step, 2], halo_s.at[step], 4 * step + 2, to_n),
            halo(halo_out.at[step, 3], halo_n.at[step], 4 * step + 3, to_s),
        ]
        for copy in now:
            copy.wait_recv()
        copies += now
        if step < 2:
            pl.semaphore_wait(known.at[step], 2)
            spread_word(step + 1, 2 * (step + 1))
        west, east = halo_w[step].astype(F32), halo_e[step].astype(F32)
        south_pack, north_pack = halo_s[step].astype(F32), halo_n[step].astype(F32)
        south_in = [pltpu.roll(south_pack, (CY - i) % CY, 1) if i else south_pack for i in range(CX)]
        north_in = [pltpu.roll(north_pack, CY - 1 - i, 1) for i in range(CX)]
        if step == 0:
            copies[0].wait_recv()
            deep = [west[LEV : LEV + 1, :]] + depth + [east[LEV : LEV + 1, :]]
            east_faces = []
            for i in range(CX + 1):
                speed = side[CX + i - 1] if i else halo_u[...].astype(F32)
                east_faces.append(faces(level < jnp.minimum(deep[i], deep[i + 1]), speed))
            coef = []
            for i in range(CX):
                here = jnp.broadcast_to(depth[i], (PAD, CY))
                there = jnp.where(
                    lane == CY - 1,
                    jnp.broadcast_to(north_in[i][LEV : LEV + 1, :], (PAD, CY)),
                    pltpu.roll(here, CY - 1, 1),
                )
                shut_n = jnp.logical_and(lane == CY - 1, p == TILES - 1)
                near_n, far_n = faces(
                    jnp.logical_and(level < jnp.minimum(here, there), jnp.logical_not(shut_n)), side[i]
                )
                below = jnp.broadcast_to(south_in[i][LEV : LEV + 1, :], (PAD, CY))
                near_b, far_b = faces(
                    jnp.logical_and(level < jnp.minimum(here, below), p != 0),
                    pltpu.roll(south_pack, CY - CX - i, 1),
                )
                near_s = jnp.where(lane == 0, near_b, pltpu.roll(near_n, 1, 1))
                far_s = jnp.where(lane == 0, far_b, pltpu.roll(far_n, 1, 1))
                near_w, far_w = east_faces[i]
                near_e, far_e = east_faces[i + 1]
                coef.append((1.0 + far_w - near_e + far_s - near_n, near_w, far_e, near_s, far_n))
        wide = [west] + rows + [east]
        for i in range(CX):
            keep, near_w, far_e, near_s, far_n = coef[i]
            south = jnp.where(lane == 0, south_in[i], pltpu.roll(rows[i], 1, 1))
            north = jnp.where(lane == CY - 1, north_in[i], pltpu.roll(rows[i], CY - 1, 1))
            cells[step + 1, i] = (
                keep * rows[i] + near_w * wide[i] - far_e * wide[i + 2] + near_s * south - far_n * north
            )

    for i in range(CX):
        at = slice(CY * i, CY * (i + 1))
        feat[0:LEV, at] = jnp.where(masks[i], cells[STEPS, i, 0:LEV, :], 0.0)
    inputs = feat[...].astype(BF16)

    acc = None
    for b in range(HID // BLK):
        at = slice(b * BLK, (b + 1) * BLK)
        before = dot(weights[:, at], inputs, ((0,), (0,)))
        stash = before.astype(BF16).astype(F32)
        gate = 0.5 * jnp.tanh(0.5 * stash) + 0.5
        act = (stash * gate).astype(BF16)
        hidden[at, :] = act
        slope[at, :] = gate * (1.0 + stash * (1.0 - gate))
        part = dot(w2_ref[:, at], act, ((1,), (0,)))
        acc = part if acc is None else acc + part
    eye = lax.broadcasted_iota(jnp.int32, (LEV, LEV), 0) == lax.broadcasted_iota(jnp.int32, (LEV, LEV), 1)
    bias2 = jnp.sum(jnp.where(eye, b2_ref[...], 0.0), axis=1, keepdims=True)
    output = acc + bias2
    total[...] = jnp.zeros((PAD, CELLS), F32)
    for i in range(CX):
        at = slice(CY * i, CY * (i + 1))
        tendency = jnp.where(masks[i], output[:, at], 0.0).astype(BF16).astype(F32)
        goal = jnp.where(masks[i], wanted[:, i, :], 0.0)
        misfit = tendency - goal
        total[0:LEV, at] = misfit * (1.0 / COLUMNS)
        fresh_out[i, 0:LEV, :] = cells[STEPS, i, 0:LEV, :] + tendency
        misfit_out[i, 0:LEV, :] = misfit
    d_out = total[...].astype(BF16)
    ones = jnp.ones((16, CELLS), BF16)
    bias_grad = dot(ones, d_out, ((1,), (1,)))
    spread = lax.broadcasted_iota(jnp.int32, (PAD, CY), 0) == LEV
    per = BLK // CY
    to_sibling = []
    for b in range(HID // BLK):
        at = slice(b * BLK, (b + 1) * BLK)
        d_hidden = dot(w2_ref[:, at], d_out[0:LEV, :], ((0,), (0,)))
        d_before = (d_hidden * slope[at, :]).astype(BF16)
        g1 = dot(inputs, d_before, ((1,), (1,)))
        g2 = dot(d_out, hidden[at, :], ((1,), (1,)))
        for t in range(per):
            lanes = slice(t * CY, (t + 1) * CY)
            tile = b * per + t
            for g in range(3):
                chunks[g % 2, 2 * tile + g // 2] = g1[PAD * g : PAD * (g + 1), lanes]
            last_part = g2[:, lanes]
            if tile == 0:
                row = jnp.concatenate([bias_grad[0:1, :], jnp.zeros((1, CY - PAD), F32)], axis=1)
                last_part = jnp.where(spread, row, last_part)
            chunks[1, 2 * tile + 1] = last_part
        some = pl.ds(2 * per * b, 2 * per)
        copy = remote(chunks.at[1 - core, some], core_in.at[some], core_send.at[b], core_recv.at[b], sibling)
        copy.start()
        to_sibling.append(copy)
    row = lax.broadcasted_iota(jnp.int32, (PAD, CY), 0)
    bias_row = 3 * LEV - 2 * PAD + core * (LEV - (3 * LEV - 2 * PAD))
    for b in range(HID // BLK):
        to_sibling[b].wait_recv()
        some = pl.ds(2 * per * b, 2 * per)
        both = chunks[core, some] + core_in[some]
        for j in range(2 * per):
            value = both[j]
            sent = value
            if j % 2:
                low = value - value.astype(BF16).astype(F32)
                value = jnp.where(row == bias_row + 1, 0.0, value)
                sent = jnp.where(row == bias_row + 1, pltpu.roll(low, 1, 0), value)
            summed[2 * per * b + j] = value
            sending[2 * per * b + j] = sent.astype(BF16)

    def scatter(k, carry):
        c, target = other_chip(k)
        remote(sending.at[c], landed.at[k - 1], send_sems.at[0], recv_sems.at[0], target).start()
        return carry

    lax.fori_loop(1, CHIPS, scatter, 0)
    whole(landed, 0).wait_recv()
    amount = summed[chip]
    for k in range(CHIPS - 1):
        amount = amount + landed[k].astype(F32)
    mine[...] = amount
    part = PAD // NZ
    for k in range(NZ):
        strips[k] = mine[part * k : part * (k + 1), :]

    pl.semaphore_wait(known.at[2], 2)

    def scatter_ring(j, carry):
        k = far_first(j)
        w, target = ring(k)
        remote(strips.at[w], strips_in.at[k - 1], send_sems.at[1], recv_sems.at[1], target).start()
        return carry

    lax.fori_loop(0, NZ - 1, scatter_ring, 0)
    whole(strips_in, 1).wait_recv()
    strip = strips[z]
    for k in range(NZ - 1):
        strip = strip + strips_in[k]
    strips_all[NZ - 1] = strip

    def gather_ring(j, carry):
        k = far_first(j)
        _, target = ring(k)
        remote(
            strips_all.at[NZ - 1], strips_all.at[k - 1], send_sems.at[2], recv_sems.at[2], target
        ).start()
        return carry

    lax.fori_loop(0, NZ - 1, gather_ring, 0)
    arrived = strips_all.at[0 : NZ - 1]
    whole(arrived, 2).wait_recv()
    for k in range(NZ):
        place_in = lax.rem(z - k + NZ - 1 + NZ, NZ)
        mine[part * k : part * (k + 1), :] = strips_all[place_in]
    has_bias = lax.rem(chip, 2) == 1
    value = mine[...]
    both = jnp.where(jnp.logical_and(row == bias_row, has_bias), pltpu.roll(value, PAD - 1, 0), 0.0) + value
    low = both - both.astype(BF16).astype(F32)
    both = jnp.where(jnp.logical_and(row == bias_row + 1, has_bias), pltpu.roll(low, 1, 0), both)
    chunk[...] = both.astype(BF16)
    gathered[core, chip] = chunk[...]

    def gather(k, carry):
        _, target = other_chip(k)
        remote(chunk, gathered.at[core, chip], send_sems.at[3], recv_sems.at[3], target).start()
        return carry

    lax.fori_loop(1, CHIPS, gather, 0)
    whole(landed, 3).wait_recv()
    forward = remote(gathered.at[core], gathered.at[core], send_sems.at[4], recv_sems.at[4], sibling)
    forward.start()
    for copy in copies + to_sibling:
        copy.wait_send()
    whole(landed, 0).wait_send()
    whole(strips_in, 1).wait_send()
    whole(arrived, 2).wait_send()
    whole(landed, 3).wait_send()
    forward.wait()


def main(*operands):
    vmem = pl.BlockSpec(memory_space=pltpu.VMEM)
    hbm = pl.BlockSpec(memory_space=pltpu.HBM)
    part = PAD // NZ
    halves = HID // BLK
    halo = pltpu.VMEM((STEPS, PAD, CY), BF16)
    return pl.pallas_call(
        main_kernel,
        out_shape=(
            jax.ShapeDtypeStruct((CX, PAD, CY), F32),
            jax.ShapeDtypeStruct((CX, PAD, CY), F32),
            jax.ShapeDtypeStruct((2, CHIPS, PAD, CY), BF16),
        ),
        in_specs=[hbm] * 9,
        out_specs=(vmem,) * 3,
        scratch_shapes=[pltpu.VMEM(a.shape, a.dtype) for a in operands]
        + [
            pltpu.VMEM((STEPS + 1, CX, PAD, CY), F32),
            pltpu.VMEM((2 * CX, PAD, CY), F32),
            pltpu.VMEM((PAD, CY), BF16),
            pltpu.VMEM((STEPS, 4, PAD, CY), BF16),
            halo, halo, halo, halo,
            pltpu.VMEM((PAD, CY), BF16),
            pltpu.VMEM((ROWS, CELLS), F32),
            pltpu.VMEM((ROWS, HID), BF16),
            pltpu.VMEM((HID, CELLS), BF16),
            pltpu.VMEM((HID, CELLS), F32),
            pltpu.VMEM((PAD, CELLS), F32),
            pltpu.VMEM((LEV, CX, CY), F32),
            pltpu.VMEM((2, CHIPS, PAD, CY), F32),
            pltpu.VMEM((CHIPS, PAD, CY), F32),
            pltpu.VMEM((CHIPS, PAD, CY), F32),
            pltpu.VMEM((CHIPS, PAD, CY), BF16),
            pltpu.VMEM((CHIPS - 1, PAD, CY), BF16),
            pltpu.VMEM((PAD, CY), F32),
            pltpu.VMEM((NZ, part, CY), F32),
            pltpu.VMEM((NZ - 1, part, CY), F32),
            pltpu.VMEM((NZ, part, CY), F32),
            pltpu.VMEM((PAD, CY), BF16),
            pltpu.SemaphoreType.DMA((len(operands),)),
            pltpu.SemaphoreType.DMA((4 * STEPS + 1,)),
            pltpu.SemaphoreType.DMA((4 * STEPS + 1,)),
            pltpu.SemaphoreType.DMA((halves,)),
            pltpu.SemaphoreType.DMA((halves,)),
            pltpu.SemaphoreType.DMA((5,)),
            pltpu.SemaphoreType.DMA((5,)),
            pltpu.SemaphoreType.REGULAR((3,)),
        ],
        compiler_params=pltpu.CompilerParams(
            collective_id=0, has_side_effects=True, vmem_limit_bytes=VMEM_LIMIT
        ),
        name="main",
    )(*operands)


def unpack_kernel(fresh, misfit, chunks, tracer_out, misfit_out, w1_ref, b1_ref, w2_ref, b2_ref, wide):
    for i in range(CX):
        tracer_out[:, i, :] = fresh[i, 0:LEV, :]
        wide[:, i, :] = misfit[i, 0:LEV, :]
    misfit_out[...] = wide[...].astype(BF16)
    rest = 3 * LEV - 2 * PAD
    for t in range(HID // CY):
        lanes = slice(t * CY, (t + 1) * CY)
        for g in range(2):
            w1_ref[PAD * g : PAD * (g + 1), lanes] = chunks[g % 2, 2 * t + g // 2].astype(F32)
        third = chunks[0, 2 * t + 1].astype(F32)
        w1_ref[2 * PAD : 3 * LEV, lanes] = third[0:rest, :]
        b1_ref[:, lanes] = third[rest : rest + 1, :] + third[rest + 1 : rest + 2, :]
        fourth = chunks[1, 2 * t + 1].astype(F32)
        w2_ref[:, lanes] = fourth[0:LEV, :]
        if t == 0:
            b2_ref[...] = fourth[LEV : LEV + 1, 0:LEV] + fourth[LEV + 1 : LEV + 2, 0:LEV]


def unpack(fresh, misfit, chunks):
    vmem = pl.BlockSpec(memory_space=pltpu.VMEM)
    return pl.pallas_call(
        unpack_kernel,
        out_shape=(
            jax.ShapeDtypeStruct((LEV, CX, CY), F32),
            jax.ShapeDtypeStruct((LEV, CX, CY), BF16),
            jax.ShapeDtypeStruct((3 * LEV, HID), F32),
            jax.ShapeDtypeStruct((1, HID), F32),
            jax.ShapeDtypeStruct((LEV, HID), F32),
            jax.ShapeDtypeStruct((1, LEV), F32),
        ),
        in_specs=[vmem] * 3,
        out_specs=(vmem,) * 6,
        scratch_shapes=[pltpu.VMEM((LEV, CX, CY), F32)],
        compiler_params=pltpu.CompilerParams(vmem_limit_bytes=VMEM_LIMIT),
        name="unpack",
    )(fresh, misfit, chunks)


def on_device(tracer, east, north, target, depth, slots, w1, b1, w2, b2):
    fresh, misfit, chunks = main(
        tracer, east, north, target, depth, w1, b1.reshape(1, HID), w2.T, b2.reshape(1, LEV)
    )
    tracer_out, misfit_out, grad_w1, grad_b1, grad_w2, grad_b2 = unpack(fresh, misfit, chunks)
    return tracer_out, misfit_out, grad_w1, grad_b1.reshape(HID), grad_w2.T, grad_b2.reshape(LEV)


def solution(mesh):
    grid = P(None, "ocx", ("ocy", "ml"))
    return jax.shard_map(
        on_device,
        mesh=mesh,
        in_specs=(grid, grid, grid, grid, P("ocx", ("ocy", "ml")), P("ocx", ("ocy", "ml"), None, None), P(), P(), P(), P()),
        out_specs=(grid, grid, P(), P(), P(), P()),
        check_vma=False,
    )
```

```python
import jax
import jax.numpy as jnp
from jax import lax
from jax.experimental import pallas as pl
from jax.experimental.pallas import tpu as pltpu
from jax.sharding import PartitionSpec as P

MESH = pl.DeviceIdType.MESH
KAPPA = 0.1
STEPS = 3
LEV = 75
PAD = 80
CX = 4
CY = 128
CELLS = CX * CY
HID = 1024
ROWS = 240
TILES = 32
NZ = 16
CHIPS = 16
COLUMNS = 262144
BLK = 256
F32 = jnp.float32
BF16 = jnp.bfloat16
VMEM_LIMIT = 40 * 1024 * 1024


def place(p):
    return lax.div(p, 8), lax.rem(p, 8)


def faces(opened, speed):
    near = jnp.where(opened, jnp.maximum(speed, 0.0) + KAPPA, 0.0)
    far = jnp.where(opened, jnp.minimum(speed, 0.0) - KAPPA, 0.0)
    return near, far


def dot(a, b, dims):
    return lax.dot_general(a, b, (dims, ((), ())), preferred_element_type=F32)


def main_kernel(
    tracer_hbm, east_hbm, north_hbm, target_hbm, depth_hbm, w1_hbm, b1_hbm, w2_hbm, b2_hbm,
    fresh_out, misfit_out, gathered,
    tracer_ref, east_ref, north_ref, target_ref, depth_ref, w1_ref, b1_ref, w2_ref, b2_ref,
    cells, side, side_u, halo_out, halo_w, halo_e, halo_s, halo_n, halo_u,
    feat, weights, hidden, slope, total, wanted, chunks, core_in, summed, sending, landed,
    mine, strips, strips_in, strips_all, chunk,
    load_sems, halo_send, halo_recv, core_send, core_recv, send_sems, recv_sems, known,
):
    z, x, m = lax.axis_index("ocx"), lax.axis_index("ocy"), lax.axis_index("ml")
    core = lax.rem(m, 2)
    chip = x * 4 + lax.div(m, 2)
    p = x * 8 + m
    sibling = (z, x, m + 1 - 2 * core)

    def other_chip(k):
        c = lax.rem(chip + k, CHIPS)
        return c, (z, lax.div(c, 4), lax.rem(c, 4) * 2 + core)

    def ring(k):
        w = lax.rem(z + k, NZ)
        return w, (w, x, m)

    def far_first(j):
        half = lax.div(j + 1, 2)
        return NZ // 2 + half * (1 - 2 * lax.rem(j, 2))

    def tile(k):
        return (z, *place(lax.rem(p + k, TILES)))

    to_e, to_w = ring(1)[1], ring(NZ - 1)[1]
    to_n, to_s = tile(1), tile(TILES - 1)

    pairs = (
        (depth_hbm, depth_ref), (tracer_hbm, tracer_ref), (north_hbm, north_ref), (east_hbm, east_ref),
        (target_hbm, target_ref), (w1_hbm, w1_ref), (b1_hbm, b1_ref), (w2_hbm, w2_ref), (b2_hbm, b2_ref),
    )
    loads = [pltpu.make_async_copy(src, dst, load_sems.at[i]) for i, (src, dst) in enumerate(pairs)]
    for load in loads:
        load.start()

    barrier = pltpu.get_barrier_semaphore()

    def signal(target):
        pl.semaphore_signal(barrier, inc=1, device_id=target, device_id_type=MESH)

    for target in (to_e, to_w, to_n, to_s):
        signal(target)

    def spread_word(number, places):
        targets = [tile(places), tile(TILES - places)]
        if places < NZ // 2:
            targets += [ring(places)[1], ring(NZ - places)[1]]
        for target in targets:
            pl.semaphore_signal(known.at[number], inc=1, device_id=target, device_id_type=MESH)

    def remote(src, dst, send_sem, recv_sem, target):
        return pltpu.make_async_remote_copy(
            src_ref=src, dst_ref=dst, send_sem=send_sem, recv_sem=recv_sem,
            device_id=target, device_id_type=MESH,
        )

    def whole(ref, number):
        return remote(ref, ref, send_sems.at[number], recv_sems.at[number], sibling)

    def halo(src, dst, number, target):
        copy = remote(src, dst, halo_send.at[number], halo_recv.at[number], target)
        copy.start()
        return copy

    level = lax.broadcasted_iota(jnp.int32, (PAD, CY), 0).astype(F32)
    lane = lax.broadcasted_iota(jnp.int32, (PAD, CY), 1)
    tail = lax.broadcasted_iota(jnp.int32, (PAD - LEV, CY), 0)
    none = jnp.zeros((PAD - LEV, CY), F32)
    for load in loads[:4]:
        load.wait()
    depth = [depth_ref[i : i + 1, :].astype(F32) for i in range(CX)]
    masks = [level[0:LEV, :] < depth[i] for i in range(CX)]
    for i in range(CX):
        at = slice(CY * i, CY * (i + 1))
        cells[0, i, 0:LEV, :] = tracer_ref[:, i, :]
        cells[0, i, LEV:PAD, :] = jnp.where(tail == 0, depth[i], 0.0)
        north_i, east_i = north_ref[:, i, :], east_ref[:, i, :]
        side[i, 0:LEV, :] = north_i
        side[i, LEV:PAD, :] = none
        side[CX + i, 0:LEV, :] = east_i
        side[CX + i, LEV:PAD, :] = none
        feat[LEV : 2 * LEV, at] = jnp.where(masks[i], east_i, 0.0)
        feat[2 * LEV : 3 * LEV, at] = jnp.where(masks[i], north_i, 0.0)
    last = lax.broadcasted_iota(jnp.int32, (ROWS - 3 * LEV, CELLS), 0)
    feat[3 * LEV : ROWS, :] = jnp.where(last < 2, 1.0, 0.0)
    side_u[...] = side[2 * CX - 1].astype(BF16)

    for load in loads[4:]:
        load.wait()
    wanted[...] = target_ref[...].astype(F32)
    edge = 3 * LEV // 16 * 16
    weights[0:edge, :] = w1_ref[0:edge, :]
    bias = b1_ref[...]
    coarse = bias.astype(BF16).astype(F32)
    row = lax.broadcasted_iota(jnp.int32, (ROWS - edge, HID), 0) + edge
    final = jnp.where(row == 3 * LEV - 1, w1_ref[3 * LEV - 1 : 3 * LEV, :].astype(F32), 0.0)
    final = jnp.where(row == 3 * LEV, coarse, final)
    final = jnp.where(row == 3 * LEV + 1, bias - coarse, final)
    weights[edge:ROWS, :] = final.astype(BF16)

    pl.semaphore_wait(barrier, 4)
    spread_word(0, 1)

    copies = [halo(side_u, halo_u, 4 * STEPS, to_e)]
    coef = None
    for step in range(STEPS):
        rows = [cells[step, i] for i in range(CX)]
        halo_out[step, 0] = rows[CX - 1].astype(BF16)
        halo_out[step, 1] = rows[0].astype(BF16)
        now = [
            halo(halo_out.at[step, 0], halo_w.at[step], 4 * step, to_e),
            halo(halo_out.at[step, 1], halo_e.at[step], 4 * step + 1, to_w),
        ]
        up = jnp.zeros((PAD, CY), F32)
        down = jnp.zeros((PAD, CY), F32)
        for i in range(CX):
            up = jnp.where(lane == i, pltpu.roll(rows[i], i + 1, 1), up)
            down = jnp.where(lane == i, pltpu.roll(rows[i], i, 1) if i else rows[i], down)
            if step == 0:
                up = jnp.where(lane == CX + i, pltpu.roll(side[i], CX + i + 1, 1), up)
        halo_out[step, 2] = up.astype(BF16)
        halo_out[step, 3] = down.astype(BF16)
        now += [
            halo(halo_out.at[step, 2], halo_s.at[step], 4 * step + 2, to_n),
            halo(halo_out.at[step, 3], halo_n.at[step], 4 * step + 3, to_s),
        ]
        for copy in now:
            copy.wait_recv()
        copies += now
        if step < 2:
            pl.semaphore_wait(known.at[step], 4)
            spread_word(step + 1, 2 * (step + 1))
        west, east = halo_w[step].astype(F32), halo_e[step].astype(F32)
        south_pack, north_pack = halo_s[step].astype(F32), halo_n[step].astype(F32)
        south_in = [pltpu.roll(south_pack, (CY - i) % CY, 1) if i else south_pack for i in range(CX)]
        north_in = [pltpu.roll(north_pack, CY - 1 - i, 1) for i in range(CX)]
        if step == 0:
            copies[0].wait_recv()
            deep = [west[LEV : LEV + 1, :]] + depth + [east[LEV : LEV + 1, :]]
            east_faces = []
            for i in range(CX + 1):
                speed = side[CX + i - 1] if i else halo_u[...].astype(F32)
                east_faces.append(faces(level < jnp.minimum(deep[i], deep[i + 1]), speed))
            coef = []
            for i in range(CX):
                here = jnp.broadcast_to(depth[i], (PAD, CY))
                there = jnp.where(
                    lane == CY - 1,
                    jnp.broadcast_to(north_in[i][LEV : LEV + 1, :], (PAD, CY)),
                    pltpu.roll(here, CY - 1, 1),
                )
                shut_n = jnp.logical_and(lane == CY - 1, p == TILES - 1)
                near_n, far_n = faces(
                    jnp.logical_and(level < jnp.minimum(here, there), jnp.logical_not(shut_n)), side[i]
                )
                below = jnp.broadcast_to(south_in[i][LEV : LEV + 1, :], (PAD, CY))
                near_b, far_b = faces(
                    jnp.logical_and(level < jnp.minimum(here, below), p != 0),
                    pltpu.roll(south_pack, CY - CX - i, 1),
                )
                near_s = jnp.where(lane == 0, near_b, pltpu.roll(near_n, 1, 1))
                far_s = jnp.where(lane == 0, far_b, pltpu.roll(far_n, 1, 1))
                near_w, far_w = east_faces[i]
                near_e, far_e = east_faces[i + 1]
                coef.append((1.0 + far_w - near_e + far_s - near_n, near_w, far_e, near_s, far_n))
        wide = [west] + rows + [east]
        for i in range(CX):
            keep, near_w, far_e, near_s, far_n = coef[i]
            south = jnp.where(lane == 0, south_in[i], pltpu.roll(rows[i], 1, 1))
            north = jnp.where(lane == CY - 1, north_in[i], pltpu.roll(rows[i], CY - 1, 1))
            cells[step + 1, i] = (
                keep * rows[i] + near_w * wide[i] - far_e * wide[i + 2] + near_s * south - far_n * north
            )

    for i in range(CX):
        at = slice(CY * i, CY * (i + 1))
        feat[0:LEV, at] = jnp.where(masks[i], cells[STEPS, i, 0:LEV, :], 0.0)
    inputs = feat[...].astype(BF16)

    acc = None
    for b in range(HID // BLK):
        at = slice(b * BLK, (b + 1) * BLK)
        before = dot(weights[:, at], inputs, ((0,), (0,)))
        stash = before.astype(BF16).astype(F32)
        gate = 0.5 * jnp.tanh(0.5 * stash) + 0.5
        act = (stash * gate).astype(BF16)
        hidden[at, :] = act
        slope[at, :] = gate * (1.0 + stash * (1.0 - gate))
        part = dot(w2_ref[:, at], act, ((1,), (0,)))
        acc = part if acc is None else acc + part
    pl.semaphore_wait(known.at[2], 4)
    spread_word(3, 8)
    eye = lax.broadcasted_iota(jnp.int32, (LEV, LEV), 0) == lax.broadcasted_iota(jnp.int32, (LEV, LEV), 1)
    bias2 = jnp.sum(jnp.where(eye, b2_ref[...], 0.0), axis=1, keepdims=True)
    output = acc + bias2
    total[...] = jnp.zeros((PAD, CELLS), F32)
    for i in range(CX):
        at = slice(CY * i, CY * (i + 1))
        tendency = jnp.where(masks[i], output[:, at], 0.0).astype(BF16).astype(F32)
        goal = jnp.where(masks[i], wanted[:, i, :], 0.0)
        misfit = tendency - goal
        total[0:LEV, at] = misfit * (1.0 / COLUMNS)
        fresh_out[i, 0:LEV, :] = cells[STEPS, i, 0:LEV, :] + tendency
        misfit_out[i, 0:LEV, :] = misfit
    d_out = total[...].astype(BF16)
    ones = jnp.ones((16, CELLS), BF16)
    bias_grad = dot(ones, d_out, ((1,), (1,)))
    spread = lax.broadcasted_iota(jnp.int32, (PAD, CY), 0) == LEV
    per = BLK // CY
    to_sibling = []
    for b in range(HID // BLK):
        at = slice(b * BLK, (b + 1) * BLK)
        d_hidden = dot(w2_ref[:, at], d_out[0:LEV, :], ((0,), (0,)))
        d_before = (d_hidden * slope[at, :]).astype(BF16)
        g1 = dot(inputs, d_before, ((1,), (1,)))
        g2 = dot(d_out, hidden[at, :], ((1,), (1,)))
        for t in range(per):
            lanes = slice(t * CY, (t + 1) * CY)
            tile = b * per + t
            for g in range(3):
                chunks[g % 2, 2 * tile + g // 2] = g1[PAD * g : PAD * (g + 1), lanes]
            last_part = g2[:, lanes]
            if tile == 0:
                row = jnp.concatenate([bias_grad[0:1, :], jnp.zeros((1, CY - PAD), F32)], axis=1)
                last_part = jnp.where(spread, row, last_part)
            chunks[1, 2 * tile + 1] = last_part
        some = pl.ds(2 * per * b, 2 * per)
        copy = remote(chunks.at[1 - core, some], core_in.at[some], core_send.at[b], core_recv.at[b], sibling)
        copy.start()
        to_sibling.append(copy)
    row = lax.broadcasted_iota(jnp.int32, (PAD, CY), 0)
    bias_row = 3 * LEV - 2 * PAD + core * (LEV - (3 * LEV - 2 * PAD))
    for b in range(HID // BLK):
        to_sibling[b].wait_recv()
        some = pl.ds(2 * per * b, 2 * per)
        both = chunks[core, some] + core_in[some]
        for j in range(2 * per):
            value = both[j]
            sent = value
            if j % 2:
                low = value - value.astype(BF16).astype(F32)
                value = jnp.where(row == bias_row + 1, 0.0, value)
                sent = jnp.where(row == bias_row + 1, pltpu.roll(low, 1, 0), value)
            summed[2 * per * b + j] = value
            sending[2 * per * b + j] = sent.astype(BF16)

    pl.semaphore_wait(known.at[3], 2)

    def scatter(k, carry):
        c, target = other_chip(k)
        remote(sending.at[c], landed.at[k - 1], send_sems.at[0], recv_sems.at[0], target).start()
        return carry

    lax.fori_loop(1, CHIPS, scatter, 0)
    whole(landed, 0).wait_recv()
    amount = summed[chip]
    for k in range(CHIPS - 1):
        amount = amount + landed[k].astype(F32)
    mine[...] = amount
    part = PAD // NZ
    for k in range(NZ):
        strips[k] = mine[part * k : part * (k + 1), :]

    def scatter_ring(j, carry):
        k = far_first(j)
        w, target = ring(k)
        remote(strips.at[w], strips_in.at[k - 1], send_sems.at[1], recv_sems.at[1], target).start()
        return carry

    lax.fori_loop(0, NZ - 1, scatter_ring, 0)
    whole(strips_in, 1).wait_recv()
    strip = strips[z]
    for k in range(NZ - 1):
        strip = strip + strips_in[k]
    strips_all[NZ - 1] = strip

    def gather_ring(j, carry):
        k = far_first(j)
        _, target = ring(k)
        remote(
            strips_all.at[NZ - 1], strips_all.at[k - 1], send_sems.at[2], recv_sems.at[2], target
        ).start()
        return carry

    lax.fori_loop(0, NZ - 1, gather_ring, 0)
    arrived = strips_all.at[0 : NZ - 1]
    whole(arrived, 2).wait_recv()
    for k in range(NZ):
        place_in = lax.rem(z - k + NZ - 1 + NZ, NZ)
        mine[part * k : part * (k + 1), :] = strips_all[place_in]
    has_bias = lax.rem(chip, 2) == 1
    value = mine[...]
    both = jnp.where(jnp.logical_and(row == bias_row, has_bias), pltpu.roll(value, PAD - 1, 0), 0.0) + value
    low = both - both.astype(BF16).astype(F32)
    both = jnp.where(jnp.logical_and(row == bias_row + 1, has_bias), pltpu.roll(low, 1, 0), both)
    chunk[...] = both.astype(BF16)
    gathered[core, chip] = chunk[...]

    def gather(k, carry):
        _, target = other_chip(k)
        remote(chunk, gathered.at[core, chip], send_sems.at[3], recv_sems.at[3], target).start()
        return carry

    lax.fori_loop(1, CHIPS, gather, 0)
    whole(landed, 3).wait_recv()
    forward = remote(gathered.at[core], gathered.at[core], send_sems.at[4], recv_sems.at[4], sibling)
    forward.start()
    for copy in copies + to_sibling:
        copy.wait_send()
    whole(landed, 0).wait_send()
    whole(strips_in, 1).wait_send()
    whole(arrived, 2).wait_send()
    whole(landed, 3).wait_send()
    forward.wait()


def main(*operands):
    vmem = pl.BlockSpec(memory_space=pltpu.VMEM)
    hbm = pl.BlockSpec(memory_space=pltpu.HBM)
    part = PAD // NZ
    halves = HID // BLK
    halo = pltpu.VMEM((STEPS, PAD, CY), BF16)
    return pl.pallas_call(
        main_kernel,
        out_shape=(
            jax.ShapeDtypeStruct((CX, PAD, CY), F32),
            jax.ShapeDtypeStruct((CX, PAD, CY), F32),
            jax.ShapeDtypeStruct((2, CHIPS, PAD, CY), BF16),
        ),
        in_specs=[hbm] * 9,
        out_specs=(vmem,) * 3,
        scratch_shapes=[pltpu.VMEM(a.shape, a.dtype) for a in operands]
        + [
            pltpu.VMEM((STEPS + 1, CX, PAD, CY), F32),
            pltpu.VMEM((2 * CX, PAD, CY), F32),
            pltpu.VMEM((PAD, CY), BF16),
            pltpu.VMEM((STEPS, 4, PAD, CY), BF16),
            halo, halo, halo, halo,
            pltpu.VMEM((PAD, CY), BF16),
            pltpu.VMEM((ROWS, CELLS), F32),
            pltpu.VMEM((ROWS, HID), BF16),
            pltpu.VMEM((HID, CELLS), BF16),
            pltpu.VMEM((HID, CELLS), F32),
            pltpu.VMEM((PAD, CELLS), F32),
            pltpu.VMEM((LEV, CX, CY), F32),
            pltpu.VMEM((2, CHIPS, PAD, CY), F32),
            pltpu.VMEM((CHIPS, PAD, CY), F32),
            pltpu.VMEM((CHIPS, PAD, CY), F32),
            pltpu.VMEM((CHIPS, PAD, CY), BF16),
            pltpu.VMEM((CHIPS - 1, PAD, CY), BF16),
            pltpu.VMEM((PAD, CY), F32),
            pltpu.VMEM((NZ, part, CY), F32),
            pltpu.VMEM((NZ - 1, part, CY), F32),
            pltpu.VMEM((NZ, part, CY), F32),
            pltpu.VMEM((PAD, CY), BF16),
            pltpu.SemaphoreType.DMA((len(operands),)),
            pltpu.SemaphoreType.DMA((4 * STEPS + 1,)),
            pltpu.SemaphoreType.DMA((4 * STEPS + 1,)),
            pltpu.SemaphoreType.DMA((halves,)),
            pltpu.SemaphoreType.DMA((halves,)),
            pltpu.SemaphoreType.DMA((5,)),
            pltpu.SemaphoreType.DMA((5,)),
            pltpu.SemaphoreType.REGULAR((4,)),
        ],
        compiler_params=pltpu.CompilerParams(
            collective_id=0, has_side_effects=True, vmem_limit_bytes=VMEM_LIMIT
        ),
        name="main",
    )(*(pltpu.with_memory_space_constraint(a, pltpu.HBM) for a in operands))


def unpack_kernel(fresh, misfit, chunks, tracer_out, misfit_out, w1_ref, b1_ref, w2_ref, b2_ref, wide):
    for i in range(CX):
        tracer_out[:, i, :] = fresh[i, 0:LEV, :]
        wide[:, i, :] = misfit[i, 0:LEV, :]
    misfit_out[...] = wide[...].astype(BF16)
    rest = 3 * LEV - 2 * PAD
    for t in range(HID // CY):
        lanes = slice(t * CY, (t + 1) * CY)
        for g in range(2):
            w1_ref[PAD * g : PAD * (g + 1), lanes] = chunks[g % 2, 2 * t + g // 2].astype(F32)
        third = chunks[0, 2 * t + 1].astype(F32)
        w1_ref[2 * PAD : 3 * LEV, lanes] = third[0:rest, :]
        b1_ref[:, lanes] = third[rest : rest + 1, :] + third[rest + 1 : rest + 2, :]
        fourth = chunks[1, 2 * t + 1].astype(F32)
        w2_ref[:, lanes] = fourth[0:LEV, :]
        if t == 0:
            b2_ref[...] = fourth[LEV : LEV + 1, 0:LEV] + fourth[LEV + 1 : LEV + 2, 0:LEV]


def unpack(fresh, misfit, chunks):
    vmem = pl.BlockSpec(memory_space=pltpu.VMEM)
    return pl.pallas_call(
        unpack_kernel,
        out_shape=(
            jax.ShapeDtypeStruct((LEV, CX, CY), F32),
            jax.ShapeDtypeStruct((LEV, CX, CY), BF16),
            jax.ShapeDtypeStruct((3 * LEV, HID), F32),
            jax.ShapeDtypeStruct((1, HID), F32),
            jax.ShapeDtypeStruct((LEV, HID), F32),
            jax.ShapeDtypeStruct((1, LEV), F32),
        ),
        in_specs=[vmem] * 3,
        out_specs=(vmem,) * 6,
        scratch_shapes=[pltpu.VMEM((LEV, CX, CY), F32)],
        compiler_params=pltpu.CompilerParams(vmem_limit_bytes=VMEM_LIMIT),
        name="unpack",
    )(fresh, misfit, chunks)


def on_device(tracer, east, north, target, depth, slots, w1, b1, w2, b2):
    fresh, misfit, chunks = main(
        tracer, east, north, target, depth, w1, b1.reshape(1, HID), w2.T, b2.reshape(1, LEV)
    )
    tracer_out, misfit_out, grad_w1, grad_b1, grad_w2, grad_b2 = unpack(fresh, misfit, chunks)
    return tracer_out, misfit_out, grad_w1, grad_b1.reshape(HID), grad_w2.T, grad_b2.reshape(LEV)


def solution(mesh):
    grid = P(None, "ocx", ("ocy", "ml"))
    return jax.shard_map(
        on_device,
        mesh=mesh,
        in_specs=(grid, grid, grid, grid, P("ocx", ("ocy", "ml")), P("ocx", ("ocy", "ml"), None, None), P(), P(), P(), P()),
        out_specs=(grid, grid, P(), P(), P(), P()),
        check_vma=False,
    )
```

```python
import jax
import jax.numpy as jnp
from jax import lax
from jax.experimental import pallas as pl
from jax.experimental.pallas import tpu as pltpu
from jax.sharding import PartitionSpec as P

MESH = pl.DeviceIdType.MESH
KAPPA = 0.1
STEPS = 3
LEV = 75
PAD = 80
CX = 4
CY = 128
CELLS = CX * CY
HID = 1024
ROWS = 240
TILES = 32
NZ = 16
CHIPS = 16
COLUMNS = 262144
REACH = 3
WIDE = CX + 2 * REACH
STRIP = 2 * REACH
NORTH_AT = (0, 1, 10, 11)
EAST_AT = (2, 6, 8, 9)
CELL_AT = (3, 4, 5, 7)
BLK = 256
F32 = jnp.float32
BF16 = jnp.bfloat16
VMEM_LIMIT = 40 * 1024 * 1024


def place(p):
    return lax.div(p, 8), lax.rem(p, 8)


def faces(opened, speed):
    near = jnp.where(opened, jnp.maximum(speed, 0.0) + KAPPA, 0.0)
    far = jnp.where(opened, jnp.minimum(speed, 0.0) - KAPPA, 0.0)
    return near, far


def dot(a, b, dims):
    return lax.dot_general(a, b, (dims, ((), ())), preferred_element_type=F32)


def main_kernel(
    tracer_hbm, east_hbm, north_hbm, target_hbm, depth_hbm, w1_hbm, b1_hbm, w2_hbm, b2_hbm,
    fresh_out, misfit_out, gathered,
    tracer_ref, east_ref, north_ref, target_ref, depth_ref, w1_ref, b1_ref, w2_ref, b2_ref,
    cells, north_own, east_own, rows_out, edges_out, halo_w, halo_e, halo_edges, pick_out, pick_rows, pick_edges,
    feat, weights, hidden, slope, total, wanted, chunks, core_in, summed, sending, landed,
    mine, strips, strips_in, strips_all, chunk,
    load_sems, halo_send, halo_recv, core_send, core_recv, send_sems, recv_sems, known,
):
    z, x, m = lax.axis_index("ocx"), lax.axis_index("ocy"), lax.axis_index("ml")
    core = lax.rem(m, 2)
    chip = x * 4 + lax.div(m, 2)
    p = x * 8 + m
    sibling = (z, x, m + 1 - 2 * core)

    def other_chip(k):
        c = lax.rem(chip + k, CHIPS)
        return c, (z, lax.div(c, 4), lax.rem(c, 4) * 2 + core)

    def ring(k):
        w = lax.rem(z + k, NZ)
        return w, (w, x, m)

    def far_first(j):
        half = lax.div(j + 1, 2)
        return NZ // 2 + half * (1 - 2 * lax.rem(j, 2))

    def tile(k):
        return (z, *place(lax.rem(p + k, TILES)))

    to_e, to_w = ring(1)[1], ring(NZ - 1)[1]
    to_n, to_s = tile(1), tile(TILES - 1)

    pairs = (
        (depth_hbm, depth_ref), (tracer_hbm, tracer_ref), (north_hbm, north_ref), (east_hbm, east_ref),
        (target_hbm, target_ref), (w1_hbm, w1_ref), (b1_hbm, b1_ref), (w2_hbm, w2_ref), (b2_hbm, b2_ref),
    )
    loads = [pltpu.make_async_copy(src, dst, load_sems.at[i]) for i, (src, dst) in enumerate(pairs)]
    for load in loads:
        load.start()

    barrier = pltpu.get_barrier_semaphore()

    def signal(target):
        pl.semaphore_signal(barrier, inc=1, device_id=target, device_id_type=MESH)

    def diagonal(dz, k):
        return (lax.rem(z + dz, NZ), *tile(k)[1:])

    to_ne, to_nw = diagonal(1, 1), diagonal(NZ - 1, 1)
    to_se, to_sw = diagonal(1, TILES - 1), diagonal(NZ - 1, TILES - 1)
    for target in (to_e, to_w, to_n, to_s, to_ne, to_nw, to_se, to_sw):
        signal(target)

    def spread_word(number, places):
        targets = [tile(places), tile(TILES - places)]
        if places < NZ // 2:
            targets += [ring(places)[1], ring(NZ - places)[1]]
        for target in targets:
            pl.semaphore_signal(known.at[number], inc=1, device_id=target, device_id_type=MESH)

    def remote(src, dst, send_sem, recv_sem, target):
        return pltpu.make_async_remote_copy(
            src_ref=src, dst_ref=dst, send_sem=send_sem, recv_sem=recv_sem,
            device_id=target, device_id_type=MESH,
        )

    def whole(ref, number):
        return remote(ref, ref, send_sems.at[number], recv_sems.at[number], sibling)

    def halo(src, dst, number, target):
        copy = remote(src, dst, halo_send.at[number], halo_recv.at[number], target)
        copy.start()
        return copy

    lane_in = lax.broadcasted_iota(jnp.int32, (CY, 2 * CY), 0)
    lane_out = lax.broadcasted_iota(jnp.int32, (CY, 2 * CY), 1)
    shift = jnp.where(lane_in >= CY - REACH, lane_out - lane_in + (CY - REACH), -999)
    shift = jnp.where(lane_in < REACH, lane_out - lane_in - CY, shift)
    for f, order in enumerate((CELL_AT, EAST_AT, NORTH_AT)):
        for i in range(CX):
            at = slice(CY * order[i], CY * (order[i] + 1))
            pick_out[at, :] = jnp.where(shift == 16 * f + 4 * i, 1.0, 0.0).astype(BF16)
    lane_in = lax.broadcasted_iota(jnp.int32, (CY, CY), 0)
    lane_out = lax.broadcasted_iota(jnp.int32, (CY, CY), 1)
    shift = jnp.where(lane_in >= CY - REACH, lane_out - lane_in + (CY - REACH) - CY // 2, -999)
    shift = jnp.where(lane_in < REACH, lane_out - lane_in - REACH, shift)
    for n in range(WIDE):
        pick_rows[CY * n : CY * (n + 1), :] = jnp.where(shift == STRIP * n, 1.0, 0.0).astype(BF16)
    lane_in = lax.broadcasted_iota(jnp.int32, (CY, 3 * CY), 0)
    lane_out = lax.broadcasted_iota(jnp.int32, (CY, 3 * CY), 1)
    field, owner, nth = lane_in // 16, (lane_in // 4) % 4, lane_in % 4
    shift = lane_out - (CY * field + STRIP * owner + nth)
    shift = jnp.where(jnp.logical_and(field < 3, nth < REACH), shift, -999)
    for n in range(6):
        dz = (0, -1, 1)[n % 3]
        here = (n // 3) * (CY // 2 + REACH) + STRIP * (REACH + CX * dz)
        hit = shift == here
        if dz == -1:
            hit = jnp.logical_and(hit, owner >= 1)
        if dz == 1:
            hit = jnp.logical_and(hit, owner <= REACH - 1)
        pick_edges[CY * n : CY * (n + 1), :] = jnp.where(hit, 1.0, 0.0).astype(BF16)

    level = lax.broadcasted_iota(jnp.int32, (PAD, CY), 0).astype(F32)
    lane = lax.broadcasted_iota(jnp.int32, (PAD, CY), 1)
    tail = lax.broadcasted_iota(jnp.int32, (PAD - LEV, CY), 0)
    none = jnp.zeros((PAD - LEV, CY), F32)
    for load in loads[:4]:
        load.wait()
    depth = [depth_ref[i : i + 1, :].astype(F32) for i in range(CX)]
    for i in range(CX):
        cells[i, 0:LEV, :] = tracer_ref[:, i, :]
        cells[i, LEV:PAD, :] = jnp.where(tail == 0, depth[i], 0.0)
        north_own[i, 0:LEV, :] = north_ref[:, i, :]
        north_own[i, LEV:PAD, :] = none
        east_own[i, 0:LEV, :] = east_ref[:, i, :]
        east_own[i, LEV:PAD, :] = none
        rows_out[CELL_AT[i]] = cells[i].astype(BF16)
        rows_out[EAST_AT[i]] = east_own[i].astype(BF16)
        rows_out[NORTH_AT[i]] = north_own[i].astype(BF16)
    edges = dot(jnp.concatenate([rows_out[n] for n in range(3 * CX)], axis=1), pick_out[...], ((1,), (0,)))
    edges_out[0] = edges[:, 0:CY].astype(BF16)
    edges_out[1] = edges[:, CY : 2 * CY].astype(BF16)

    pl.semaphore_wait(barrier, 8)
    copies = [
        halo(rows_out.at[4:12], halo_w, 0, to_e),
        halo(rows_out.at[0:7], halo_e, 1, to_w),
        halo(edges_out.at[0], halo_edges.at[0], 2, to_n),
        halo(edges_out.at[0], halo_edges.at[1], 3, to_ne),
        halo(edges_out.at[0], halo_edges.at[2], 4, to_nw),
        halo(edges_out.at[1], halo_edges.at[3], 5, to_s),
        halo(edges_out.at[1], halo_edges.at[4], 6, to_se),
        halo(edges_out.at[1], halo_edges.at[5], 7, to_sw),
    ]
    spread_word(0, 1)

    masks = [level[0:LEV, :] < depth[i] for i in range(CX)]
    for i in range(CX):
        at = slice(CY * i, CY * (i + 1))
        feat[LEV : 2 * LEV, at] = jnp.where(masks[i], east_own[i, 0:LEV, :], 0.0)
        feat[2 * LEV : 3 * LEV, at] = jnp.where(masks[i], north_own[i, 0:LEV, :], 0.0)
    last = lax.broadcasted_iota(jnp.int32, (ROWS - 3 * LEV, CELLS), 0)
    feat[3 * LEV : ROWS, :] = jnp.where(last < 2, 1.0, 0.0)
    for load in loads[4:]:
        load.wait()
    wanted[...] = target_ref[...].astype(F32)
    edge = 3 * LEV // 16 * 16
    weights[0:edge, :] = w1_ref[0:edge, :]
    bias = b1_ref[...]
    coarse = bias.astype(BF16).astype(F32)
    row = lax.broadcasted_iota(jnp.int32, (ROWS - edge, HID), 0) + edge
    final = jnp.where(row == 3 * LEV - 1, w1_ref[3 * LEV - 1 : 3 * LEV, :].astype(F32), 0.0)
    final = jnp.where(row == 3 * LEV, coarse, final)
    final = jnp.where(row == 3 * LEV + 1, bias - coarse, final)
    weights[edge:ROWS, :] = final.astype(BF16)

    pl.semaphore_wait(known.at[0], 4)
    spread_word(1, 2)
    for copy in copies:
        copy.wait_recv()

    cell_rows = [halo_w[0], halo_w[1], halo_w[3]] + [rows_out[n] for n in CELL_AT] + [halo_e[3], halo_e[4], halo_e[5]]
    east_rows = [halo_w[2], halo_w[4], halo_w[5]] + [rows_out[n] for n in EAST_AT] + [halo_e[2], halo_e[6]]
    north_rows = [halo_w[6], halo_w[7]] + [rows_out[n] for n in NORTH_AT] + [halo_e[0], halo_e[1]]
    beyond = dot(jnp.concatenate([halo_edges[n] for n in range(6)], axis=1), pick_edges[...], ((1,), (0,)))

    def strip_of(some, first, f):
        own = dot(
            jnp.concatenate(some, axis=1), pick_rows[CY * first : CY * (first + len(some)), :], ((1,), (0,))
        )
        return own + beyond[:, CY * f : CY * (f + 1)]

    def turn(value, by):
        by = by % CY
        return pltpu.roll(value, by, 1) if by else value

    strip = strip_of(cell_rows, 0, 0)
    deep_here = jnp.broadcast_to(strip[LEV : LEV + 1, :], (PAD, CY))
    near_e, far_e = faces(level < jnp.minimum(deep_here, turn(deep_here, -STRIP)), strip_of(east_rows, 0, 1))
    nth = lane % (CY // 2)
    nth = nth - STRIP * ((nth * 43) // 256)
    border = jnp.logical_or(
        jnp.logical_and(lane < CY // 2, p == 0), jnp.logical_and(lane >= CY // 2, p == TILES - 1)
    )
    shut = jnp.logical_and(nth == REACH - 1, border)
    opened = jnp.logical_and(level < jnp.minimum(deep_here, turn(deep_here, -1)), jnp.logical_not(shut))
    strip_near, strip_far = faces(opened, strip_of(north_rows, 1, 2))
    near_w, far_w = turn(near_e, STRIP), turn(far_e, STRIP)
    near_s, far_s = turn(strip_near, 1), turn(strip_far, 1)
    strip_coef = (1.0 + far_w - near_e + far_s - strip_near, near_w, far_e, near_s, strip_far)
    strips_at = [strip]
    for step in range(STEPS - 1):
        keep, near_w, far_e, near_s, far_n = strip_coef
        strip = (
            keep * strip + near_w * turn(strip, STRIP) - far_e * turn(strip, -STRIP)
            + near_s * turn(strip, 1) - far_n * turn(strip, -1)
        )
        strips_at.append(strip)

    now = [
        cells[n - REACH] if REACH <= n < REACH + CX else cell_rows[n].astype(F32) for n in range(WIDE)
    ]
    deep = [jnp.broadcast_to(value[LEV : LEV + 1, :], (PAD, CY)) for value in now]
    east_faces = []
    for n in range(WIDE - 1):
        speed = east_own[n - REACH] if REACH <= n < REACH + CX else east_rows[n].astype(F32)
        east_faces.append(faces(level < jnp.minimum(deep[n], deep[n + 1]), speed))
    shut_n = jnp.logical_and(lane == CY - 1, p == TILES - 1)
    coef = [None] * WIDE
    for n in range(1, WIDE - 1):
        speed = north_own[n - REACH] if REACH <= n < REACH + CX else north_rows[n - 1].astype(F32)
        there = jnp.where(
            lane == CY - 1, turn(deep_here, CY - 1 - (CY // 2 + STRIP * n + REACH)), turn(deep[n], -1)
        )
        opened = jnp.logical_and(level < jnp.minimum(deep[n], there), jnp.logical_not(shut_n))
        near_n, far_n = faces(opened, speed)
        below = -(STRIP * n + REACH - 1)
        near_s = jnp.where(lane == 0, turn(strip_near, below), turn(near_n, 1))
        far_s = jnp.where(lane == 0, turn(strip_far, below), turn(far_n, 1))
        near_w, far_w = east_faces[n - 1]
        near_e, far_e = east_faces[n]
        coef[n] = (1.0 + far_w - near_e + far_s - near_n, near_w, far_e, near_s, far_n)
    for step in range(STEPS):
        after = list(now)
        for n in range(step + 1, WIDE - 1 - step):
            keep, near_w, far_e, near_s, far_n = coef[n]
            strip = strips_at[step]
            south = jnp.where(lane == 0, turn(strip, -(STRIP * n + REACH - 1)), turn(now[n], 1))
            north = jnp.where(
                lane == CY - 1, turn(strip, CY - 1 - (CY // 2 + STRIP * n + REACH)), turn(now[n], -1)
            )
            after[n] = (
                keep * now[n] + near_w * now[n - 1] - far_e * now[n + 1] + near_s * south - far_n * north
            )
        now = after
    for i in range(CX):
        cells[i] = now[REACH + i]
    pl.semaphore_wait(known.at[1], 4)
    spread_word(2, 4)

    for i in range(CX):
        at = slice(CY * i, CY * (i + 1))
        feat[0:LEV, at] = jnp.where(masks[i], cells[i, 0:LEV, :], 0.0)
    inputs = feat[...].astype(BF16)

    acc = None
    for b in range(HID // BLK):
        at = slice(b * BLK, (b + 1) * BLK)
        before = dot(weights[:, at], inputs, ((0,), (0,)))
        stash = before.astype(BF16).astype(F32)
        gate = 0.5 * jnp.tanh(0.5 * stash) + 0.5
        act = (stash * gate).astype(BF16)
        hidden[at, :] = act
        slope[at, :] = gate * (1.0 + stash * (1.0 - gate))
        part = dot(w2_ref[:, at], act, ((1,), (0,)))
        acc = part if acc is None else acc + part
    pl.semaphore_wait(known.at[2], 4)
    spread_word(3, 8)
    eye = lax.broadcasted_iota(jnp.int32, (LEV, LEV), 0) == lax.broadcasted_iota(jnp.int32, (LEV, LEV), 1)
    bias2 = jnp.sum(jnp.where(eye, b2_ref[...], 0.0), axis=1, keepdims=True)
    output = acc + bias2
    total[...] = jnp.zeros((PAD, CELLS), F32)
    for i in range(CX):
        at = slice(CY * i, CY * (i + 1))
        tendency = jnp.where(masks[i], output[:, at], 0.0).astype(BF16).astype(F32)
        goal = jnp.where(masks[i], wanted[:, i, :], 0.0)
        misfit = tendency - goal
        total[0:LEV, at] = misfit * (1.0 / COLUMNS)
        fresh_out[i, 0:LEV, :] = cells[i, 0:LEV, :] + tendency
        misfit_out[i, 0:LEV, :] = misfit
    d_out = total[...].astype(BF16)
    ones = jnp.ones((16, CELLS), BF16)
    bias_grad = dot(ones, d_out, ((1,), (1,)))
    spread = lax.broadcasted_iota(jnp.int32, (PAD, CY), 0) == LEV
    per = BLK // CY
    to_sibling = []
    for b in range(HID // BLK):
        at = slice(b * BLK, (b + 1) * BLK)
        d_hidden = dot(w2_ref[:, at], d_out[0:LEV, :], ((0,), (0,)))
        d_before = (d_hidden * slope[at, :]).astype(BF16)
        g1 = dot(inputs, d_before, ((1,), (1,)))
        g2 = dot(d_out, hidden[at, :], ((1,), (1,)))
        for t in range(per):
            lanes = slice(t * CY, (t + 1) * CY)
            tile = b * per + t
            for g in range(3):
                chunks[g % 2, 2 * tile + g // 2] = g1[PAD * g : PAD * (g + 1), lanes]
            last_part = g2[:, lanes]
            if tile == 0:
                row = jnp.concatenate([bias_grad[0:1, :], jnp.zeros((1, CY - PAD), F32)], axis=1)
                last_part = jnp.where(spread, row, last_part)
            chunks[1, 2 * tile + 1] = last_part
        some = pl.ds(2 * per * b, 2 * per)
        copy = remote(chunks.at[1 - core, some], core_in.at[some], core_send.at[b], core_recv.at[b], sibling)
        copy.start()
        to_sibling.append(copy)
    row = lax.broadcasted_iota(jnp.int32, (PAD, CY), 0)
    bias_row = 3 * LEV - 2 * PAD + core * (LEV - (3 * LEV - 2 * PAD))
    for b in range(HID // BLK):
        to_sibling[b].wait_recv()
        some = pl.ds(2 * per * b, 2 * per)
        both = chunks[core, some] + core_in[some]
        for j in range(2 * per):
            value = both[j]
            sent = value
            if j % 2:
                low = value - value.astype(BF16).astype(F32)
                value = jnp.where(row == bias_row + 1, 0.0, value)
                sent = jnp.where(row == bias_row + 1, pltpu.roll(low, 1, 0), value)
            summed[2 * per * b + j] = value
            sending[2 * per * b + j] = sent.astype(BF16)

    pl.semaphore_wait(known.at[3], 2)

    def scatter(k, carry):
        c, target = other_chip(k)
        remote(sending.at[c], landed.at[k - 1], send_sems.at[0], recv_sems.at[0], target).start()
        return carry

    lax.fori_loop(1, CHIPS, scatter, 0)
    whole(landed, 0).wait_recv()
    amount = summed[chip]
    for k in range(CHIPS - 1):
        amount = amount + landed[k].astype(F32)
    mine[...] = amount
    part = PAD // NZ
    for k in range(NZ):
        strips[k] = mine[part * k : part * (k + 1), :]

    def scatter_ring(j, carry):
        k = far_first(j)
        w, target = ring(k)
        remote(strips.at[w], strips_in.at[k - 1], send_sems.at[1], recv_sems.at[1], target).start()
        return carry

    lax.fori_loop(0, NZ - 1, scatter_ring, 0)
    whole(strips_in, 1).wait_recv()
    strip = strips[z]
    for k in range(NZ - 1):
        strip = strip + strips_in[k]
    strips_all[NZ - 1] = strip

    def gather_ring(j, carry):
        k = far_first(j)
        _, target = ring(k)
        remote(
            strips_all.at[NZ - 1], strips_all.at[k - 1], send_sems.at[2], recv_sems.at[2], target
        ).start()
        return carry

    lax.fori_loop(0, NZ - 1, gather_ring, 0)
    arrived = strips_all.at[0 : NZ - 1]
    whole(arrived, 2).wait_recv()
    for k in range(NZ):
        place_in = lax.rem(z - k + NZ - 1 + NZ, NZ)
        mine[part * k : part * (k + 1), :] = strips_all[place_in]
    has_bias = lax.rem(chip, 2) == 1
    value = mine[...]
    both = jnp.where(jnp.logical_and(row == bias_row, has_bias), pltpu.roll(value, PAD - 1, 0), 0.0) + value
    low = both - both.astype(BF16).astype(F32)
    both = jnp.where(jnp.logical_and(row == bias_row + 1, has_bias), pltpu.roll(low, 1, 0), both)
    chunk[...] = both.astype(BF16)
    gathered[core, chip] = chunk[...]

    def gather(k, carry):
        _, target = other_chip(k)
        remote(chunk, gathered.at[core, chip], send_sems.at[3], recv_sems.at[3], target).start()
        return carry

    lax.fori_loop(1, CHIPS, gather, 0)
    whole(landed, 3).wait_recv()
    forward = remote(gathered.at[core], gathered.at[core], send_sems.at[4], recv_sems.at[4], sibling)
    forward.start()
    for copy in copies + to_sibling:
        copy.wait_send()
    whole(landed, 0).wait_send()
    whole(strips_in, 1).wait_send()
    whole(arrived, 2).wait_send()
    whole(landed, 3).wait_send()
    forward.wait()


def main(*operands):
    vmem = pl.BlockSpec(memory_space=pltpu.VMEM)
    hbm = pl.BlockSpec(memory_space=pltpu.HBM)
    part = PAD // NZ
    halves = HID // BLK
    return pl.pallas_call(
        main_kernel,
        out_shape=(
            jax.ShapeDtypeStruct((CX, PAD, CY), F32),
            jax.ShapeDtypeStruct((CX, PAD, CY), F32),
            jax.ShapeDtypeStruct((2, CHIPS, PAD, CY), BF16),
        ),
        in_specs=[hbm] * 9,
        out_specs=(vmem,) * 3,
        scratch_shapes=[pltpu.VMEM(a.shape, a.dtype) for a in operands]
        + [
            pltpu.VMEM((CX, PAD, CY), F32),
            pltpu.VMEM((CX, PAD, CY), F32),
            pltpu.VMEM((CX, PAD, CY), F32),
            pltpu.VMEM((3 * CX, PAD, CY), BF16),
            pltpu.VMEM((2, PAD, CY), BF16),
            pltpu.VMEM((8, PAD, CY), BF16),
            pltpu.VMEM((7, PAD, CY), BF16),
            pltpu.VMEM((6, PAD, CY), BF16),
            pltpu.VMEM((3 * CX * CY, 2 * CY), BF16),
            pltpu.VMEM((WIDE * CY, CY), BF16),
            pltpu.VMEM((6 * CY, 3 * CY), BF16),
            pltpu.VMEM((ROWS, CELLS), F32),
            pltpu.VMEM((ROWS, HID), BF16),
            pltpu.VMEM((HID, CELLS), BF16),
            pltpu.VMEM((HID, CELLS), F32),
            pltpu.VMEM((PAD, CELLS), F32),
            pltpu.VMEM((LEV, CX, CY), F32),
            pltpu.VMEM((2, CHIPS, PAD, CY), F32),
            pltpu.VMEM((CHIPS, PAD, CY), F32),
            pltpu.VMEM((CHIPS, PAD, CY), F32),
            pltpu.VMEM((CHIPS, PAD, CY), BF16),
            pltpu.VMEM((CHIPS - 1, PAD, CY), BF16),
            pltpu.VMEM((PAD, CY), F32),
            pltpu.VMEM((NZ, part, CY), F32),
            pltpu.VMEM((NZ - 1, part, CY), F32),
            pltpu.VMEM((NZ, part, CY), F32),
            pltpu.VMEM((PAD, CY), BF16),
            pltpu.SemaphoreType.DMA((len(operands),)),
            pltpu.SemaphoreType.DMA((8,)),
            pltpu.SemaphoreType.DMA((8,)),
            pltpu.SemaphoreType.DMA((halves,)),
            pltpu.SemaphoreType.DMA((halves,)),
            pltpu.SemaphoreType.DMA((5,)),
            pltpu.SemaphoreType.DMA((5,)),
            pltpu.SemaphoreType.REGULAR((4,)),
        ],
        compiler_params=pltpu.CompilerParams(
            collective_id=0, has_side_effects=True, vmem_limit_bytes=VMEM_LIMIT
        ),
        name="main",
    )(*(pltpu.with_memory_space_constraint(a, pltpu.HBM) for a in operands))


def unpack_kernel(fresh, misfit, chunks, tracer_out, misfit_out, w1_ref, b1_ref, w2_ref, b2_ref, wide):
    for i in range(CX):
        tracer_out[:, i, :] = fresh[i, 0:LEV, :]
        wide[:, i, :] = misfit[i, 0:LEV, :]
    misfit_out[...] = wide[...].astype(BF16)
    rest = 3 * LEV - 2 * PAD
    for t in range(HID // CY):
        lanes = slice(t * CY, (t + 1) * CY)
        for g in range(2):
            w1_ref[PAD * g : PAD * (g + 1), lanes] = chunks[g % 2, 2 * t + g // 2].astype(F32)
        third = chunks[0, 2 * t + 1].astype(F32)
        w1_ref[2 * PAD : 3 * LEV, lanes] = third[0:rest, :]
        b1_ref[:, lanes] = third[rest : rest + 1, :] + third[rest + 1 : rest + 2, :]
        fourth = chunks[1, 2 * t + 1].astype(F32)
        w2_ref[:, lanes] = fourth[0:LEV, :]
        if t == 0:
            b2_ref[...] = fourth[LEV : LEV + 1, 0:LEV] + fourth[LEV + 1 : LEV + 2, 0:LEV]


def unpack(fresh, misfit, chunks):
    vmem = pl.BlockSpec(memory_space=pltpu.VMEM)
    return pl.pallas_call(
        unpack_kernel,
        out_shape=(
            jax.ShapeDtypeStruct((LEV, CX, CY), F32),
            jax.ShapeDtypeStruct((LEV, CX, CY), BF16),
            jax.ShapeDtypeStruct((3 * LEV, HID), F32),
            jax.ShapeDtypeStruct((1, HID), F32),
            jax.ShapeDtypeStruct((LEV, HID), F32),
            jax.ShapeDtypeStruct((1, LEV), F32),
        ),
        in_specs=[vmem] * 3,
        out_specs=(vmem,) * 6,
        scratch_shapes=[pltpu.VMEM((LEV, CX, CY), F32)],
        compiler_params=pltpu.CompilerParams(vmem_limit_bytes=VMEM_LIMIT),
        name="unpack",
    )(fresh, misfit, chunks)


def on_device(tracer, east, north, target, depth, slots, w1, b1, w2, b2):
    fresh, misfit, chunks = main(
        tracer, east, north, target, depth, w1, b1.reshape(1, HID), w2.T, b2.reshape(1, LEV)
    )
    tracer_out, misfit_out, grad_w1, grad_b1, grad_w2, grad_b2 = unpack(fresh, misfit, chunks)
    return tracer_out, misfit_out, grad_w1, grad_b1.reshape(HID), grad_w2.T, grad_b2.reshape(LEV)


def solution(mesh):
    grid = P(None, "ocx", ("ocy", "ml"))
    return jax.shard_map(
        on_device,
        mesh=mesh,
        in_specs=(grid, grid, grid, grid, P("ocx", ("ocy", "ml")), P("ocx", ("ocy", "ml"), None, None), P(), P(), P(), P()),
        out_specs=(grid, grid, P(), P(), P(), P()),
        check_vma=False,
    )
```

```python
import jax
import jax.numpy as jnp
from jax import lax
from jax.experimental import pallas as pl
from jax.experimental.pallas import tpu as pltpu
from jax.sharding import PartitionSpec as P

MESH = pl.DeviceIdType.MESH
KAPPA = 0.1
STEPS = 3
LEV = 75
PAD = 80
CX = 4
CY = 128
CELLS = CX * CY
HID = 1024
ROWS = 240
TILES = 32
NZ = 16
CHIPS = 16
COLUMNS = 262144
REACH = 3
WIDE = CX + 2 * REACH
STRIP = 2 * REACH
NORTH_AT = (0, 1, 10, 11)
EAST_AT = (2, 6, 8, 9)
CELL_AT = (3, 4, 5, 7)
BLK = 256
STEPS_XY = (
    (2, 2), (2, 1), (2, 3), (1, 2), (3, 2), (1, 1), (1, 3), (3, 1), (3, 3), (2, 0), (0, 2), (1, 0), (3, 0), (0, 1), (0, 3)
)
STEPS_Z = (8, 7, 9, 6, 10, 5, 11, 4, 12, 3, 13, 2, 14, 1, 15)
F32 = jnp.float32
BF16 = jnp.bfloat16
VMEM_LIMIT = 40 * 1024 * 1024


def place(p):
    return lax.div(p, 8), lax.rem(p, 8)


def faces(opened, speed):
    near = jnp.where(opened, jnp.maximum(speed, 0.0) + KAPPA, 0.0)
    far = jnp.where(opened, jnp.minimum(speed, 0.0) - KAPPA, 0.0)
    return near, far


def dot(a, b, dims):
    return lax.dot_general(a, b, (dims, ((), ())), preferred_element_type=F32)


def main_kernel(
    tracer_hbm, east_hbm, north_hbm, target_hbm, depth_hbm, w1_hbm, b1_hbm, w2_hbm, b2_hbm,
    fresh_out, misfit_out, gathered,
    tracer_ref, east_ref, north_ref, target_ref, depth_ref, w1_ref, b1_ref, w2_ref, b2_ref,
    cells, north_own, east_own, rows_out, edges_out, halo_w, halo_e, halo_edges, pick_out, pick_rows, pick_edges,
    feat, weights, hidden, slope, total, wanted, chunks, core_in, sending, landed,
    mine, strips, strips_in, strips_all, chunk,
    load_sems, halo_send, halo_recv, core_send, core_recv, send_sems, recv_sems, known_tiles, known_ring,
):
    z, x, m = lax.axis_index("ocx"), lax.axis_index("ocy"), lax.axis_index("ml")
    core = lax.rem(m, 2)
    chip = x * 4 + lax.div(m, 2)
    p = x * 8 + m
    sibling = (z, x, m + 1 - 2 * core)

    def other_chip(dx, dy):
        to_x, to_m = lax.rem(x + dx, 4), lax.rem(m + 2 * dy, 8)
        return to_x * 4 + lax.div(to_m, 2), (z, to_x, to_m)

    def ring(k):
        w = lax.rem(z + k, NZ)
        return w, (w, x, m)

    def tile(k):
        return (z, *place(lax.rem(p + k, TILES)))

    to_e, to_w = ring(1)[1], ring(NZ - 1)[1]
    to_n, to_s = tile(1), tile(TILES - 1)

    pairs = (
        (depth_hbm, depth_ref), (tracer_hbm, tracer_ref), (north_hbm, north_ref), (east_hbm, east_ref),
        (target_hbm, target_ref), (w1_hbm, w1_ref), (b1_hbm, b1_ref), (w2_hbm, w2_ref), (b2_hbm, b2_ref),
    )
    loads = [pltpu.make_async_copy(src, dst, load_sems.at[i]) for i, (src, dst) in enumerate(pairs)]
    for load in loads:
        load.start()

    barrier = pltpu.get_barrier_semaphore()

    def signal(target):
        pl.semaphore_signal(barrier, inc=1, device_id=target, device_id_type=MESH)

    def diagonal(dz, k):
        return (lax.rem(z + dz, NZ), *tile(k)[1:])

    to_ne, to_nw = diagonal(1, 1), diagonal(NZ - 1, 1)
    to_se, to_sw = diagonal(1, TILES - 1), diagonal(NZ - 1, TILES - 1)
    for target in (to_e, to_w, to_n, to_s, to_ne, to_nw, to_se, to_sw):
        signal(target)

    def spread_word(known, number, ahead, behind):
        for target in (ahead, behind):
            pl.semaphore_signal(known.at[number], inc=1, device_id=target, device_id_type=MESH)

    def spread_tiles(number):
        spread_word(known_tiles, number, tile(1 << number), tile(TILES - (1 << number)))

    def spread_ring(number):
        spread_word(known_ring, number, ring(1 << number)[1], ring(NZ - (1 << number))[1])

    def remote(src, dst, send_sem, recv_sem, target):
        return pltpu.make_async_remote_copy(
            src_ref=src, dst_ref=dst, send_sem=send_sem, recv_sem=recv_sem,
            device_id=target, device_id_type=MESH,
        )

    def whole(ref, number):
        return remote(ref, ref, send_sems.at[number], recv_sems.at[number], sibling)

    def halo(src, dst, number, target):
        copy = remote(src, dst, halo_send.at[number], halo_recv.at[number], target)
        copy.start()
        return copy

    lane_in = lax.broadcasted_iota(jnp.int32, (CY, 2 * CY), 0)
    lane_out = lax.broadcasted_iota(jnp.int32, (CY, 2 * CY), 1)
    shift = jnp.where(lane_in >= CY - REACH, lane_out - lane_in + (CY - REACH), -999)
    shift = jnp.where(lane_in < REACH, lane_out - lane_in - CY, shift)
    for f, order in enumerate((CELL_AT, EAST_AT, NORTH_AT)):
        for i in range(CX):
            at = slice(CY * order[i], CY * (order[i] + 1))
            pick_out[at, :] = jnp.where(shift == 16 * f + 4 * i, 1.0, 0.0).astype(BF16)
    lane_in = lax.broadcasted_iota(jnp.int32, (CY, CY), 0)
    lane_out = lax.broadcasted_iota(jnp.int32, (CY, CY), 1)
    shift = jnp.where(lane_in >= CY - REACH, lane_out - lane_in + (CY - REACH) - CY // 2, -999)
    shift = jnp.where(lane_in < REACH, lane_out - lane_in - REACH, shift)
    for n in range(WIDE):
        pick_rows[CY * n : CY * (n + 1), :] = jnp.where(shift == STRIP * n, 1.0, 0.0).astype(BF16)
    lane_in = lax.broadcasted_iota(jnp.int32, (CY, 3 * CY), 0)
    lane_out = lax.broadcasted_iota(jnp.int32, (CY, 3 * CY), 1)
    field, owner, nth = lane_in // 16, (lane_in // 4) % 4, lane_in % 4
    shift = lane_out - (CY * field + STRIP * owner + nth)
    shift = jnp.where(jnp.logical_and(field < 3, nth < REACH), shift, -999)
    for n in range(6):
        dz = (0, -1, 1)[n % 3]
        here = (n // 3) * (CY // 2 + REACH) + STRIP * (REACH + CX * dz)
        hit = shift == here
        if dz == -1:
            hit = jnp.logical_and(hit, owner >= 1)
        if dz == 1:
            hit = jnp.logical_and(hit, owner <= REACH - 1)
        pick_edges[CY * n : CY * (n + 1), :] = jnp.where(hit, 1.0, 0.0).astype(BF16)

    level = lax.broadcasted_iota(jnp.int32, (PAD, CY), 0).astype(F32)
    lane = lax.broadcasted_iota(jnp.int32, (PAD, CY), 1)
    tail = lax.broadcasted_iota(jnp.int32, (PAD - LEV, CY), 0)
    none = jnp.zeros((PAD - LEV, CY), F32)
    for load in loads[:4]:
        load.wait()
    depth = [depth_ref[i : i + 1, :].astype(F32) for i in range(CX)]
    for i in range(CX):
        cells[i, 0:LEV, :] = tracer_ref[:, i, :]
        cells[i, LEV:PAD, :] = jnp.where(tail == 0, depth[i], 0.0)
        north_own[i, 0:LEV, :] = north_ref[:, i, :]
        north_own[i, LEV:PAD, :] = none
        east_own[i, 0:LEV, :] = east_ref[:, i, :]
        east_own[i, LEV:PAD, :] = none
        rows_out[CELL_AT[i]] = cells[i].astype(BF16)
        rows_out[EAST_AT[i]] = east_own[i].astype(BF16)
        rows_out[NORTH_AT[i]] = north_own[i].astype(BF16)
    pl.semaphore_wait(barrier, 8)
    copies = [halo(rows_out.at[4:12], halo_w, 0, to_e), halo(rows_out.at[0:7], halo_e, 1, to_w)]
    spread_tiles(0)
    spread_ring(0)
    edges = dot(jnp.concatenate([rows_out[n] for n in range(3 * CX)], axis=1), pick_out[...], ((1,), (0,)))
    edges_out[0] = edges[:, 0:CY].astype(BF16)
    edges_out[1] = edges[:, CY : 2 * CY].astype(BF16)
    copies += [
        halo(edges_out.at[0], halo_edges.at[0], 2, to_n),
        halo(edges_out.at[0], halo_edges.at[1], 3, to_ne),
        halo(edges_out.at[0], halo_edges.at[2], 4, to_nw),
        halo(edges_out.at[1], halo_edges.at[3], 5, to_s),
        halo(edges_out.at[1], halo_edges.at[4], 6, to_se),
        halo(edges_out.at[1], halo_edges.at[5], 7, to_sw),
    ]

    masks = [level[0:LEV, :] < depth[i] for i in range(CX)]
    for i in range(CX):
        at = slice(CY * i, CY * (i + 1))
        feat[LEV : 2 * LEV, at] = jnp.where(masks[i], east_own[i, 0:LEV, :], 0.0)
        feat[2 * LEV : 3 * LEV, at] = jnp.where(masks[i], north_own[i, 0:LEV, :], 0.0)
    last = lax.broadcasted_iota(jnp.int32, (ROWS - 3 * LEV, CELLS), 0)
    feat[3 * LEV : ROWS, :] = jnp.where(last < 2, 1.0, 0.0)
    pl.semaphore_wait(known_tiles.at[0], 2)
    spread_tiles(1)
    pl.semaphore_wait(known_ring.at[0], 2)
    spread_ring(1)
    for load in loads[4:]:
        load.wait()
    wanted[...] = target_ref[...].astype(F32)
    edge = 3 * LEV // 16 * 16
    weights[0:edge, :] = w1_ref[0:edge, :]
    bias = b1_ref[...]
    coarse = bias.astype(BF16).astype(F32)
    row = lax.broadcasted_iota(jnp.int32, (ROWS - edge, HID), 0) + edge
    final = jnp.where(row == 3 * LEV - 1, w1_ref[3 * LEV - 1 : 3 * LEV, :].astype(F32), 0.0)
    final = jnp.where(row == 3 * LEV, coarse, final)
    final = jnp.where(row == 3 * LEV + 1, bias - coarse, final)
    weights[edge:ROWS, :] = final.astype(BF16)

    pl.semaphore_wait(known_tiles.at[1], 2)
    spread_tiles(2)
    for copy in copies:
        copy.wait_recv()
    pl.semaphore_wait(known_tiles.at[2], 2)
    spread_tiles(3)
    pl.semaphore_wait(known_ring.at[1], 2)
    spread_ring(2)

    cell_rows = [halo_w[0], halo_w[1], halo_w[3]] + [rows_out[n] for n in CELL_AT] + [halo_e[3], halo_e[4], halo_e[5]]
    east_rows = [halo_w[2], halo_w[4], halo_w[5]] + [rows_out[n] for n in EAST_AT] + [halo_e[2], halo_e[6]]
    north_rows = [halo_w[6], halo_w[7]] + [rows_out[n] for n in NORTH_AT] + [halo_e[0], halo_e[1]]
    beyond = dot(jnp.concatenate([halo_edges[n] for n in range(6)], axis=1), pick_edges[...], ((1,), (0,)))

    def strip_of(some, first, f):
        own = dot(
            jnp.concatenate(some, axis=1), pick_rows[CY * first : CY * (first + len(some)), :], ((1,), (0,))
        )
        return own + beyond[:, CY * f : CY * (f + 1)]

    def turn(value, by):
        by = by % CY
        return pltpu.roll(value, by, 1) if by else value

    strip = strip_of(cell_rows, 0, 0)
    deep_here = jnp.broadcast_to(strip[LEV : LEV + 1, :], (PAD, CY))
    near_e, far_e = faces(level < jnp.minimum(deep_here, turn(deep_here, -STRIP)), strip_of(east_rows, 0, 1))
    nth = lane % (CY // 2)
    nth = nth - STRIP * ((nth * 43) // 256)
    border = jnp.logical_or(
        jnp.logical_and(lane < CY // 2, p == 0), jnp.logical_and(lane >= CY // 2, p == TILES - 1)
    )
    shut = jnp.logical_and(nth == REACH - 1, border)
    opened = jnp.logical_and(level < jnp.minimum(deep_here, turn(deep_here, -1)), jnp.logical_not(shut))
    strip_near, strip_far = faces(opened, strip_of(north_rows, 1, 2))
    near_w, far_w = turn(near_e, STRIP), turn(far_e, STRIP)
    near_s, far_s = turn(strip_near, 1), turn(strip_far, 1)
    strip_coef = (1.0 + far_w - near_e + far_s - strip_near, near_w, far_e, near_s, strip_far)
    strips_at = [strip]
    for step in range(STEPS - 1):
        keep, near_w, far_e, near_s, far_n = strip_coef
        strip = (
            keep * strip + near_w * turn(strip, STRIP) - far_e * turn(strip, -STRIP)
            + near_s * turn(strip, 1) - far_n * turn(strip, -1)
        )
        strips_at.append(strip)

    now = [
        cells[n - REACH] if REACH <= n < REACH + CX else cell_rows[n].astype(F32) for n in range(WIDE)
    ]
    deep = [jnp.broadcast_to(value[LEV : LEV + 1, :], (PAD, CY)) for value in now]
    east_faces = []
    for n in range(WIDE - 1):
        speed = east_own[n - REACH] if REACH <= n < REACH + CX else east_rows[n].astype(F32)
        east_faces.append(faces(level < jnp.minimum(deep[n], deep[n + 1]), speed))
    shut_n = jnp.logical_and(lane == CY - 1, p == TILES - 1)
    coef = [None] * WIDE
    for n in range(1, WIDE - 1):
        speed = north_own[n - REACH] if REACH <= n < REACH + CX else north_rows[n - 1].astype(F32)
        there = jnp.where(
            lane == CY - 1, turn(deep_here, CY - 1 - (CY // 2 + STRIP * n + REACH)), turn(deep[n], -1)
        )
        opened = jnp.logical_and(level < jnp.minimum(deep[n], there), jnp.logical_not(shut_n))
        near_n, far_n = faces(opened, speed)
        below = -(STRIP * n + REACH - 1)
        near_s = jnp.where(lane == 0, turn(strip_near, below), turn(near_n, 1))
        far_s = jnp.where(lane == 0, turn(strip_far, below), turn(far_n, 1))
        near_w, far_w = east_faces[n - 1]
        near_e, far_e = east_faces[n]
        coef[n] = (1.0 + far_w - near_e + far_s - near_n, near_w, far_e, near_s, far_n)
    for step in range(STEPS):
        after = list(now)
        for n in range(step + 1, WIDE - 1 - step):
            keep, near_w, far_e, near_s, far_n = coef[n]
            strip = strips_at[step]
            south = jnp.where(lane == 0, turn(strip, -(STRIP * n + REACH - 1)), turn(now[n], 1))
            north = jnp.where(
                lane == CY - 1, turn(strip, CY - 1 - (CY // 2 + STRIP * n + REACH)), turn(now[n], -1)
            )
            after[n] = (
                keep * now[n] + near_w * now[n - 1] - far_e * now[n + 1] + near_s * south - far_n * north
            )
        now = after
    for i in range(CX):
        cells[i] = now[REACH + i]
    for i in range(CX):
        at = slice(CY * i, CY * (i + 1))
        feat[0:LEV, at] = jnp.where(masks[i], cells[i, 0:LEV, :], 0.0)
    inputs = feat[...].astype(BF16)

    acc = None
    for b in range(HID // BLK):
        at = slice(b * BLK, (b + 1) * BLK)
        before = dot(weights[:, at], inputs, ((0,), (0,)))
        stash = before.astype(BF16).astype(F32)
        gate = 0.5 * jnp.tanh(0.5 * stash) + 0.5
        act = (stash * gate).astype(BF16)
        hidden[at, :] = act
        slope[at, :] = gate * (1.0 + stash * (1.0 - gate))
        part = dot(w2_ref[:, at], act, ((1,), (0,)))
        acc = part if acc is None else acc + part
    eye = lax.broadcasted_iota(jnp.int32, (LEV, LEV), 0) == lax.broadcasted_iota(jnp.int32, (LEV, LEV), 1)
    bias2 = jnp.sum(jnp.where(eye, b2_ref[...], 0.0), axis=1, keepdims=True)
    output = acc + bias2
    total[...] = jnp.zeros((PAD, CELLS), F32)
    for i in range(CX):
        at = slice(CY * i, CY * (i + 1))
        tendency = jnp.where(masks[i], output[:, at], 0.0).astype(BF16).astype(F32)
        goal = jnp.where(masks[i], wanted[:, i, :], 0.0)
        misfit = tendency - goal
        total[0:LEV, at] = misfit * (1.0 / COLUMNS)
        fresh_out[i, 0:LEV, :] = cells[i, 0:LEV, :] + tendency
        misfit_out[i, 0:LEV, :] = misfit
    d_out = total[...].astype(BF16)
    ones = jnp.ones((16, CELLS), BF16)
    bias_grad = dot(ones, d_out, ((1,), (1,)))
    spread = lax.broadcasted_iota(jnp.int32, (PAD, CY), 0) == LEV
    per = BLK // CY
    to_sibling = []
    for b in range(HID // BLK):
        at = slice(b * BLK, (b + 1) * BLK)
        d_hidden = dot(w2_ref[:, at], d_out[0:LEV, :], ((0,), (0,)))
        d_before = (d_hidden * slope[at, :]).astype(BF16)
        g1 = dot(inputs, d_before, ((1,), (1,)))
        g2 = dot(d_out, hidden[at, :], ((1,), (1,)))
        for t in range(per):
            lanes = slice(t * CY, (t + 1) * CY)
            tile = b * per + t
            for g in range(3):
                chunks[g % 2, 2 * tile + g // 2] = g1[PAD * g : PAD * (g + 1), lanes]
            last_part = g2[:, lanes]
            if tile == 0:
                row = jnp.concatenate([bias_grad[0:1, :], jnp.zeros((1, CY - PAD), F32)], axis=1)
                last_part = jnp.where(spread, row, last_part)
            chunks[1, 2 * tile + 1] = last_part
        some = pl.ds(2 * per * b, 2 * per)
        copy = remote(chunks.at[1 - core, some], core_in.at[some], core_send.at[b], core_recv.at[b], sibling)
        copy.start()
        to_sibling.append(copy)
    row = lax.broadcasted_iota(jnp.int32, (PAD, CY), 0)
    bias_row = 3 * LEV - 2 * PAD + core * (LEV - (3 * LEV - 2 * PAD))
    for b in range(HID // BLK):
        to_sibling[b].wait_recv()
        some = pl.ds(2 * per * b, 2 * per)
        both = chunks[core, some] + core_in[some]
        for j in range(2 * per):
            value = both[j]
            sent = value
            if j % 2:
                low = value - value.astype(BF16).astype(F32)
                sent = jnp.where(row == bias_row + 1, pltpu.roll(low, 1, 0), value)
            sending[2 * per * b + j] = sent.astype(BF16)

    pl.semaphore_wait(known_tiles.at[3], 2)

    for n, (dx, dy) in enumerate(STEPS_XY):
        c, target = other_chip(dx, dy)
        remote(sending.at[c], landed.at[n], send_sems.at[0], recv_sems.at[0], target).start()
    has_bias = lax.rem(chip, 2) == 1
    amount = chunks[core, chip] + core_in[chip]
    amount = jnp.where(jnp.logical_and(row == bias_row + 1, has_bias), 0.0, amount)
    whole(landed, 0).wait_recv()
    for k in range(CHIPS - 1):
        amount = amount + landed[k].astype(F32)
    mine[...] = amount
    part = PAD // NZ
    for k in range(NZ):
        strips[k] = mine[part * k : part * (k + 1), :]

    pl.semaphore_wait(known_ring.at[2], 2)
    for n, k in enumerate(STEPS_Z):
        w, target = ring(k)
        remote(strips.at[w], strips_in.at[n], send_sems.at[1], recv_sems.at[1], target).start()
    whole(strips_in, 1).wait_recv()
    strip = strips[z]
    for n in range(NZ - 1):
        strip = strip + strips_in[n]
    strips_all[z] = strip
    for k in STEPS_Z:
        _, target = ring(k)
        remote(strips_all.at[z], strips_all.at[z], send_sems.at[2], recv_sems.at[2], target).start()
    whole(strips_in, 2).wait_recv()
    for k in range(NZ):
        mine[part * k : part * (k + 1), :] = strips_all[k]
    value = mine[...]
    both = jnp.where(jnp.logical_and(row == bias_row, has_bias), pltpu.roll(value, PAD - 1, 0), 0.0) + value
    low = both - both.astype(BF16).astype(F32)
    both = jnp.where(jnp.logical_and(row == bias_row + 1, has_bias), pltpu.roll(low, 1, 0), both)
    chunk[...] = both.astype(BF16)
    gathered[core, chip] = chunk[...]

    for dx, dy in STEPS_XY:
        _, target = other_chip(dx, dy)
        remote(chunk, gathered.at[core, chip], send_sems.at[3], recv_sems.at[3], target).start()
    whole(landed, 3).wait_recv()
    forward = remote(gathered.at[core], gathered.at[core], send_sems.at[4], recv_sems.at[4], sibling)
    forward.start()
    for copy in copies + to_sibling:
        copy.wait_send()
    whole(landed, 0).wait_send()
    whole(strips_in, 1).wait_send()
    whole(strips_in, 2).wait_send()
    whole(landed, 3).wait_send()
    forward.wait()


def main(*operands):
    vmem = pl.BlockSpec(memory_space=pltpu.VMEM)
    hbm = pl.BlockSpec(memory_space=pltpu.HBM)
    part = PAD // NZ
    halves = HID // BLK
    return pl.pallas_call(
        main_kernel,
        out_shape=(
            jax.ShapeDtypeStruct((CX, PAD, CY), F32),
            jax.ShapeDtypeStruct((CX, PAD, CY), F32),
            jax.ShapeDtypeStruct((2, CHIPS, PAD, CY), BF16),
        ),
        in_specs=[hbm] * 9,
        out_specs=(vmem,) * 3,
        scratch_shapes=[pltpu.VMEM(a.shape, a.dtype) for a in operands]
        + [
            pltpu.VMEM((CX, PAD, CY), F32),
            pltpu.VMEM((CX, PAD, CY), F32),
            pltpu.VMEM((CX, PAD, CY), F32),
            pltpu.VMEM((3 * CX, PAD, CY), BF16),
            pltpu.VMEM((2, PAD, CY), BF16),
            pltpu.VMEM((8, PAD, CY), BF16),
            pltpu.VMEM((7, PAD, CY), BF16),
            pltpu.VMEM((6, PAD, CY), BF16),
            pltpu.VMEM((3 * CX * CY, 2 * CY), BF16),
            pltpu.VMEM((WIDE * CY, CY), BF16),
            pltpu.VMEM((6 * CY, 3 * CY), BF16),
            pltpu.VMEM((ROWS, CELLS), F32),
            pltpu.VMEM((ROWS, HID), BF16),
            pltpu.VMEM((HID, CELLS), BF16),
            pltpu.VMEM((HID, CELLS), F32),
            pltpu.VMEM((PAD, CELLS), F32),
            pltpu.VMEM((LEV, CX, CY), F32),
            pltpu.VMEM((2, CHIPS, PAD, CY), F32),
            pltpu.VMEM((CHIPS, PAD, CY), F32),
            pltpu.VMEM((CHIPS, PAD, CY), BF16),
            pltpu.VMEM((CHIPS - 1, PAD, CY), BF16),
            pltpu.VMEM((PAD, CY), F32),
            pltpu.VMEM((NZ, part, CY), F32),
            pltpu.VMEM((NZ - 1, part, CY), F32),
            pltpu.VMEM((NZ, part, CY), F32),
            pltpu.VMEM((PAD, CY), BF16),
            pltpu.SemaphoreType.DMA((len(operands),)),
            pltpu.SemaphoreType.DMA((8,)),
            pltpu.SemaphoreType.DMA((8,)),
            pltpu.SemaphoreType.DMA((halves,)),
            pltpu.SemaphoreType.DMA((halves,)),
            pltpu.SemaphoreType.DMA((5,)),
            pltpu.SemaphoreType.DMA((5,)),
            pltpu.SemaphoreType.REGULAR((4,)),
            pltpu.SemaphoreType.REGULAR((3,)),
        ],
        compiler_params=pltpu.CompilerParams(
            collective_id=0, has_side_effects=True, vmem_limit_bytes=VMEM_LIMIT
        ),
        name="main",
    )(*(pltpu.with_memory_space_constraint(a, pltpu.HBM) for a in operands))


def unpack_kernel(fresh, misfit, chunks, tracer_out, misfit_out, w1_ref, b1_ref, w2_ref, b2_ref, wide):
    for i in range(CX):
        tracer_out[:, i, :] = fresh[i, 0:LEV, :]
        wide[:, i, :] = misfit[i, 0:LEV, :]
    misfit_out[...] = wide[...].astype(BF16)
    rest = 3 * LEV - 2 * PAD
    for t in range(HID // CY):
        lanes = slice(t * CY, (t + 1) * CY)
        for g in range(2):
            w1_ref[PAD * g : PAD * (g + 1), lanes] = chunks[g % 2, 2 * t + g // 2].astype(F32)
        third = chunks[0, 2 * t + 1].astype(F32)
        w1_ref[2 * PAD : 3 * LEV, lanes] = third[0:rest, :]
        b1_ref[:, lanes] = third[rest : rest + 1, :] + third[rest + 1 : rest + 2, :]
        fourth = chunks[1, 2 * t + 1].astype(F32)
        w2_ref[:, lanes] = fourth[0:LEV, :]
        if t == 0:
            b2_ref[...] = fourth[LEV : LEV + 1, 0:LEV] + fourth[LEV + 1 : LEV + 2, 0:LEV]


def unpack(fresh, misfit, chunks):
    vmem = pl.BlockSpec(memory_space=pltpu.VMEM)
    return pl.pallas_call(
        unpack_kernel,
        out_shape=(
            jax.ShapeDtypeStruct((LEV, CX, CY), F32),
            jax.ShapeDtypeStruct((LEV, CX, CY), BF16),
            jax.ShapeDtypeStruct((3 * LEV, HID), F32),
            jax.ShapeDtypeStruct((1, HID), F32),
            jax.ShapeDtypeStruct((LEV, HID), F32),
            jax.ShapeDtypeStruct((1, LEV), F32),
        ),
        in_specs=[vmem] * 3,
        out_specs=(vmem,) * 6,
        scratch_shapes=[pltpu.VMEM((LEV, CX, CY), F32)],
        compiler_params=pltpu.CompilerParams(vmem_limit_bytes=VMEM_LIMIT),
        name="unpack",
    )(fresh, misfit, chunks)


def on_device(tracer, east, north, target, depth, slots, w1, b1, w2, b2):
    fresh, misfit, chunks = main(
        tracer, east, north, target, depth, w1, b1.reshape(1, HID), w2.T, b2.reshape(1, LEV)
    )
    tracer_out, misfit_out, grad_w1, grad_b1, grad_w2, grad_b2 = unpack(fresh, misfit, chunks)
    return tracer_out, misfit_out, grad_w1, grad_b1.reshape(HID), grad_w2.T, grad_b2.reshape(LEV)


def solution(mesh):
    grid = P(None, "ocx", ("ocy", "ml"))
    return jax.shard_map(
        on_device,
        mesh=mesh,
        in_specs=(grid, grid, grid, grid, P("ocx", ("ocy", "ml")), P("ocx", ("ocy", "ml"), None, None), P(), P(), P(), P()),
        out_specs=(grid, grid, P(), P(), P(), P()),
        check_vma=False,
    )
```

```python
import functools

import jax
import jax.numpy as jnp
from jax import lax
from jax.experimental import pallas as pl
from jax.experimental.pallas import tpu as pltpu
from jax.sharding import PartitionSpec as P

MESH = pl.DeviceIdType.MESH
KAPPA = 0.1
STEPS = 3
LEV = 75
PAD = 80
CX = 4
CY = 128
CELLS = CX * CY
HID = 1024
ROWS = 240
TILES = 32
NZ = 16
CHIPS = 16
COLUMNS = 262144
REACH = 3
WIDE = CX + 2 * REACH
STRIP = 2 * REACH
NORTH_AT = (0, 1, 10, 11)
EAST_AT = (2, 6, 8, 9)
CELL_AT = (3, 4, 5, 7)
BLK = 256
STEPS_XY = (
    (2, 2), (2, 1), (2, 3), (1, 2), (3, 2), (1, 1), (1, 3), (3, 1), (3, 3), (2, 0), (0, 2), (1, 0), (3, 0), (0, 1), (0, 3)
)
STEPS_Z = (8, 7, 9, 6, 10, 5, 11, 4, 12, 3, 13, 2, 14, 1, 15)
F32 = jnp.float32
BF16 = jnp.bfloat16
VMEM_LIMIT = 40 * 1024 * 1024


def place(p):
    return lax.div(p, 8), lax.rem(p, 8)


def faces(opened, speed):
    near = jnp.where(opened, jnp.maximum(speed, 0.0) + KAPPA, 0.0)
    far = jnp.where(opened, jnp.minimum(speed, 0.0) - KAPPA, 0.0)
    return near, far


def dot(a, b, dims):
    return lax.dot_general(a, b, (dims, ((), ())), preferred_element_type=F32)


def main_kernel(
    tracer_hbm, east_hbm, north_hbm, target_hbm, depth_hbm, w1_hbm, b1_hbm, w2_hbm, b2_hbm,
    tracer_out, misfit_out, w1_out, b1_out, w2_out, b2_out,
    tracer_ref, east_ref, north_ref, target_ref, depth_ref, w1_ref, b1_ref, w2_ref, b2_ref,
    cells, north_own, east_own, rows_out, edges_out, halo_w, halo_e, halo_edges, pick_out, pick_rows, pick_edges,
    fresh, misfits, gathered, feat, weights, hidden, slope, total, wanted, chunks, core_in, sending, landed,
    mine, strips, strips_in, strips_all, chunk,
    load_sems, halo_send, halo_recv, core_send, core_recv, send_sems, recv_sems, known_tiles, known_ring,
):
    z, x, m = lax.axis_index("ocx"), lax.axis_index("ocy"), lax.axis_index("ml")
    core = lax.rem(m, 2)
    chip = x * 4 + lax.div(m, 2)
    p = x * 8 + m
    sibling = (z, x, m + 1 - 2 * core)

    def other_chip(dx, dy):
        to_x, to_m = lax.rem(x + dx, 4), lax.rem(m + 2 * dy, 8)
        return to_x * 4 + lax.div(to_m, 2), (z, to_x, to_m)

    def ring(k):
        w = lax.rem(z + k, NZ)
        return w, (w, x, m)

    def tile(k):
        return (z, *place(lax.rem(p + k, TILES)))

    to_e, to_w = ring(1)[1], ring(NZ - 1)[1]
    to_n, to_s = tile(1), tile(TILES - 1)

    pairs = (
        (depth_hbm, depth_ref), (tracer_hbm, tracer_ref), (north_hbm, north_ref), (east_hbm, east_ref),
        (target_hbm, target_ref), (w1_hbm, w1_ref), (b1_hbm, b1_ref), (w2_hbm, w2_ref), (b2_hbm, b2_ref),
    )
    loads = [pltpu.make_async_copy(src, dst, load_sems.at[i]) for i, (src, dst) in enumerate(pairs)]
    for load in loads[:4]:
        load.start()

    barrier = pltpu.get_barrier_semaphore()

    def signal(target):
        pl.semaphore_signal(barrier, inc=1, device_id=target, device_id_type=MESH)

    def diagonal(dz, k):
        return (lax.rem(z + dz, NZ), *tile(k)[1:])

    to_ne, to_nw = diagonal(1, 1), diagonal(NZ - 1, 1)
    to_se, to_sw = diagonal(1, TILES - 1), diagonal(NZ - 1, TILES - 1)
    for target in (to_e, to_w, to_n, to_s, to_ne, to_nw, to_se, to_sw):
        signal(target)
    for load in loads[4:]:
        load.start()

    def spread_word(known, number, ahead, behind):
        for target in (ahead, behind):
            pl.semaphore_signal(known.at[number], inc=1, device_id=target, device_id_type=MESH)

    def spread_tiles(number):
        spread_word(known_tiles, number, tile(1 << number), tile(TILES - (1 << number)))

    def spread_ring(number):
        spread_word(known_ring, number, ring(1 << number)[1], ring(NZ - (1 << number))[1])

    def remote(src, dst, send_sem, recv_sem, target):
        return pltpu.make_async_remote_copy(
            src_ref=src, dst_ref=dst, send_sem=send_sem, recv_sem=recv_sem,
            device_id=target, device_id_type=MESH,
        )

    def whole(ref, number):
        return remote(ref, ref, send_sems.at[number], recv_sems.at[number], sibling)

    def halo(src, dst, number, target):
        copy = remote(src, dst, halo_send.at[number], halo_recv.at[number], target)
        copy.start()
        return copy

    lane_in = lax.broadcasted_iota(jnp.int32, (CY, 2 * CY), 0)
    lane_out = lax.broadcasted_iota(jnp.int32, (CY, 2 * CY), 1)
    shift = jnp.where(lane_in >= CY - REACH, lane_out - lane_in + (CY - REACH), -999)
    shift = jnp.where(lane_in < REACH, lane_out - lane_in - CY, shift)
    for f, order in enumerate((CELL_AT, EAST_AT, NORTH_AT)):
        for i in range(CX):
            at = slice(CY * order[i], CY * (order[i] + 1))
            pick_out[at, :] = jnp.where(shift == 16 * f + 4 * i, 1.0, 0.0).astype(BF16)
    lane_in = lax.broadcasted_iota(jnp.int32, (CY, CY), 0)
    lane_out = lax.broadcasted_iota(jnp.int32, (CY, CY), 1)
    shift = jnp.where(lane_in >= CY - REACH, lane_out - lane_in + (CY - REACH) - CY // 2, -999)
    shift = jnp.where(lane_in < REACH, lane_out - lane_in - REACH, shift)
    for n in range(WIDE):
        pick_rows[CY * n : CY * (n + 1), :] = jnp.where(shift == STRIP * n, 1.0, 0.0).astype(BF16)
    lane_in = lax.broadcasted_iota(jnp.int32, (CY, 3 * CY), 0)
    lane_out = lax.broadcasted_iota(jnp.int32, (CY, 3 * CY), 1)
    field, owner, nth = lane_in // 16, (lane_in // 4) % 4, lane_in % 4
    shift = lane_out - (CY * field + STRIP * owner + nth)
    shift = jnp.where(jnp.logical_and(field < 3, nth < REACH), shift, -999)
    for n in range(6):
        dz = (0, -1, 1)[n % 3]
        here = (n // 3) * (CY // 2 + REACH) + STRIP * (REACH + CX * dz)
        hit = shift == here
        if dz == -1:
            hit = jnp.logical_and(hit, owner >= 1)
        if dz == 1:
            hit = jnp.logical_and(hit, owner <= REACH - 1)
        pick_edges[CY * n : CY * (n + 1), :] = jnp.where(hit, 1.0, 0.0).astype(BF16)

    level = lax.broadcasted_iota(jnp.int32, (PAD, CY), 0).astype(F32)
    lane = lax.broadcasted_iota(jnp.int32, (PAD, CY), 1)
    tail = lax.broadcasted_iota(jnp.int32, (PAD - LEV, CY), 0)
    none = jnp.zeros((PAD - LEV, CY), F32)
    for load in loads[:4]:
        load.wait()
    depth = [depth_ref[i : i + 1, :].astype(F32) for i in range(CX)]
    for i in range(CX):
        cells[i, 0:LEV, :] = tracer_ref[:, i, :]
        cells[i, LEV:PAD, :] = jnp.where(tail == 0, depth[i], 0.0)
        north_own[i, 0:LEV, :] = north_ref[:, i, :]
        north_own[i, LEV:PAD, :] = none
        east_own[i, 0:LEV, :] = east_ref[:, i, :]
        east_own[i, LEV:PAD, :] = none
        rows_out[CELL_AT[i]] = cells[i].astype(BF16)
        rows_out[EAST_AT[i]] = east_own[i].astype(BF16)
        rows_out[NORTH_AT[i]] = north_own[i].astype(BF16)
    pl.semaphore_wait(barrier, 8)
    copies = [halo(rows_out.at[4:12], halo_w, 0, to_e), halo(rows_out.at[0:7], halo_e, 1, to_w)]
    spread_tiles(0)
    spread_ring(0)
    edges = dot(jnp.concatenate([rows_out[n] for n in range(3 * CX)], axis=1), pick_out[...], ((1,), (0,)))
    edges_out[0] = edges[:, 0:CY].astype(BF16)
    edges_out[1] = edges[:, CY : 2 * CY].astype(BF16)
    copies += [
        halo(edges_out.at[0], halo_edges.at[0], 2, to_n),
        halo(edges_out.at[0], halo_edges.at[1], 3, to_ne),
        halo(edges_out.at[0], halo_edges.at[2], 4, to_nw),
        halo(edges_out.at[1], halo_edges.at[3], 5, to_s),
        halo(edges_out.at[1], halo_edges.at[4], 6, to_se),
        halo(edges_out.at[1], halo_edges.at[5], 7, to_sw),
    ]

    masks = [level[0:LEV, :] < depth[i] for i in range(CX)]
    for i in range(CX):
        at = slice(CY * i, CY * (i + 1))
        feat[LEV : 2 * LEV, at] = jnp.where(masks[i], east_own[i, 0:LEV, :], 0.0)
        feat[2 * LEV : 3 * LEV, at] = jnp.where(masks[i], north_own[i, 0:LEV, :], 0.0)
    last = lax.broadcasted_iota(jnp.int32, (ROWS - 3 * LEV, CELLS), 0)
    feat[3 * LEV : ROWS, :] = jnp.where(last < 2, 1.0, 0.0)
    pl.semaphore_wait(known_tiles.at[0], 2)
    spread_tiles(1)
    pl.semaphore_wait(known_ring.at[0], 2)
    spread_ring(1)
    for load in loads[4:]:
        load.wait()
    wanted[...] = target_ref[...].astype(F32)
    edge = 3 * LEV // 16 * 16
    weights[0:edge, :] = w1_ref[0:edge, :]
    bias = b1_ref[...]
    coarse = bias.astype(BF16).astype(F32)
    row = lax.broadcasted_iota(jnp.int32, (ROWS - edge, HID), 0) + edge
    final = jnp.where(row == 3 * LEV - 1, w1_ref[3 * LEV - 1 : 3 * LEV, :].astype(F32), 0.0)
    final = jnp.where(row == 3 * LEV, coarse, final)
    final = jnp.where(row == 3 * LEV + 1, bias - coarse, final)
    weights[edge:ROWS, :] = final.astype(BF16)

    pl.semaphore_wait(known_tiles.at[1], 2)
    spread_tiles(2)
    for copy in copies:
        copy.wait_recv()

    cell_rows = [halo_w[0], halo_w[1], halo_w[3]] + [rows_out[n] for n in CELL_AT] + [halo_e[3], halo_e[4], halo_e[5]]
    east_rows = [halo_w[2], halo_w[4], halo_w[5]] + [rows_out[n] for n in EAST_AT] + [halo_e[2], halo_e[6]]
    north_rows = [halo_w[6], halo_w[7]] + [rows_out[n] for n in NORTH_AT] + [halo_e[0], halo_e[1]]
    beyond = dot(jnp.concatenate([halo_edges[n] for n in range(6)], axis=1), pick_edges[...], ((1,), (0,)))

    def strip_of(some, first, f):
        own = dot(
            jnp.concatenate(some, axis=1), pick_rows[CY * first : CY * (first + len(some)), :], ((1,), (0,))
        )
        return own + beyond[:, CY * f : CY * (f + 1)]

    def turn(value, by):
        by = by % CY
        return pltpu.roll(value, by, 1) if by else value

    strip = strip_of(cell_rows, 0, 0)
    deep_here = jnp.broadcast_to(strip[LEV : LEV + 1, :], (PAD, CY))
    near_e, far_e = faces(level < jnp.minimum(deep_here, turn(deep_here, -STRIP)), strip_of(east_rows, 0, 1))
    nth = lane % (CY // 2)
    nth = nth - STRIP * ((nth * 43) // 256)
    border = jnp.logical_or(
        jnp.logical_and(lane < CY // 2, p == 0), jnp.logical_and(lane >= CY // 2, p == TILES - 1)
    )
    shut = jnp.logical_and(nth == REACH - 1, border)
    opened = jnp.logical_and(level < jnp.minimum(deep_here, turn(deep_here, -1)), jnp.logical_not(shut))
    strip_near, strip_far = faces(opened, strip_of(north_rows, 1, 2))
    near_w, far_w = turn(near_e, STRIP), turn(far_e, STRIP)
    near_s, far_s = turn(strip_near, 1), turn(strip_far, 1)
    strip_coef = (1.0 + far_w - near_e + far_s - strip_near, near_w, far_e, near_s, strip_far)
    strips_at = [strip]
    for step in range(STEPS - 1):
        keep, near_w, far_e, near_s, far_n = strip_coef
        strip = (
            keep * strip + near_w * turn(strip, STRIP) - far_e * turn(strip, -STRIP)
            + near_s * turn(strip, 1) - far_n * turn(strip, -1)
        )
        strips_at.append(strip)

    now = [
        cells[n - REACH] if REACH <= n < REACH + CX else cell_rows[n].astype(F32) for n in range(WIDE)
    ]
    deep = [jnp.broadcast_to(value[LEV : LEV + 1, :], (PAD, CY)) for value in now]
    east_faces = []
    for n in range(WIDE - 1):
        speed = east_own[n - REACH] if REACH <= n < REACH + CX else east_rows[n].astype(F32)
        east_faces.append(faces(level < jnp.minimum(deep[n], deep[n + 1]), speed))
    shut_n = jnp.logical_and(lane == CY - 1, p == TILES - 1)
    coef = [None] * WIDE
    for n in range(1, WIDE - 1):
        speed = north_own[n - REACH] if REACH <= n < REACH + CX else north_rows[n - 1].astype(F32)
        there = jnp.where(
            lane == CY - 1, turn(deep_here, CY - 1 - (CY // 2 + STRIP * n + REACH)), turn(deep[n], -1)
        )
        opened = jnp.logical_and(level < jnp.minimum(deep[n], there), jnp.logical_not(shut_n))
        near_n, far_n = faces(opened, speed)
        below = -(STRIP * n + REACH - 1)
        near_s = jnp.where(lane == 0, turn(strip_near, below), turn(near_n, 1))
        far_s = jnp.where(lane == 0, turn(strip_far, below), turn(far_n, 1))
        near_w, far_w = east_faces[n - 1]
        near_e, far_e = east_faces[n]
        coef[n] = (1.0 + far_w - near_e + far_s - near_n, near_w, far_e, near_s, far_n)
    for step in range(STEPS):
        after = list(now)
        for n in range(step + 1, WIDE - 1 - step):
            keep, near_w, far_e, near_s, far_n = coef[n]
            strip = strips_at[step]
            south = jnp.where(lane == 0, turn(strip, -(STRIP * n + REACH - 1)), turn(now[n], 1))
            north = jnp.where(
                lane == CY - 1, turn(strip, CY - 1 - (CY // 2 + STRIP * n + REACH)), turn(now[n], -1)
            )
            after[n] = (
                keep * now[n] + near_w * now[n - 1] - far_e * now[n + 1] + near_s * south - far_n * north
            )
        now = after
    for i in range(CX):
        cells[i] = now[REACH + i]
    pl.semaphore_wait(known_tiles.at[2], 2)
    spread_tiles(3)
    for i in range(CX):
        at = slice(CY * i, CY * (i + 1))
        feat[0:LEV, at] = jnp.where(masks[i], cells[i, 0:LEV, :], 0.0)
    inputs = feat[...].astype(BF16)

    acc = None
    for b in range(HID // BLK):
        at = slice(b * BLK, (b + 1) * BLK)
        before = dot(weights[:, at], inputs, ((0,), (0,)))
        stash = before.astype(BF16).astype(F32)
        gate = 0.5 * jnp.tanh(0.5 * stash) + 0.5
        act = (stash * gate).astype(BF16)
        hidden[at, :] = act
        slope[at, :] = gate * (1.0 + stash * (1.0 - gate))
        part = dot(w2_ref[:, at], act, ((1,), (0,)))
        acc = part if acc is None else acc + part
    pl.semaphore_wait(known_ring.at[1], 2)
    spread_ring(2)
    eye = lax.broadcasted_iota(jnp.int32, (LEV, LEV), 0) == lax.broadcasted_iota(jnp.int32, (LEV, LEV), 1)
    bias2 = jnp.sum(jnp.where(eye, b2_ref[...], 0.0), axis=1, keepdims=True)
    output = acc + bias2
    total[...] = jnp.zeros((PAD, CELLS), F32)
    for i in range(CX):
        at = slice(CY * i, CY * (i + 1))
        tendency = jnp.where(masks[i], output[:, at], 0.0).astype(BF16).astype(F32)
        goal = jnp.where(masks[i], wanted[:, i, :], 0.0)
        misfit = tendency - goal
        total[0:LEV, at] = misfit * (1.0 / COLUMNS)
        fresh[i, 0:LEV, :] = cells[i, 0:LEV, :] + tendency
        misfits[i, 0:LEV, :] = misfit
    d_out = total[...].astype(BF16)
    ones = jnp.ones((16, CELLS), BF16)
    bias_grad = dot(ones, d_out, ((1,), (1,)))
    spread = lax.broadcasted_iota(jnp.int32, (PAD, CY), 0) == LEV
    per = BLK // CY
    to_sibling = []
    for b in range(HID // BLK):
        at = slice(b * BLK, (b + 1) * BLK)
        d_hidden = dot(w2_ref[:, at], d_out[0:LEV, :], ((0,), (0,)))
        d_before = (d_hidden * slope[at, :]).astype(BF16)
        g1 = dot(inputs, d_before, ((1,), (1,)))
        g2 = dot(d_out, hidden[at, :], ((1,), (1,)))
        for t in range(per):
            lanes = slice(t * CY, (t + 1) * CY)
            tile = b * per + t
            for g in range(3):
                chunks[g % 2, 2 * tile + g // 2] = g1[PAD * g : PAD * (g + 1), lanes]
            last_part = g2[:, lanes]
            if tile == 0:
                row = jnp.concatenate([bias_grad[0:1, :], jnp.zeros((1, CY - PAD), F32)], axis=1)
                last_part = jnp.where(spread, row, last_part)
            chunks[1, 2 * tile + 1] = last_part
        some = pl.ds(2 * per * b, 2 * per)
        copy = remote(chunks.at[1 - core, some], core_in.at[some], core_send.at[b], core_recv.at[b], sibling)
        copy.start()
        to_sibling.append(copy)
    row = lax.broadcasted_iota(jnp.int32, (PAD, CY), 0)
    bias_row = 3 * LEV - 2 * PAD + core * (LEV - (3 * LEV - 2 * PAD))
    for b in range(HID // BLK):
        to_sibling[b].wait_recv()
        some = pl.ds(2 * per * b, 2 * per)
        both = chunks[core, some] + core_in[some]
        for j in range(2 * per):
            value = both[j]
            sent = value
            if j % 2:
                low = value - value.astype(BF16).astype(F32)
                sent = jnp.where(row == bias_row + 1, pltpu.roll(low, 1, 0), value)
            sending[2 * per * b + j] = sent.astype(BF16)

    pl.semaphore_wait(known_tiles.at[3], 2)

    for n, (dx, dy) in enumerate(STEPS_XY):
        c, target = other_chip(dx, dy)
        remote(sending.at[c], landed.at[n], send_sems.at[0], recv_sems.at[0], target).start()
    for i in range(CX):
        tracer_out[:, i, :] = fresh[i, 0:LEV, :]
        wanted[:, i, :] = misfits[i, 0:LEV, :]
    misfit_out[...] = wanted[...].astype(BF16)
    has_bias = lax.rem(chip, 2) == 1
    amount = chunks[core, chip] + core_in[chip]
    amount = jnp.where(jnp.logical_and(row == bias_row + 1, has_bias), 0.0, amount)
    whole(landed, 0).wait_recv()
    for k in range(CHIPS - 1):
        amount = amount + landed[k].astype(F32)
    mine[...] = amount
    part = PAD // NZ
    for k in range(NZ):
        strips[k] = mine[part * k : part * (k + 1), :]

    pl.semaphore_wait(known_ring.at[2], 2)
    for n, k in enumerate(STEPS_Z):
        w, target = ring(k)
        remote(strips.at[w], strips_in.at[n], send_sems.at[1], recv_sems.at[1], target).start()
    whole(strips_in, 1).wait_recv()
    strip = strips[z]
    for n in range(NZ - 1):
        strip = strip + strips_in[n]
    strips_all[z] = strip
    for k in STEPS_Z:
        _, target = ring(k)
        remote(strips_all.at[z], strips_all.at[z], send_sems.at[2], recv_sems.at[2], target).start()
    whole(strips_in, 2).wait_recv()
    for k in range(NZ):
        mine[part * k : part * (k + 1), :] = strips_all[k]
    value = mine[...]
    both = jnp.where(jnp.logical_and(row == bias_row, has_bias), pltpu.roll(value, PAD - 1, 0), 0.0) + value
    low = both - both.astype(BF16).astype(F32)
    both = jnp.where(jnp.logical_and(row == bias_row + 1, has_bias), pltpu.roll(low, 1, 0), both)
    chunk[...] = both.astype(BF16)
    gathered[core, chip] = chunk[...]

    for dx, dy in STEPS_XY:
        _, target = other_chip(dx, dy)
        remote(chunk, gathered.at[core, chip], send_sems.at[3], recv_sems.at[3], target).start()
    whole(landed, 3).wait_recv()
    forward = remote(gathered.at[core], gathered.at[core], send_sems.at[4], recv_sems.at[4], sibling)
    forward.start()

    def unpack(half):
        rest = 3 * LEV - 2 * PAD
        for t in range(HID // CY):
            lanes = slice(t * CY, (t + 1) * CY)
            w1_out[PAD * half : PAD * (half + 1), lanes] = gathered[half, 2 * t].astype(F32)
            value = gathered[half, 2 * t + 1].astype(F32)
            if half == 0:
                w1_out[2 * PAD : 3 * LEV, lanes] = value[0:rest, :]
                b1_out[:, lanes] = value[rest : rest + 1, :] + value[rest + 1 : rest + 2, :]
            else:
                w2_out[:, lanes] = value[0:LEV, :]
                if t == 0:
                    b2_out[...] = value[LEV : LEV + 1, 0:LEV] + value[LEV + 1 : LEV + 2, 0:LEV]

    for half in range(2):
        pl.when(core == half)(functools.partial(unpack, half))
    for copy in copies + to_sibling:
        copy.wait_send()
    whole(landed, 0).wait_send()
    whole(strips_in, 1).wait_send()
    whole(strips_in, 2).wait_send()
    whole(landed, 3).wait_send()
    forward.wait()
    for half in range(2):
        pl.when(core != half)(functools.partial(unpack, half))


def main(*operands):
    vmem = pl.BlockSpec(memory_space=pltpu.VMEM)
    hbm = pl.BlockSpec(memory_space=pltpu.HBM)
    part = PAD // NZ
    halves = HID // BLK
    return pl.pallas_call(
        main_kernel,
        out_shape=(
            jax.ShapeDtypeStruct((LEV, CX, CY), F32),
            jax.ShapeDtypeStruct((LEV, CX, CY), BF16),
            jax.ShapeDtypeStruct((3 * LEV, HID), F32),
            jax.ShapeDtypeStruct((1, HID), F32),
            jax.ShapeDtypeStruct((LEV, HID), F32),
            jax.ShapeDtypeStruct((1, LEV), F32),
        ),
        in_specs=[hbm] * 9,
        out_specs=(vmem,) * 6,
        scratch_shapes=[pltpu.VMEM(a.shape, a.dtype) for a in operands]
        + [
            pltpu.VMEM((CX, PAD, CY), F32),
            pltpu.VMEM((CX, PAD, CY), F32),
            pltpu.VMEM((CX, PAD, CY), F32),
            pltpu.VMEM((3 * CX, PAD, CY), BF16),
            pltpu.VMEM((2, PAD, CY), BF16),
            pltpu.VMEM((8, PAD, CY), BF16),
            pltpu.VMEM((7, PAD, CY), BF16),
            pltpu.VMEM((6, PAD, CY), BF16),
            pltpu.VMEM((3 * CX * CY, 2 * CY), BF16),
            pltpu.VMEM((WIDE * CY, CY), BF16),
            pltpu.VMEM((6 * CY, 3 * CY), BF16),
            pltpu.VMEM((CX, PAD, CY), F32),
            pltpu.VMEM((CX, PAD, CY), F32),
            pltpu.VMEM((2, CHIPS, PAD, CY), BF16),
            pltpu.VMEM((ROWS, CELLS), F32),
            pltpu.VMEM((ROWS, HID), BF16),
            pltpu.VMEM((HID, CELLS), BF16),
            pltpu.VMEM((HID, CELLS), F32),
            pltpu.VMEM((PAD, CELLS), F32),
            pltpu.VMEM((LEV, CX, CY), F32),
            pltpu.VMEM((2, CHIPS, PAD, CY), F32),
            pltpu.VMEM((CHIPS, PAD, CY), F32),
            pltpu.VMEM((CHIPS, PAD, CY), BF16),
            pltpu.VMEM((CHIPS - 1, PAD, CY), BF16),
            pltpu.VMEM((PAD, CY), F32),
            pltpu.VMEM((NZ, part, CY), F32),
            pltpu.VMEM((NZ - 1, part, CY), F32),
            pltpu.VMEM((NZ, part, CY), F32),
            pltpu.VMEM((PAD, CY), BF16),
            pltpu.SemaphoreType.DMA((len(operands),)),
            pltpu.SemaphoreType.DMA((8,)),
            pltpu.SemaphoreType.DMA((8,)),
            pltpu.SemaphoreType.DMA((halves,)),
            pltpu.SemaphoreType.DMA((halves,)),
            pltpu.SemaphoreType.DMA((5,)),
            pltpu.SemaphoreType.DMA((5,)),
            pltpu.SemaphoreType.REGULAR((4,)),
            pltpu.SemaphoreType.REGULAR((3,)),
        ],
        compiler_params=pltpu.CompilerParams(
            collective_id=0, has_side_effects=True, vmem_limit_bytes=VMEM_LIMIT
        ),
        name="main",
    )(*(pltpu.with_memory_space_constraint(a, pltpu.HBM) for a in operands))


def store_kernel(*refs):
    count = len(refs) // 2
    copies = [pltpu.make_async_copy(refs[i], refs[count + i], refs[-1].at[i]) for i in (2, 4, 0, 1, 3, 5)]
    for copy in copies:
        copy.start()
    for copy in copies:
        copy.wait()


def store(*results):
    vmem = pl.BlockSpec(memory_space=pltpu.VMEM)
    hbm = pl.BlockSpec(memory_space=pltpu.HBM)
    return pl.pallas_call(
        store_kernel,
        out_shape=tuple(jax.ShapeDtypeStruct(a.shape, a.dtype) for a in results),
        in_specs=[vmem] * len(results),
        out_specs=(hbm,) * len(results),
        scratch_shapes=[pltpu.SemaphoreType.DMA((len(results),))],
        compiler_params=pltpu.CompilerParams(vmem_limit_bytes=16 * 1024 * 1024),
        name="store",
    )(*results)


def on_device(tracer, east, north, target, depth, slots, w1, b1, w2, b2):
    results = main(tracer, east, north, target, depth, w1, b1.reshape(1, HID), w2.T, b2.reshape(1, LEV))
    tracer_out, misfit_out, grad_w1, grad_b1, grad_w2, grad_b2 = store(*results)
    return tracer_out, misfit_out, grad_w1, grad_b1.reshape(HID), grad_w2.T, grad_b2.reshape(LEV)


def solution(mesh):
    grid = P(None, "ocx", ("ocy", "ml"))
    return jax.shard_map(
        on_device,
        mesh=mesh,
        in_specs=(grid, grid, grid, grid, P("ocx", ("ocy", "ml")), P("ocx", ("ocy", "ml"), None, None), P(), P(), P(), P()),
        out_specs=(grid, grid, P(), P(), P(), P()),
        check_vma=False,
    )
```

```python
import functools

import jax
import jax.numpy as jnp
from jax import lax
from jax.experimental import pallas as pl
from jax.experimental.pallas import tpu as pltpu
from jax.sharding import PartitionSpec as P

MESH = pl.DeviceIdType.MESH
KAPPA = 0.1
STEPS = 3
LEV = 75
PAD = 80
CX = 4
CY = 128
CELLS = CX * CY
HID = 1024
ROWS = 240
TILES = 32
NZ = 16
CHIPS = 16
COLUMNS = 262144
REACH = 3
WIDE = CX + 2 * REACH
STRIP = 4 * REACH
LATS = 16 * 3
CORNER = 16
EDGE = LATS + 2 * CORNER
NORTH_AT = (0, 1, 10, 11)
EAST_AT = (2, 6, 8, 9)
CELL_AT = (3, 4, 5, 7)
BLK = 256
STEPS_XY = (
    (2, 2), (2, 1), (2, 3), (1, 2), (3, 2), (1, 1), (1, 3), (3, 1), (3, 3), (2, 0), (0, 2), (1, 0), (3, 0), (0, 1), (0, 3)
)
STEPS_Z = (8, 7, 9, 6, 10, 5, 11, 4, 12, 3, 13, 2, 14, 1, 15)
F32 = jnp.float32
BF16 = jnp.bfloat16
VMEM_LIMIT = 40 * 1024 * 1024


def place(p):
    return lax.div(p, 8), lax.rem(p, 8)


def faces(opened, speed):
    near = jnp.where(opened, jnp.maximum(speed, 0.0) + KAPPA, 0.0)
    far = jnp.where(opened, jnp.minimum(speed, 0.0) - KAPPA, 0.0)
    return near, far


def dot(a, b, dims):
    return lax.dot_general(a, b, (dims, ((), ())), preferred_element_type=F32)


def main_kernel(
    tracer_hbm, east_hbm, north_hbm, target_hbm, depth_hbm, w1_hbm, b1_hbm, w2_hbm, b2_hbm,
    tracer_out, misfit_out, w1_out, b1_out, w2_out, b2_out,
    tracer_ref, east_ref, north_ref, target_ref, depth_ref, w1_ref, b1_ref, w2_ref, b2_ref,
    cells, north_own, east_own, rows_out, edges_out, halo_w, halo_e, halo_edges, pick_out, pick_rows, pick_edges,
    fresh, misfits, gathered, feat, weights, hidden, slope, total, wanted, chunks, core_in, sending, landed,
    mine, strips, strips_in, strips_all, chunk,
    load_sems, halo_send, halo_recv, core_send, core_recv, send_sems, recv_sems,
    gather_send, gather_recv, forward_send, forward_recv, known_tiles, known_ring,
):
    z, x, m = lax.axis_index("ocx"), lax.axis_index("ocy"), lax.axis_index("ml")
    core = lax.rem(m, 2)
    chip = x * 4 + lax.div(m, 2)
    p = x * 8 + m
    sibling = (z, x, m + 1 - 2 * core)

    def other_chip(dx, dy):
        to_x, to_m = lax.rem(x + dx, 4), lax.rem(m + 2 * dy, 8)
        return to_x * 4 + lax.div(to_m, 2), (z, to_x, to_m)

    def ring(k):
        w = lax.rem(z + k, NZ)
        return w, (w, x, m)

    def tile(k):
        return (z, *place(lax.rem(p + k, TILES)))

    to_e, to_w = ring(1)[1], ring(NZ - 1)[1]
    to_n, to_s = tile(1), tile(TILES - 1)

    pairs = (
        (depth_hbm, depth_ref), (tracer_hbm, tracer_ref), (north_hbm, north_ref), (east_hbm, east_ref),
        (target_hbm, target_ref), (w1_hbm, w1_ref), (b1_hbm, b1_ref), (w2_hbm, w2_ref), (b2_hbm, b2_ref),
    )
    loads = [pltpu.make_async_copy(src, dst, load_sems.at[i]) for i, (src, dst) in enumerate(pairs)]
    for load in loads[:4]:
        load.start()

    barrier = pltpu.get_barrier_semaphore()

    def signal(target):
        pl.semaphore_signal(barrier, inc=1, device_id=target, device_id_type=MESH)

    def diagonal(dz, k):
        return (lax.rem(z + dz, NZ), *tile(k)[1:])

    to_ne, to_nw = diagonal(1, 1), diagonal(NZ - 1, 1)
    to_se, to_sw = diagonal(1, TILES - 1), diagonal(NZ - 1, TILES - 1)
    for target in (to_e, to_w, to_n, to_s, to_ne, to_nw, to_se, to_sw):
        signal(target)
    for load in loads[4:]:
        load.start()

    def spread_word(known, number, ahead, behind):
        for target in (ahead, behind):
            pl.semaphore_signal(known.at[number], inc=1, device_id=target, device_id_type=MESH)

    def spread_tiles(number):
        spread_word(known_tiles, number, tile(1 << number), tile(TILES - (1 << number)))

    def spread_ring(number):
        spread_word(known_ring, number, ring(1 << number)[1], ring(NZ - (1 << number))[1])

    def remote(src, dst, send_sem, recv_sem, target):
        return pltpu.make_async_remote_copy(
            src_ref=src, dst_ref=dst, send_sem=send_sem, recv_sem=recv_sem,
            device_id=target, device_id_type=MESH,
        )

    def whole(ref, number):
        return remote(ref, ref, send_sems.at[number], recv_sems.at[number], sibling)

    def halo(src, dst, number, target):
        copy = remote(src, dst, halo_send.at[number], halo_recv.at[number], target)
        copy.start()
        return copy

    item = lax.broadcasted_iota(jnp.int32, (2 * EDGE, CY), 0)
    lane_in = lax.broadcasted_iota(jnp.int32, (2 * EDGE, CY), 1)
    southern = item >= EDGE
    item = jnp.where(southern, item - EDGE, item)
    nth = jnp.where(southern, lane_in, lane_in - (CY - REACH))
    key = jnp.where(jnp.logical_and(nth >= 0, nth < REACH), item - nth, -999)
    nth = jnp.where(southern, nth, nth - 1)
    corner_key = jnp.where(jnp.logical_and(nth >= 0, nth < 2), item - nth, -999)
    for f, order in enumerate((CELL_AT, EAST_AT, NORTH_AT)):
        for i in range(CX):
            at = slice(CY * order[i], CY * (order[i] + 1))
            first = LATS + 4 * f + (2 * (i - 2) if i >= 2 else CORNER + 2 * i)
            hit = jnp.logical_or(key == 16 * f + 4 * i, corner_key == first)
            pick_out[:, at] = jnp.where(hit, 1.0, 0.0).astype(BF16)

    level = lax.broadcasted_iota(jnp.int32, (PAD, CY), 0).astype(F32)
    lane = lax.broadcasted_iota(jnp.int32, (PAD, CY), 1)
    tail = lax.broadcasted_iota(jnp.int32, (PAD - LEV, CY), 0)
    none = jnp.zeros((PAD - LEV, CY), F32)
    for load in loads[:4]:
        load.wait()
    depth = [depth_ref[i : i + 1, :].astype(F32) for i in range(CX)]
    for i in range(CX):
        cells[i, 0:LEV, :] = tracer_ref[:, i, :]
        cells[i, LEV:PAD, :] = jnp.where(tail == 0, depth[i], 0.0)
        north_own[i, 0:LEV, :] = north_ref[:, i, :]
        north_own[i, LEV:PAD, :] = none
        east_own[i, 0:LEV, :] = east_ref[:, i, :]
        east_own[i, LEV:PAD, :] = none
        rows_out[CELL_AT[i]] = cells[i].astype(BF16)
        rows_out[EAST_AT[i]] = east_own[i].astype(BF16)
        rows_out[NORTH_AT[i]] = north_own[i].astype(BF16)
    pl.semaphore_wait(barrier, 8)
    copies = [halo(rows_out.at[4:12], halo_w, 0, to_e), halo(rows_out.at[0:7], halo_e, 1, to_w)]
    spread_tiles(0)
    spread_ring(0)
    sources = jnp.concatenate([rows_out[n] for n in range(3 * CX)], axis=1)
    sources = jnp.concatenate([sources, jnp.zeros((CY - PAD, 3 * CX * CY), BF16)], axis=0)
    edges_out[...] = dot(pick_out[...], sources, ((1,), (1,))).astype(BF16)
    to_east, to_west = slice(LATS, LATS + CORNER), slice(LATS + CORNER, EDGE)
    for side, targets in enumerate(((to_n, to_ne, to_nw), (to_s, to_se, to_sw))):
        for n, some in enumerate((slice(0, LATS), to_east, to_west)):
            mine_at = edges_out.at[EDGE * side + some.start : EDGE * side + some.stop]
            there_at = halo_edges.at[EDGE * side + some.start : EDGE * side + some.stop]
            copies.append(halo(mine_at, there_at, 2 + 3 * side + n, targets[n]))

    lane_in = lax.broadcasted_iota(jnp.int32, (CY, CY), 0)
    lane_out = lax.broadcasted_iota(jnp.int32, (CY, CY), 1)
    shift = jnp.where(lane_in >= CY - REACH, lane_out - 2 * (lane_in - (CY - REACH)) + REACH, -999)
    shift = jnp.where(lane_in < REACH, lane_out - 2 * (lane_in + REACH), shift)
    shift = jnp.where(shift >= CY, shift - CY, shift)
    for n in range(WIDE):
        pick_rows[CY * n : CY * (n + 1), :] = jnp.where(shift == STRIP * n, 1.0, 0.0).astype(BF16)
    item = lax.broadcasted_iota(jnp.int32, (LATS, 3 * CY), 0)
    lane_out = lax.broadcasted_iota(jnp.int32, (LATS, 3 * CY), 1)
    shift = lane_out - (CY * (item // 16) + STRIP * (REACH + (item // 4) % 4) + 2 * (item % 4))
    shift = jnp.where(item % 4 < REACH, shift, -999)
    pick_edges[0:LATS, :] = jnp.where(shift == 0, 1.0, 0.0).astype(BF16)
    pick_edges[EDGE : EDGE + LATS, :] = jnp.where(shift == REACH, 1.0, 0.0).astype(BF16)
    item = lax.broadcasted_iota(jnp.int32, (CORNER, 3 * CY), 0)
    lane_out = lax.broadcasted_iota(jnp.int32, (CORNER, 3 * CY), 1)
    shift = lane_out - (CY * (item // 4) + STRIP * ((item // 2) % 2) + 2 * (item % 2))
    shift = jnp.where(item < 12, shift, -999)
    for n, (first, beside) in enumerate(((1, 2), (WIDE - REACH, 2), (1, REACH), (WIDE - REACH, REACH))):
        at = EDGE * (n // 2) + LATS + CORNER * (n % 2)
        pick_edges[at : at + CORNER, :] = jnp.where(shift == STRIP * first + beside, 1.0, 0.0).astype(BF16)

    masks = [level[0:LEV, :] < depth[i] for i in range(CX)]
    for i in range(CX):
        at = slice(CY * i, CY * (i + 1))
        feat[LEV : 2 * LEV, at] = jnp.where(masks[i], east_own[i, 0:LEV, :], 0.0)
        feat[2 * LEV : 3 * LEV, at] = jnp.where(masks[i], north_own[i, 0:LEV, :], 0.0)
    last = lax.broadcasted_iota(jnp.int32, (ROWS - 3 * LEV, CELLS), 0)
    feat[3 * LEV : ROWS, :] = jnp.where(last < 2, 1.0, 0.0)
    pl.semaphore_wait(known_tiles.at[0], 2)
    spread_tiles(1)
    pl.semaphore_wait(known_ring.at[0], 2)
    spread_ring(1)
    for load in loads[4:]:
        load.wait()
    wanted[...] = target_ref[...].astype(F32)
    edge = 3 * LEV // 16 * 16
    weights[0:edge, :] = w1_ref[0:edge, :]
    bias = b1_ref[...]
    coarse = bias.astype(BF16).astype(F32)
    row = lax.broadcasted_iota(jnp.int32, (ROWS - edge, HID), 0) + edge
    final = jnp.where(row == 3 * LEV - 1, w1_ref[3 * LEV - 1 : 3 * LEV, :].astype(F32), 0.0)
    final = jnp.where(row == 3 * LEV, coarse, final)
    final = jnp.where(row == 3 * LEV + 1, bias - coarse, final)
    weights[edge:ROWS, :] = final.astype(BF16)

    pl.semaphore_wait(known_tiles.at[1], 2)
    spread_tiles(2)
    for copy in copies:
        copy.wait_recv()

    cell_rows = [halo_w[0], halo_w[1], halo_w[3]] + [rows_out[n] for n in CELL_AT] + [halo_e[3], halo_e[4], halo_e[5]]
    east_rows = [halo_w[2], halo_w[4], halo_w[5]] + [rows_out[n] for n in EAST_AT] + [halo_e[2], halo_e[6]]
    north_rows = [halo_w[6], halo_w[7]] + [rows_out[n] for n in NORTH_AT] + [halo_e[0], halo_e[1]]
    beyond = dot(halo_edges[...], pick_edges[...], ((0,), (0,)))[0:PAD, :]

    def strip_of(some, first, f):
        own = dot(
            jnp.concatenate(some, axis=1), pick_rows[CY * first : CY * (first + len(some)), :], ((1,), (0,))
        )
        return own + beyond[:, CY * f : CY * (f + 1)]

    def turn(value, by):
        by = by % CY
        return pltpu.roll(value, by, 1) if by else value

    strip = strip_of(cell_rows, 0, 0)
    deep_here = jnp.broadcast_to(strip[LEV : LEV + 1, :], (PAD, CY))
    near_e, far_e = faces(level < jnp.minimum(deep_here, turn(deep_here, -STRIP)), strip_of(east_rows, 0, 1))
    at_south = jnp.logical_and(lane % STRIP == 2 * (REACH - 1), p == 0)
    at_north = jnp.logical_and(lane % STRIP == 2 * (REACH - 1) - REACH, p == TILES - 1)
    shut = jnp.logical_or(at_south, at_north)
    opened = jnp.logical_and(level < jnp.minimum(deep_here, turn(deep_here, -2)), jnp.logical_not(shut))
    strip_near, strip_far = faces(opened, strip_of(north_rows, 1, 2))
    near_w, far_w = turn(near_e, STRIP), turn(far_e, STRIP)
    near_s, far_s = turn(strip_near, 2), turn(strip_far, 2)
    strip_coef = (1.0 + far_w - near_e + far_s - strip_near, near_w, far_e, near_s, strip_far)
    strips_at = [strip]
    for step in range(STEPS - 1):
        keep, near_w, far_e, near_s, far_n = strip_coef
        strip = (
            keep * strip + near_w * turn(strip, STRIP) - far_e * turn(strip, -STRIP)
            + near_s * turn(strip, 2) - far_n * turn(strip, -2)
        )
        strips_at.append(strip)

    now = [
        cells[n - REACH] if REACH <= n < REACH + CX else cell_rows[n].astype(F32) for n in range(WIDE)
    ]
    deep = [jnp.broadcast_to(value[LEV : LEV + 1, :], (PAD, CY)) for value in now]
    east_faces = []
    for n in range(WIDE - 1):
        speed = east_own[n - REACH] if REACH <= n < REACH + CX else east_rows[n].astype(F32)
        east_faces.append(faces(level < jnp.minimum(deep[n], deep[n + 1]), speed))
    coef = [None] * WIDE
    for n in range(1, WIDE - 1):
        speed = north_own[n - REACH] if REACH <= n < REACH + CX else north_rows[n - 1].astype(F32)
        near_n, far_n = faces(level < jnp.minimum(deep[n], turn(deep[n], -1)), speed)
        edge_at = -(STRIP * n + 2)
        near_n = jnp.where(lane == CY - 1, turn(strip_near, edge_at), near_n)
        far_n = jnp.where(lane == CY - 1, turn(strip_far, edge_at), far_n)
        beyond_at = -(STRIP * n + 2 * (REACH - 1))
        near_s = jnp.where(lane == 0, turn(strip_near, beyond_at), turn(near_n, 1))
        far_s = jnp.where(lane == 0, turn(strip_far, beyond_at), turn(far_n, 1))
        near_w, far_w = east_faces[n - 1]
        near_e, far_e = east_faces[n]
        coef[n] = (1.0 + far_w - near_e + far_s - near_n, near_w, far_e, near_s, far_n)
    for step in range(STEPS):
        after = list(now)
        for n in range(step + 1, WIDE - 1 - step):
            keep, near_w, far_e, near_s, far_n = coef[n]
            past = turn(strips_at[step], -(STRIP * n + 2 * (REACH - 1)))
            south = jnp.where(lane == 0, past, turn(now[n], 1))
            north = jnp.where(lane == CY - 1, past, turn(now[n], -1))
            after[n] = (
                keep * now[n] + near_w * now[n - 1] - far_e * now[n + 1] + near_s * south - far_n * north
            )
        now = after
    for i in range(CX):
        cells[i] = now[REACH + i]
    pl.semaphore_wait(known_tiles.at[2], 2)
    spread_tiles(3)
    for i in range(CX):
        at = slice(CY * i, CY * (i + 1))
        feat[0:LEV, at] = jnp.where(masks[i], cells[i, 0:LEV, :], 0.0)
    inputs = feat[...].astype(BF16)

    acc = None
    for b in range(HID // BLK):
        at = slice(b * BLK, (b + 1) * BLK)
        before = dot(weights[:, at], inputs, ((0,), (0,)))
        stash = before.astype(BF16).astype(F32)
        gate = 0.5 * jnp.tanh(0.5 * stash) + 0.5
        act = (stash * gate).astype(BF16)
        hidden[at, :] = act
        slope[at, :] = gate * (1.0 + stash * (1.0 - gate))
        part = dot(w2_ref[:, at], act, ((1,), (0,)))
        acc = part if acc is None else acc + part
    pl.semaphore_wait(known_ring.at[1], 2)
    spread_ring(2)
    eye = lax.broadcasted_iota(jnp.int32, (LEV, LEV), 0) == lax.broadcasted_iota(jnp.int32, (LEV, LEV), 1)
    bias2 = jnp.sum(jnp.where(eye, b2_ref[...], 0.0), axis=1, keepdims=True)
    output = acc + bias2
    total[...] = jnp.zeros((PAD, CELLS), F32)
    for i in range(CX):
        at = slice(CY * i, CY * (i + 1))
        tendency = jnp.where(masks[i], output[:, at], 0.0).astype(BF16).astype(F32)
        goal = jnp.where(masks[i], wanted[:, i, :], 0.0)
        misfit = tendency - goal
        total[0:LEV, at] = misfit * (1.0 / COLUMNS)
        fresh[i, 0:LEV, :] = cells[i, 0:LEV, :] + tendency
        misfits[i, 0:LEV, :] = misfit
    d_out = total[...].astype(BF16)
    ones = jnp.ones((16, CELLS), BF16)
    bias_grad = dot(ones, d_out, ((1,), (1,)))
    spread = lax.broadcasted_iota(jnp.int32, (PAD, CY), 0) == LEV
    per = BLK // CY
    to_sibling = []
    for b in range(HID // BLK):
        at = slice(b * BLK, (b + 1) * BLK)
        d_hidden = dot(w2_ref[:, at], d_out[0:LEV, :], ((0,), (0,)))
        d_before = (d_hidden * slope[at, :]).astype(BF16)
        g1 = dot(inputs, d_before, ((1,), (1,)))
        g2 = dot(d_out, hidden[at, :], ((1,), (1,)))
        for t in range(per):
            lanes = slice(t * CY, (t + 1) * CY)
            tile = b * per + t
            for g in range(3):
                chunks[g % 2, 2 * tile + g // 2] = g1[PAD * g : PAD * (g + 1), lanes]
            last_part = g2[:, lanes]
            if tile == 0:
                row = jnp.concatenate([bias_grad[0:1, :], jnp.zeros((1, CY - PAD), F32)], axis=1)
                last_part = jnp.where(spread, row, last_part)
            chunks[1, 2 * tile + 1] = last_part
        some = pl.ds(2 * per * b, 2 * per)
        copy = remote(chunks.at[1 - core, some], core_in.at[some], core_send.at[b], core_recv.at[b], sibling)
        copy.start()
        to_sibling.append(copy)
    row = lax.broadcasted_iota(jnp.int32, (PAD, CY), 0)
    bias_row = 3 * LEV - 2 * PAD + core * (LEV - (3 * LEV - 2 * PAD))
    for b in range(HID // BLK):
        to_sibling[b].wait_recv()
        some = pl.ds(2 * per * b, 2 * per)
        both = chunks[core, some] + core_in[some]
        for j in range(2 * per):
            value = both[j]
            sent = value
            if j % 2:
                low = value - value.astype(BF16).astype(F32)
                sent = jnp.where(row == bias_row + 1, pltpu.roll(low, 1, 0), value)
            sending[2 * per * b + j] = sent.astype(BF16)

    pl.semaphore_wait(known_tiles.at[3], 2)

    for n, (dx, dy) in enumerate(STEPS_XY):
        c, target = other_chip(dx, dy)
        remote(sending.at[c], landed.at[n], send_sems.at[0], recv_sems.at[0], target).start()
    for i in range(CX):
        tracer_out[:, i, :] = fresh[i, 0:LEV, :]
        wanted[:, i, :] = misfits[i, 0:LEV, :]
    misfit_out[...] = wanted[...].astype(BF16)
    has_bias = lax.rem(chip, 2) == 1
    amount = chunks[core, chip] + core_in[chip]
    amount = jnp.where(jnp.logical_and(row == bias_row + 1, has_bias), 0.0, amount)
    whole(landed, 0).wait_recv()
    for k in range(CHIPS - 1):
        amount = amount + landed[k].astype(F32)
    mine[...] = amount
    part = PAD // NZ
    for k in range(NZ):
        strips[k] = mine[part * k : part * (k + 1), :]

    pl.semaphore_wait(known_ring.at[2], 2)
    for n, k in enumerate(STEPS_Z):
        w, target = ring(k)
        remote(strips.at[w], strips_in.at[n], send_sems.at[1], recv_sems.at[1], target).start()
    whole(strips_in, 1).wait_recv()
    strip = strips[z]
    for n in range(NZ - 1):
        strip = strip + strips_in[n]
    strips_all[z] = strip
    for k in STEPS_Z:
        _, target = ring(k)
        remote(strips_all.at[z], strips_all.at[z], send_sems.at[2], recv_sems.at[2], target).start()
    whole(strips_in, 2).wait_recv()
    for k in range(NZ):
        mine[part * k : part * (k + 1), :] = strips_all[k]
    value = mine[...]
    both = jnp.where(jnp.logical_and(row == bias_row, has_bias), pltpu.roll(value, PAD - 1, 0), 0.0) + value
    low = both - both.astype(BF16).astype(F32)
    both = jnp.where(jnp.logical_and(row == bias_row + 1, has_bias), pltpu.roll(low, 1, 0), both)
    chunk[...] = both.astype(BF16)
    gathered[core, 0] = chunk[...]
    forwards = []
    for dx in (2, 1, 3, 0):
        for dy in (2, 1, 3, 0):
            if dx or dy:
                _, target = other_chip(dx, dy)
                slot = gathered.at[core, 4 * dx + dy]
                remote(chunk, slot, gather_send.at[dx], gather_recv.at[dx], target).start()
    for dx in (2, 1, 3, 0):
        some = gathered.at[core, 4 * dx + (dx == 0) : 4 * dx + 4]
        remote(some, some, gather_send.at[dx], gather_recv.at[dx], sibling).wait_recv()
        some = gathered.at[core, 4 * dx : 4 * dx + 4]
        forwards.append(remote(some, some, forward_send.at[dx], forward_recv.at[dx], sibling))
        forwards[-1].start()

    def unpack(half):
        rest = 3 * LEV - 2 * PAD
        y = lax.div(m, 2)
        for t in range(HID // CY):
            lanes = slice(t * CY, (t + 1) * CY)
            from_x = lax.rem(x + 4 - t // 2, 4) * 4
            first = from_x + lax.rem(y + 4 - 2 * (t % 2), 4)
            second = from_x + lax.rem(y + 3 - 2 * (t % 2), 4)
            w1_out[PAD * half : PAD * (half + 1), lanes] = gathered[half, first].astype(F32)
            value = gathered[half, second].astype(F32)
            if half == 0:
                w1_out[2 * PAD : 3 * LEV, lanes] = value[0:rest, :]
                b1_out[:, lanes] = value[rest : rest + 1, :] + value[rest + 1 : rest + 2, :]
            else:
                w2_out[:, lanes] = value[0:LEV, :]
                if t == 0:
                    b2_out[...] = value[LEV : LEV + 1, 0:LEV] + value[LEV + 1 : LEV + 2, 0:LEV]

    for half in range(2):
        pl.when(core == half)(functools.partial(unpack, half))
    for copy in copies + to_sibling:
        copy.wait_send()
    whole(landed, 0).wait_send()
    whole(strips_in, 1).wait_send()
    whole(strips_in, 2).wait_send()
    for dx in (2, 1, 3, 0):
        some = gathered.at[core, 4 * dx + (dx == 0) : 4 * dx + 4]
        remote(some, some, gather_send.at[dx], gather_recv.at[dx], sibling).wait_send()
    for forward in forwards:
        forward.wait()
    for half in range(2):
        pl.when(core != half)(functools.partial(unpack, half))


def main(*operands):
    vmem = pl.BlockSpec(memory_space=pltpu.VMEM)
    hbm = pl.BlockSpec(memory_space=pltpu.HBM)
    part = PAD // NZ
    halves = HID // BLK
    return pl.pallas_call(
        main_kernel,
        out_shape=(
            jax.ShapeDtypeStruct((LEV, CX, CY), F32),
            jax.ShapeDtypeStruct((LEV, CX, CY), BF16),
            jax.ShapeDtypeStruct((3 * LEV, HID), F32),
            jax.ShapeDtypeStruct((1, HID), F32),
            jax.ShapeDtypeStruct((LEV, HID), F32),
            jax.ShapeDtypeStruct((1, LEV), F32),
        ),
        in_specs=[hbm] * 9,
        out_specs=(vmem,) * 6,
        scratch_shapes=[pltpu.VMEM(a.shape, a.dtype) for a in operands]
        + [
            pltpu.VMEM((CX, PAD, CY), F32),
            pltpu.VMEM((CX, PAD, CY), F32),
            pltpu.VMEM((CX, PAD, CY), F32),
            pltpu.VMEM((3 * CX, PAD, CY), BF16),
            pltpu.VMEM((2 * EDGE, CY), BF16),
            pltpu.VMEM((8, PAD, CY), BF16),
            pltpu.VMEM((7, PAD, CY), BF16),
            pltpu.VMEM((2 * EDGE, CY), BF16),
            pltpu.VMEM((2 * EDGE, 3 * CX * CY), BF16),
            pltpu.VMEM((WIDE * CY, CY), BF16),
            pltpu.VMEM((2 * EDGE, 3 * CY), BF16),
            pltpu.VMEM((CX, PAD, CY), F32),
            pltpu.VMEM((CX, PAD, CY), F32),
            pltpu.VMEM((2, CHIPS, PAD, CY), BF16),
            pltpu.VMEM((ROWS, CELLS), F32),
            pltpu.VMEM((ROWS, HID), BF16),
            pltpu.VMEM((HID, CELLS), BF16),
            pltpu.VMEM((HID, CELLS), F32),
            pltpu.VMEM((PAD, CELLS), F32),
            pltpu.VMEM((LEV, CX, CY), F32),
            pltpu.VMEM((2, CHIPS, PAD, CY), F32),
            pltpu.VMEM((CHIPS, PAD, CY), F32),
            pltpu.VMEM((CHIPS, PAD, CY), BF16),
            pltpu.VMEM((CHIPS - 1, PAD, CY), BF16),
            pltpu.VMEM((PAD, CY), F32),
            pltpu.VMEM((NZ, part, CY), F32),
            pltpu.VMEM((NZ - 1, part, CY), F32),
            pltpu.VMEM((NZ, part, CY), F32),
            pltpu.VMEM((PAD, CY), BF16),
            pltpu.SemaphoreType.DMA((len(operands),)),
            pltpu.SemaphoreType.DMA((8,)),
            pltpu.SemaphoreType.DMA((8,)),
            pltpu.SemaphoreType.DMA((halves,)),
            pltpu.SemaphoreType.DMA((halves,)),
            pltpu.SemaphoreType.DMA((3,)),
            pltpu.SemaphoreType.DMA((3,)),
            pltpu.SemaphoreType.DMA((4,)),
            pltpu.SemaphoreType.DMA((4,)),
            pltpu.SemaphoreType.DMA((4,)),
            pltpu.SemaphoreType.DMA((4,)),
            pltpu.SemaphoreType.REGULAR((4,)),
            pltpu.SemaphoreType.REGULAR((3,)),
        ],
        compiler_params=pltpu.CompilerParams(
            collective_id=0, has_side_effects=True, vmem_limit_bytes=VMEM_LIMIT
        ),
        name="main",
    )(*(pltpu.with_memory_space_constraint(a, pltpu.HBM) for a in operands))


def store_kernel(*refs):
    count = len(refs) // 2
    copies = [pltpu.make_async_copy(refs[i], refs[count + i], refs[-1].at[i]) for i in (2, 4, 0, 1, 3, 5)]
    for copy in copies:
        copy.start()
    for copy in copies:
        copy.wait()


def store(*results):
    vmem = pl.BlockSpec(memory_space=pltpu.VMEM)
    hbm = pl.BlockSpec(memory_space=pltpu.HBM)
    return pl.pallas_call(
        store_kernel,
        out_shape=tuple(jax.ShapeDtypeStruct(a.shape, a.dtype) for a in results),
        in_specs=[vmem] * len(results),
        out_specs=(hbm,) * len(results),
        scratch_shapes=[pltpu.SemaphoreType.DMA((len(results),))],
        compiler_params=pltpu.CompilerParams(vmem_limit_bytes=16 * 1024 * 1024),
        name="store",
    )(*results)


def on_device(tracer, east, north, target, depth, slots, w1, b1, w2, b2):
    results = main(tracer, east, north, target, depth, w1, b1.reshape(1, HID), w2.T, b2.reshape(1, LEV))
    tracer_out, misfit_out, grad_w1, grad_b1, grad_w2, grad_b2 = store(*results)
    return tracer_out, misfit_out, grad_w1, grad_b1.reshape(HID), grad_w2.T, grad_b2.reshape(LEV)


def solution(mesh):
    grid = P(None, "ocx", ("ocy", "ml"))
    return jax.shard_map(
        on_device,
        mesh=mesh,
        in_specs=(grid, grid, grid, grid, P("ocx", ("ocy", "ml")), P("ocx", ("ocy", "ml"), None, None), P(), P(), P(), P()),
        out_specs=(grid, grid, P(), P(), P(), P()),
        check_vma=False,
    )
```

```python
import functools

import jax
import jax.numpy as jnp
from jax import lax
from jax.experimental import pallas as pl
from jax.experimental.pallas import tpu as pltpu
from jax.sharding import PartitionSpec as P

MESH = pl.DeviceIdType.MESH
KAPPA = 0.1
STEPS = 3
LEV = 75
PAD = 80
CX = 4
CY = 128
CELLS = CX * CY
HID = 1024
ROWS = 240
TILES = 32
NZ = 16
CHIPS = 16
COLUMNS = 262144
REACH = 3
WIDE = CX + 2 * REACH
STRIP = 4 * REACH
LATS = 16 * 3
CORNER = 16
EDGE = LATS + 2 * CORNER
NORTH_AT = (0, 1, 2, 3)
EAST_AT = (4, 5, 6, 7)
CELL_AT = (8, 9, 10, 11)
BLK = 256
STEPS_XY = (
    (2, 2), (2, 1), (2, 3), (1, 2), (3, 2), (1, 1), (1, 3), (3, 1), (3, 3), (2, 0), (0, 2), (1, 0), (3, 0), (0, 1), (0, 3)
)
STEPS_Z = (8, 7, 9, 6, 10, 5, 11, 4, 12, 3, 13, 2, 14, 1, 15)
F32 = jnp.float32
BF16 = jnp.bfloat16
VMEM_LIMIT = 40 * 1024 * 1024


def place(p):
    return lax.div(p, 8), lax.rem(p, 8)


def faces(opened, speed):
    near = jnp.where(opened, jnp.maximum(speed, 0.0) + KAPPA, 0.0)
    far = jnp.where(opened, jnp.minimum(speed, 0.0) - KAPPA, 0.0)
    return near, far


def dot(a, b, dims):
    return lax.dot_general(a, b, (dims, ((), ())), preferred_element_type=F32)


def main_kernel(
    tracer_hbm, east_hbm, north_hbm, target_hbm, depth_hbm, w1_hbm, b1_hbm, w2_hbm, b2_hbm,
    tracer_out, misfit_out, w1_out, b1_out, w2_out, b2_out,
    tracer_ref, east_ref, north_ref, target_ref, depth_ref, w1_ref, b1_ref, w2_ref, b2_ref,
    cells, north_own, east_own, rows_out, edges_out, halo_w, halo_e, halo_edges, pick_out, pick_rows, pick_edges,
    fresh, misfits, gathered, feat, weights, hidden, slope, total, wanted, chunks, core_in, sending, landed,
    mine, strips, strips_in, strips_all, chunk,
    load_sems, halo_send, halo_recv, core_send, core_recv, send_sems, recv_sems,
    gather_send, gather_recv, forward_send, forward_recv, known_tiles, known_ring,
):
    z, x, m = lax.axis_index("ocx"), lax.axis_index("ocy"), lax.axis_index("ml")
    core = lax.rem(m, 2)
    chip = x * 4 + lax.div(m, 2)
    p = x * 8 + m
    sibling = (z, x, m + 1 - 2 * core)

    def other_chip(dx, dy):
        to_x, to_m = lax.rem(x + dx, 4), lax.rem(m + 2 * dy, 8)
        return to_x * 4 + lax.div(to_m, 2), (z, to_x, to_m)

    def ring(k):
        w = lax.rem(z + k, NZ)
        return w, (w, x, m)

    def tile(k):
        return (z, *place(lax.rem(p + k, TILES)))

    to_e, to_w = ring(1)[1], ring(NZ - 1)[1]
    to_n, to_s = tile(1), tile(TILES - 1)

    pairs = (
        (north_hbm, north_ref), (east_hbm, east_ref), (depth_hbm, depth_ref), (tracer_hbm, tracer_ref),
        (target_hbm, target_ref), (w1_hbm, w1_ref), (b1_hbm, b1_ref), (w2_hbm, w2_ref), (b2_hbm, b2_ref),
    )
    loads = [pltpu.make_async_copy(src, dst, load_sems.at[i]) for i, (src, dst) in enumerate(pairs)]
    for load in loads[:4]:
        load.start()

    barrier = pltpu.get_barrier_semaphore()

    def signal(target):
        pl.semaphore_signal(barrier, inc=1, device_id=target, device_id_type=MESH)

    def diagonal(dz, k):
        return (lax.rem(z + dz, NZ), *tile(k)[1:])

    to_ne, to_nw = diagonal(1, 1), diagonal(NZ - 1, 1)
    to_se, to_sw = diagonal(1, TILES - 1), diagonal(NZ - 1, TILES - 1)
    for target in (to_e, to_w, to_n, to_s, to_ne, to_nw, to_se, to_sw):
        signal(target)

    def spread_word(known, number, ahead, behind):
        for target in (ahead, behind):
            pl.semaphore_signal(known.at[number], inc=1, device_id=target, device_id_type=MESH)

    def spread_tiles(number):
        spread_word(known_tiles, number, tile(1 << number), tile(TILES - (1 << number)))

    def spread_ring(number):
        spread_word(known_ring, number, ring(1 << number)[1], ring(NZ - (1 << number))[1])

    def remote(src, dst, send_sem, recv_sem, target):
        return pltpu.make_async_remote_copy(
            src_ref=src, dst_ref=dst, send_sem=send_sem, recv_sem=recv_sem,
            device_id=target, device_id_type=MESH,
        )

    def whole(ref, number):
        return remote(ref, ref, send_sems.at[number], recv_sems.at[number], sibling)

    def halo(src, dst, number, target):
        copy = remote(src, dst, halo_send.at[number], halo_recv.at[number], target)
        copy.start()
        return copy

    item = lax.broadcasted_iota(jnp.int32, (2 * EDGE, CY), 0)
    lane_in = lax.broadcasted_iota(jnp.int32, (2 * EDGE, CY), 1)
    southern = item >= EDGE
    item = jnp.where(southern, item - EDGE, item)
    nth = jnp.where(southern, lane_in, lane_in - (CY - REACH))
    key = jnp.where(jnp.logical_and(nth >= 0, nth < REACH), item - nth, -999)
    nth = jnp.where(southern, nth, nth - 1)
    corner_key = jnp.where(jnp.logical_and(nth >= 0, nth < 2), item - nth, -999)
    for f, order in enumerate((CELL_AT, EAST_AT, NORTH_AT)):
        for i in range(CX):
            at = slice(CY * order[i], CY * (order[i] + 1))
            first = LATS + 4 * f + (2 * (i - 2) if i >= 2 else CORNER + 2 * i)
            hit = jnp.logical_or(key == 16 * f + 4 * i, corner_key == first)
            pick_out[:, at] = jnp.where(hit, 1.0, 0.0).astype(BF16)

    level = lax.broadcasted_iota(jnp.int32, (PAD, CY), 0).astype(F32)
    lane = lax.broadcasted_iota(jnp.int32, (PAD, CY), 1)
    tail = lax.broadcasted_iota(jnp.int32, (PAD - LEV, CY), 0)
    none = jnp.zeros((PAD - LEV, CY), F32)
    copies = []

    def send_rows(first, east_from, east_rows_n, west_rows_n, east_at, west_at):
        number = len(copies)
        start = first + east_from
        copies.append(
            halo(rows_out.at[start : start + east_rows_n], halo_w.at[east_at : east_at + east_rows_n], number, to_e)
        )
        copies.append(
            halo(rows_out.at[first : first + west_rows_n], halo_e.at[west_at : west_at + west_rows_n], number + 1, to_w)
        )

    loads[0].wait()
    for i in range(CX):
        north_own[i, 0:LEV, :] = north_ref[:, i, :]
        north_own[i, LEV:PAD, :] = none
        rows_out[NORTH_AT[i]] = north_own[i].astype(BF16)
    pl.semaphore_wait(barrier, 8)
    send_rows(NORTH_AT[0], 2, 2, 2, 0, 0)
    loads[1].wait()
    for i in range(CX):
        east_own[i, 0:LEV, :] = east_ref[:, i, :]
        east_own[i, LEV:PAD, :] = none
        rows_out[EAST_AT[i]] = east_own[i].astype(BF16)
    send_rows(EAST_AT[0], 1, 3, 2, 2, 2)
    for load in loads[2:4]:
        load.wait()
    depth = [depth_ref[i : i + 1, :].astype(F32) for i in range(CX)]
    for i in range(CX):
        cells[i, 0:LEV, :] = tracer_ref[:, i, :]
        cells[i, LEV:PAD, :] = jnp.where(tail == 0, depth[i], 0.0)
        rows_out[CELL_AT[i]] = cells[i].astype(BF16)
    send_rows(CELL_AT[0], 1, 3, 3, 5, 4)
    for load in loads[4:]:
        load.start()
    spread_tiles(0)
    spread_ring(0)
    sources = jnp.concatenate([rows_out[n] for n in range(3 * CX)], axis=1)
    sources = jnp.concatenate([sources, jnp.zeros((CY - PAD, 3 * CX * CY), BF16)], axis=0)
    edges_out[...] = dot(pick_out[...], sources, ((1,), (1,))).astype(BF16)
    to_east, to_west = slice(LATS, LATS + CORNER), slice(LATS + CORNER, EDGE)
    for side, targets in enumerate(((to_n, to_ne, to_nw), (to_s, to_se, to_sw))):
        for n, some in enumerate((slice(0, LATS), to_east, to_west)):
            mine_at = edges_out.at[EDGE * side + some.start : EDGE * side + some.stop]
            there_at = halo_edges.at[EDGE * side + some.start : EDGE * side + some.stop]
            copies.append(halo(mine_at, there_at, len(copies), targets[n]))

    lane_in = lax.broadcasted_iota(jnp.int32, (CY, CY), 0)
    lane_out = lax.broadcasted_iota(jnp.int32, (CY, CY), 1)
    shift = jnp.where(lane_in >= CY - REACH, lane_out - 2 * (lane_in - (CY - REACH)) + REACH, -999)
    shift = jnp.where(lane_in < REACH, lane_out - 2 * (lane_in + REACH), shift)
    shift = jnp.where(shift >= CY, shift - CY, shift)
    for n in range(WIDE):
        pick_rows[CY * n : CY * (n + 1), :] = jnp.where(shift == STRIP * n, 1.0, 0.0).astype(BF16)
    item = lax.broadcasted_iota(jnp.int32, (LATS, 3 * CY), 0)
    lane_out = lax.broadcasted_iota(jnp.int32, (LATS, 3 * CY), 1)
    shift = lane_out - (CY * (item // 16) + STRIP * (REACH + (item // 4) % 4) + 2 * (item % 4))
    shift = jnp.where(item % 4 < REACH, shift, -999)
    pick_edges[0:LATS, :] = jnp.where(shift == 0, 1.0, 0.0).astype(BF16)
    pick_edges[EDGE : EDGE + LATS, :] = jnp.where(shift == REACH, 1.0, 0.0).astype(BF16)
    item = lax.broadcasted_iota(jnp.int32, (CORNER, 3 * CY), 0)
    lane_out = lax.broadcasted_iota(jnp.int32, (CORNER, 3 * CY), 1)
    shift = lane_out - (CY * (item // 4) + STRIP * ((item // 2) % 2) + 2 * (item % 2))
    shift = jnp.where(item < 12, shift, -999)
    for n, (first, beside) in enumerate(((1, 2), (WIDE - REACH, 2), (1, REACH), (WIDE - REACH, REACH))):
        at = EDGE * (n // 2) + LATS + CORNER * (n % 2)
        pick_edges[at : at + CORNER, :] = jnp.where(shift == STRIP * first + beside, 1.0, 0.0).astype(BF16)

    masks = [level[0:LEV, :] < depth[i] for i in range(CX)]
    for i in range(CX):
        at = slice(CY * i, CY * (i + 1))
        feat[LEV : 2 * LEV, at] = jnp.where(masks[i], east_own[i, 0:LEV, :], 0.0)
        feat[2 * LEV : 3 * LEV, at] = jnp.where(masks[i], north_own[i, 0:LEV, :], 0.0)
    last = lax.broadcasted_iota(jnp.int32, (ROWS - 3 * LEV, CELLS), 0)
    feat[3 * LEV : ROWS, :] = jnp.where(last < 2, 1.0, 0.0)
    pl.semaphore_wait(known_tiles.at[0], 2)
    spread_tiles(1)
    pl.semaphore_wait(known_ring.at[0], 2)
    spread_ring(1)
    for load in loads[4:]:
        load.wait()
    wanted[...] = target_ref[...].astype(F32)
    edge = 3 * LEV // 16 * 16
    weights[0:edge, :] = w1_ref[0:edge, :]
    bias = b1_ref[...]
    coarse = bias.astype(BF16).astype(F32)
    row = lax.broadcasted_iota(jnp.int32, (ROWS - edge, HID), 0) + edge
    final = jnp.where(row == 3 * LEV - 1, w1_ref[3 * LEV - 1 : 3 * LEV, :].astype(F32), 0.0)
    final = jnp.where(row == 3 * LEV, coarse, final)
    final = jnp.where(row == 3 * LEV + 1, bias - coarse, final)
    weights[edge:ROWS, :] = final.astype(BF16)

    pl.semaphore_wait(known_tiles.at[1], 2)
    spread_tiles(2)
    for copy in copies:
        copy.wait_recv()

    cell_rows = [halo_w[5 + n] for n in range(3)] + [rows_out[n] for n in CELL_AT] + [halo_e[4 + n] for n in range(3)]
    east_rows = [halo_w[2 + n] for n in range(3)] + [rows_out[n] for n in EAST_AT] + [halo_e[2 + n] for n in range(2)]
    north_rows = [halo_w[n] for n in range(2)] + [rows_out[n] for n in NORTH_AT] + [halo_e[n] for n in range(2)]
    beyond = dot(halo_edges[...], pick_edges[...], ((0,), (0,)))[0:PAD, :]

    def strip_of(some, first, f):
        own = dot(
            jnp.concatenate(some, axis=1), pick_rows[CY * first : CY * (first + len(some)), :], ((1,), (0,))
        )
        return own + beyond[:, CY * f : CY * (f + 1)]

    def turn(value, by):
        by = by % CY
        return pltpu.roll(value, by, 1) if by else value

    strip = strip_of(cell_rows, 0, 0)
    deep_here = jnp.broadcast_to(strip[LEV : LEV + 1, :], (PAD, CY))
    near_e, far_e = faces(level < jnp.minimum(deep_here, turn(deep_here, -STRIP)), strip_of(east_rows, 0, 1))
    at_south = jnp.logical_and(lane % STRIP == 2 * (REACH - 1), p == 0)
    at_north = jnp.logical_and(lane % STRIP == 2 * (REACH - 1) - REACH, p == TILES - 1)
    shut = jnp.logical_or(at_south, at_north)
    opened = jnp.logical_and(level < jnp.minimum(deep_here, turn(deep_here, -2)), jnp.logical_not(shut))
    strip_near, strip_far = faces(opened, strip_of(north_rows, 1, 2))
    near_w, far_w = turn(near_e, STRIP), turn(far_e, STRIP)
    near_s, far_s = turn(strip_near, 2), turn(strip_far, 2)
    strip_coef = (1.0 + far_w - near_e + far_s - strip_near, near_w, far_e, near_s, strip_far)
    strips_at = [strip]
    for step in range(STEPS - 1):
        keep, near_w, far_e, near_s, far_n = strip_coef
        strip = (
            keep * strip + near_w * turn(strip, STRIP) - far_e * turn(strip, -STRIP)
            + near_s * turn(strip, 2) - far_n * turn(strip, -2)
        )
        strips_at.append(strip)

    now = [
        cells[n - REACH] if REACH <= n < REACH + CX else cell_rows[n].astype(F32) for n in range(WIDE)
    ]
    deep = [jnp.broadcast_to(value[LEV : LEV + 1, :], (PAD, CY)) for value in now]
    east_faces = []
    for n in range(WIDE - 1):
        speed = east_own[n - REACH] if REACH <= n < REACH + CX else east_rows[n].astype(F32)
        east_faces.append(faces(level < jnp.minimum(deep[n], deep[n + 1]), speed))
    coef = [None] * WIDE
    for n in range(1, WIDE - 1):
        speed = north_own[n - REACH] if REACH <= n < REACH + CX else north_rows[n - 1].astype(F32)
        near_n, far_n = faces(level < jnp.minimum(deep[n], turn(deep[n], -1)), speed)
        edge_at = -(STRIP * n + 2)
        near_n = jnp.where(lane == CY - 1, turn(strip_near, edge_at), near_n)
        far_n = jnp.where(lane == CY - 1, turn(strip_far, edge_at), far_n)
        beyond_at = -(STRIP * n + 2 * (REACH - 1))
        near_s = jnp.where(lane == 0, turn(strip_near, beyond_at), turn(near_n, 1))
        far_s = jnp.where(lane == 0, turn(strip_far, beyond_at), turn(far_n, 1))
        near_w, far_w = east_faces[n - 1]
        near_e, far_e = east_faces[n]
        coef[n] = (1.0 + far_w - near_e + far_s - near_n, near_w, far_e, near_s, far_n)
    for step in range(STEPS):
        after = list(now)
        for n in range(step + 1, WIDE - 1 - step):
            keep, near_w, far_e, near_s, far_n = coef[n]
            past = turn(strips_at[step], -(STRIP * n + 2 * (REACH - 1)))
            south = jnp.where(lane == 0, past, turn(now[n], 1))
            north = jnp.where(lane == CY - 1, past, turn(now[n], -1))
            after[n] = (
                keep * now[n] + near_w * now[n - 1] - far_e * now[n + 1] + near_s * south - far_n * north
            )
        now = after
    for i in range(CX):
        cells[i] = now[REACH + i]
    pl.semaphore_wait(known_tiles.at[2], 2)
    spread_tiles(3)
    for i in range(CX):
        at = slice(CY * i, CY * (i + 1))
        feat[0:LEV, at] = jnp.where(masks[i], cells[i, 0:LEV, :], 0.0)
    inputs = feat[...].astype(BF16)

    acc = None
    for b in range(HID // BLK):
        at = slice(b * BLK, (b + 1) * BLK)
        before = dot(weights[:, at], inputs, ((0,), (0,)))
        stash = before.astype(BF16).astype(F32)
        gate = 0.5 * jnp.tanh(0.5 * stash) + 0.5
        act = (stash * gate).astype(BF16)
        hidden[at, :] = act
        slope[at, :] = gate * (1.0 + stash * (1.0 - gate))
        part = dot(w2_ref[:, at], act, ((1,), (0,)))
        acc = part if acc is None else acc + part
    pl.semaphore_wait(known_ring.at[1], 2)
    spread_ring(2)
    eye = lax.broadcasted_iota(jnp.int32, (LEV, LEV), 0) == lax.broadcasted_iota(jnp.int32, (LEV, LEV), 1)
    bias2 = jnp.sum(jnp.where(eye, b2_ref[...], 0.0), axis=1, keepdims=True)
    output = acc + bias2
    total[...] = jnp.zeros((PAD, CELLS), F32)
    for i in range(CX):
        at = slice(CY * i, CY * (i + 1))
        tendency = jnp.where(masks[i], output[:, at], 0.0).astype(BF16).astype(F32)
        goal = jnp.where(masks[i], wanted[:, i, :], 0.0)
        misfit = tendency - goal
        total[0:LEV, at] = misfit * (1.0 / COLUMNS)
        fresh[i, 0:LEV, :] = cells[i, 0:LEV, :] + tendency
        misfits[i, 0:LEV, :] = misfit
    d_out = total[...].astype(BF16)
    ones = jnp.ones((16, CELLS), BF16)
    bias_grad = dot(ones, d_out, ((1,), (1,)))
    spread = lax.broadcasted_iota(jnp.int32, (PAD, CY), 0) == LEV
    per = BLK // CY
    to_sibling = []
    for b in range(HID // BLK):
        at = slice(b * BLK, (b + 1) * BLK)
        d_hidden = dot(w2_ref[:, at], d_out[0:LEV, :], ((0,), (0,)))
        d_before = (d_hidden * slope[at, :]).astype(BF16)
        g1 = dot(inputs, d_before, ((1,), (1,)))
        g2 = dot(d_out, hidden[at, :], ((1,), (1,)))
        for t in range(per):
            lanes = slice(t * CY, (t + 1) * CY)
            tile = b * per + t
            for g in range(3):
                chunks[g % 2, 2 * tile + g // 2] = g1[PAD * g : PAD * (g + 1), lanes]
            last_part = g2[:, lanes]
            if tile == 0:
                row = jnp.concatenate([bias_grad[0:1, :], jnp.zeros((1, CY - PAD), F32)], axis=1)
                last_part = jnp.where(spread, row, last_part)
            chunks[1, 2 * tile + 1] = last_part
        some = pl.ds(2 * per * b, 2 * per)
        copy = remote(chunks.at[1 - core, some], core_in.at[some], core_send.at[b], core_recv.at[b], sibling)
        copy.start()
        to_sibling.append(copy)
    row = lax.broadcasted_iota(jnp.int32, (PAD, CY), 0)
    bias_row = 3 * LEV - 2 * PAD + core * (LEV - (3 * LEV - 2 * PAD))
    for b in range(HID // BLK):
        to_sibling[b].wait_recv()
        some = pl.ds(2 * per * b, 2 * per)
        both = chunks[core, some] + core_in[some]
        for j in range(2 * per):
            value = both[j]
            sent = value
            if j % 2:
                low = value - value.astype(BF16).astype(F32)
                sent = jnp.where(row == bias_row + 1, pltpu.roll(low, 1, 0), value)
            sending[2 * per * b + j] = sent.astype(BF16)

    pl.semaphore_wait(known_tiles.at[3], 2)

    for n, (dx, dy) in enumerate(STEPS_XY):
        c, target = other_chip(dx, dy)
        remote(sending.at[c], landed.at[n], send_sems.at[0], recv_sems.at[0], target).start()
    for i in range(CX):
        tracer_out[:, i, :] = fresh[i, 0:LEV, :]
        wanted[:, i, :] = misfits[i, 0:LEV, :]
    misfit_out[...] = wanted[...].astype(BF16)
    has_bias = lax.rem(chip, 2) == 1
    amount = chunks[core, chip] + core_in[chip]
    amount = jnp.where(jnp.logical_and(row == bias_row + 1, has_bias), 0.0, amount)
    whole(landed, 0).wait_recv()
    for k in range(CHIPS - 1):
        amount = amount + landed[k].astype(F32)
    mine[...] = amount
    part = PAD // NZ
    for k in range(NZ):
        strips[k] = mine[part * k : part * (k + 1), :]

    pl.semaphore_wait(known_ring.at[2], 2)
    for n, k in enumerate(STEPS_Z):
        w, target = ring(k)
        remote(strips.at[w], strips_in.at[n], send_sems.at[1], recv_sems.at[1], target).start()
    whole(strips_in, 1).wait_recv()
    strip = strips[z]
    for n in range(NZ - 1):
        strip = strip + strips_in[n]
    strips_all[z] = strip
    for k in STEPS_Z:
        _, target = ring(k)
        remote(strips_all.at[z], strips_all.at[z], send_sems.at[2], recv_sems.at[2], target).start()
    whole(strips_in, 2).wait_recv()
    for k in range(NZ):
        mine[part * k : part * (k + 1), :] = strips_all[k]
    value = mine[...]
    both = jnp.where(jnp.logical_and(row == bias_row, has_bias), pltpu.roll(value, PAD - 1, 0), 0.0) + value
    low = both - both.astype(BF16).astype(F32)
    both = jnp.where(jnp.logical_and(row == bias_row + 1, has_bias), pltpu.roll(low, 1, 0), both)
    chunk[...] = both.astype(BF16)
    gathered[core, 0] = chunk[...]
    forwards = []
    for dx in (2, 1, 3, 0):
        for dy in (2, 1, 3, 0):
            if dx or dy:
                _, target = other_chip(dx, dy)
                slot = gathered.at[core, 4 * dx + dy]
                remote(chunk, slot, gather_send.at[dx], gather_recv.at[dx], target).start()
    for dx in (2, 1, 3, 0):
        some = gathered.at[core, 4 * dx + (dx == 0) : 4 * dx + 4]
        remote(some, some, gather_send.at[dx], gather_recv.at[dx], sibling).wait_recv()
        some = gathered.at[core, 4 * dx : 4 * dx + 4]
        forwards.append(remote(some, some, forward_send.at[dx], forward_recv.at[dx], sibling))
        forwards[-1].start()

    def unpack(half):
        rest = 3 * LEV - 2 * PAD
        y = lax.div(m, 2)
        for t in range(HID // CY):
            lanes = slice(t * CY, (t + 1) * CY)
            from_x = lax.rem(x + 4 - t // 2, 4) * 4
            first = from_x + lax.rem(y + 4 - 2 * (t % 2), 4)
            second = from_x + lax.rem(y + 3 - 2 * (t % 2), 4)
            w1_out[PAD * half : PAD * (half + 1), lanes] = gathered[half, first].astype(F32)
            value = gathered[half, second].astype(F32)
            if half == 0:
                w1_out[2 * PAD : 3 * LEV, lanes] = value[0:rest, :]
                b1_out[:, lanes] = value[rest : rest + 1, :] + value[rest + 1 : rest + 2, :]
            else:
                w2_out[:, lanes] = value[0:LEV, :]
                if t == 0:
                    b2_out[...] = value[LEV : LEV + 1, 0:LEV] + value[LEV + 1 : LEV + 2, 0:LEV]

    for half in range(2):
        pl.when(core == half)(functools.partial(unpack, half))
    for copy in copies + to_sibling:
        copy.wait_send()
    whole(landed, 0).wait_send()
    whole(strips_in, 1).wait_send()
    whole(strips_in, 2).wait_send()
    for dx in (2, 1, 3, 0):
        some = gathered.at[core, 4 * dx + (dx == 0) : 4 * dx + 4]
        remote(some, some, gather_send.at[dx], gather_recv.at[dx], sibling).wait_send()
    for forward in forwards:
        forward.wait()
    for half in range(2):
        pl.when(core != half)(functools.partial(unpack, half))


def main(*operands):
    vmem = pl.BlockSpec(memory_space=pltpu.VMEM)
    hbm = pl.BlockSpec(memory_space=pltpu.HBM)
    part = PAD // NZ
    halves = HID // BLK
    return pl.pallas_call(
        main_kernel,
        out_shape=(
            jax.ShapeDtypeStruct((LEV, CX, CY), F32),
            jax.ShapeDtypeStruct((LEV, CX, CY), BF16),
            jax.ShapeDtypeStruct((3 * LEV, HID), F32),
            jax.ShapeDtypeStruct((1, HID), F32),
            jax.ShapeDtypeStruct((LEV, HID), F32),
            jax.ShapeDtypeStruct((1, LEV), F32),
        ),
        in_specs=[hbm] * 9,
        out_specs=(vmem,) * 6,
        scratch_shapes=[pltpu.VMEM(a.shape, a.dtype) for a in operands]
        + [
            pltpu.VMEM((CX, PAD, CY), F32),
            pltpu.VMEM((CX, PAD, CY), F32),
            pltpu.VMEM((CX, PAD, CY), F32),
            pltpu.VMEM((3 * CX, PAD, CY), BF16),
            pltpu.VMEM((2 * EDGE, CY), BF16),
            pltpu.VMEM((8, PAD, CY), BF16),
            pltpu.VMEM((7, PAD, CY), BF16),
            pltpu.VMEM((2 * EDGE, CY), BF16),
            pltpu.VMEM((2 * EDGE, 3 * CX * CY), BF16),
            pltpu.VMEM((WIDE * CY, CY), BF16),
            pltpu.VMEM((2 * EDGE, 3 * CY), BF16),
            pltpu.VMEM((CX, PAD, CY), F32),
            pltpu.VMEM((CX, PAD, CY), F32),
            pltpu.VMEM((2, CHIPS, PAD, CY), BF16),
            pltpu.VMEM((ROWS, CELLS), F32),
            pltpu.VMEM((ROWS, HID), BF16),
            pltpu.VMEM((HID, CELLS), BF16),
            pltpu.VMEM((HID, CELLS), F32),
            pltpu.VMEM((PAD, CELLS), F32),
            pltpu.VMEM((LEV, CX, CY), F32),
            pltpu.VMEM((2, CHIPS, PAD, CY), F32),
            pltpu.VMEM((CHIPS, PAD, CY), F32),
            pltpu.VMEM((CHIPS, PAD, CY), BF16),
            pltpu.VMEM((CHIPS - 1, PAD, CY), BF16),
            pltpu.VMEM((PAD, CY), F32),
            pltpu.VMEM((NZ, part, CY), F32),
            pltpu.VMEM((NZ - 1, part, CY), F32),
            pltpu.VMEM((NZ, part, CY), F32),
            pltpu.VMEM((PAD, CY), BF16),
            pltpu.SemaphoreType.DMA((len(operands),)),
            pltpu.SemaphoreType.DMA((12,)),
            pltpu.SemaphoreType.DMA((12,)),
            pltpu.SemaphoreType.DMA((halves,)),
            pltpu.SemaphoreType.DMA((halves,)),
            pltpu.SemaphoreType.DMA((3,)),
            pltpu.SemaphoreType.DMA((3,)),
            pltpu.SemaphoreType.DMA((4,)),
            pltpu.SemaphoreType.DMA((4,)),
            pltpu.SemaphoreType.DMA((4,)),
            pltpu.SemaphoreType.DMA((4,)),
            pltpu.SemaphoreType.REGULAR((4,)),
            pltpu.SemaphoreType.REGULAR((3,)),
        ],
        compiler_params=pltpu.CompilerParams(
            collective_id=0, has_side_effects=True, vmem_limit_bytes=VMEM_LIMIT
        ),
        name="main",
    )(*(pltpu.with_memory_space_constraint(a, pltpu.HBM) for a in operands))


def store_kernel(*refs):
    count = len(refs) // 2
    copies = [pltpu.make_async_copy(refs[i], refs[count + i], refs[-1].at[i]) for i in (2, 4, 0, 1, 3, 5)]
    for copy in copies:
        copy.start()
    for copy in copies:
        copy.wait()


def store(*results):
    vmem = pl.BlockSpec(memory_space=pltpu.VMEM)
    hbm = pl.BlockSpec(memory_space=pltpu.HBM)
    return pl.pallas_call(
        store_kernel,
        out_shape=tuple(jax.ShapeDtypeStruct(a.shape, a.dtype) for a in results),
        in_specs=[vmem] * len(results),
        out_specs=(hbm,) * len(results),
        scratch_shapes=[pltpu.SemaphoreType.DMA((len(results),))],
        compiler_params=pltpu.CompilerParams(vmem_limit_bytes=16 * 1024 * 1024),
        name="store",
    )(*results)


def on_device(tracer, east, north, target, depth, slots, w1, b1, w2, b2):
    results = main(tracer, east, north, target, depth, w1, b1.reshape(1, HID), w2.T, b2.reshape(1, LEV))
    tracer_out, misfit_out, grad_w1, grad_b1, grad_w2, grad_b2 = store(*results)
    return tracer_out, misfit_out, grad_w1, grad_b1.reshape(HID), grad_w2.T, grad_b2.reshape(LEV)


def solution(mesh):
    grid = P(None, "ocx", ("ocy", "ml"))
    return jax.shard_map(
        on_device,
        mesh=mesh,
        in_specs=(grid, grid, grid, grid, P("ocx", ("ocy", "ml")), P("ocx", ("ocy", "ml"), None, None), P(), P(), P(), P()),
        out_specs=(grid, grid, P(), P(), P(), P()),
        check_vma=False,
    )
```

```python
import functools

import jax
import jax.numpy as jnp
from jax import lax
from jax.experimental import pallas as pl
from jax.experimental.pallas import tpu as pltpu
from jax.sharding import PartitionSpec as P

MESH = pl.DeviceIdType.MESH
KAPPA = 0.1
STEPS = 3
LEV = 75
PAD = 80
CX = 4
CY = 128
CELLS = CX * CY
HID = 1024
ROWS = 240
TILES = 32
NZ = 16
CHIPS = 16
COLUMNS = 262144
REACH = 3
WIDE = CX + 2 * REACH
STRIP = 4 * REACH
LATS = 16 * 3
CORNER = 16
EDGE = LATS + 2 * CORNER
NORTH_AT = (0, 1, 10, 11)
EAST_AT = (2, 6, 8, 9)
CELL_AT = (3, 4, 5, 7)
BLK = 256
STEPS_XY = (
    (2, 2), (2, 1), (2, 3), (1, 2), (3, 2), (1, 1), (1, 3), (3, 1), (3, 3), (2, 0), (0, 2), (1, 0), (3, 0), (0, 1), (0, 3)
)
STEPS_Z = (8, 7, 9, 6, 10, 5, 11, 4, 12, 3, 13, 2, 14, 1, 15)
F32 = jnp.float32
BF16 = jnp.bfloat16
VMEM_LIMIT = 40 * 1024 * 1024


def place(p):
    return lax.div(p, 8), lax.rem(p, 8)


def faces(opened, speed):
    near = jnp.where(opened, jnp.maximum(speed, 0.0) + KAPPA, 0.0)
    far = jnp.where(opened, jnp.minimum(speed, 0.0) - KAPPA, 0.0)
    return near, far


def dot(a, b, dims):
    return lax.dot_general(a, b, (dims, ((), ())), preferred_element_type=F32)


def main_kernel(
    tracer_hbm, east_hbm, north_hbm, target_hbm, depth_hbm, w1_hbm, b1_hbm, w2_hbm, b2_hbm,
    tracer_out, misfit_out, w1_out, b1_out, w2_out, b2_out,
    tracer_ref, east_ref, north_ref, target_ref, depth_ref, w1_ref, b1_ref, w2_ref, b2_ref,
    cells, north_own, east_own, rows_out, edges_out, halo_w, halo_e, halo_edges, pick_out, pick_rows, pick_edges,
    staged, fresh, misfits, gathered, feat, weights, hidden, slope, total, wanted, chunks, core_in, sending, landed,
    mine, strips, strips_in, strips_all, chunk,
    load_sems, halo_send, halo_recv, core_send, core_recv, send_sems, recv_sems,
    gather_send, gather_recv, forward_send, forward_recv, known_tiles, known_ring,
):
    z, x, m = lax.axis_index("ocx"), lax.axis_index("ocy"), lax.axis_index("ml")
    core = lax.rem(m, 2)
    chip = x * 4 + lax.div(m, 2)
    p = x * 8 + m
    sibling = (z, x, m + 1 - 2 * core)

    def other_chip(dx, dy):
        to_x, to_m = lax.rem(x + dx, 4), lax.rem(m + 2 * dy, 8)
        return to_x * 4 + lax.div(to_m, 2), (z, to_x, to_m)

    def ring(k):
        w = lax.rem(z + k, NZ)
        return w, (w, x, m)

    def tile(k):
        return (z, *place(lax.rem(p + k, TILES)))

    to_e, to_w = ring(1)[1], ring(NZ - 1)[1]
    to_n, to_s = tile(1), tile(TILES - 1)

    pairs = (
        (depth_hbm, depth_ref), (tracer_hbm, tracer_ref.at[0:LEV]), (north_hbm, north_ref.at[0:LEV]), (east_hbm, east_ref.at[0:LEV]),
        (target_hbm, target_ref), (w1_hbm, w1_ref), (b1_hbm, b1_ref), (w2_hbm, w2_ref), (b2_hbm, b2_ref),
    )
    loads = [pltpu.make_async_copy(src, dst, load_sems.at[i]) for i, (src, dst) in enumerate(pairs)]
    for load in loads[:4]:
        load.start()

    barrier = pltpu.get_barrier_semaphore()

    def signal(target):
        pl.semaphore_signal(barrier, inc=1, device_id=target, device_id_type=MESH)

    def diagonal(dz, k):
        return (lax.rem(z + dz, NZ), *tile(k)[1:])

    to_ne, to_nw = diagonal(1, 1), diagonal(NZ - 1, 1)
    to_se, to_sw = diagonal(1, TILES - 1), diagonal(NZ - 1, TILES - 1)
    for target in (to_e, to_w, to_n, to_s, to_ne, to_nw, to_se, to_sw):
        signal(target)
    for load in loads[4:]:
        load.start()

    def spread_word(known, number, ahead, behind):
        for target in (ahead, behind):
            pl.semaphore_signal(known.at[number], inc=1, device_id=target, device_id_type=MESH)

    def spread_tiles(number):
        spread_word(known_tiles, number, tile(1 << number), tile(TILES - (1 << number)))

    def spread_ring(number):
        spread_word(known_ring, number, ring(1 << number)[1], ring(NZ - (1 << number))[1])

    def remote(src, dst, send_sem, recv_sem, target):
        return pltpu.make_async_remote_copy(
            src_ref=src, dst_ref=dst, send_sem=send_sem, recv_sem=recv_sem,
            device_id=target, device_id_type=MESH,
        )

    def whole(ref, number):
        return remote(ref, ref, send_sems.at[number], recv_sems.at[number], sibling)

    def halo(src, dst, number, target):
        copy = remote(src, dst, halo_send.at[number], halo_recv.at[number], target)
        copy.start()
        return copy

    item = lax.broadcasted_iota(jnp.int32, (2 * EDGE, CY), 0)
    lane_in = lax.broadcasted_iota(jnp.int32, (2 * EDGE, CY), 1)
    southern = item >= EDGE
    item = jnp.where(southern, item - EDGE, item)
    nth = jnp.where(southern, lane_in, lane_in - (CY - REACH))
    key = jnp.where(jnp.logical_and(nth >= 0, nth < REACH), item - nth, -999)
    nth = jnp.where(southern, nth, nth - 1)
    corner_key = jnp.where(jnp.logical_and(nth >= 0, nth < 2), item - nth, -999)
    for f, order in enumerate((CELL_AT, EAST_AT, NORTH_AT)):
        for i in range(CX):
            at = slice(CY * order[i], CY * (order[i] + 1))
            first = LATS + 4 * f + (2 * (i - 2) if i >= 2 else CORNER + 2 * i)
            hit = jnp.logical_or(key == 16 * f + 4 * i, corner_key == first)
            pick_out[:, at] = jnp.where(hit, 1.0, 0.0).astype(BF16)

    level = lax.broadcasted_iota(jnp.int32, (PAD, CY), 0).astype(F32)
    lane = lax.broadcasted_iota(jnp.int32, (PAD, CY), 1)
    tail = lax.broadcasted_iota(jnp.int32, (PAD - LEV, CY), 0)
    none = jnp.zeros((PAD - LEV, CY), F32)
    for load in loads[:4]:
        load.wait()
    depth = [depth_ref[i : i + 1, :].astype(F32) for i in range(CX)]
    for i in range(CX):
        cells[i, 0:LEV, :] = tracer_ref[0:LEV, i, :]
        cells[i, LEV:PAD, :] = jnp.where(tail == 0, depth[i], 0.0)
        north_own[i, 0:LEV, :] = north_ref[0:LEV, i, :]
        north_own[i, LEV:PAD, :] = none
        east_own[i, 0:LEV, :] = east_ref[0:LEV, i, :]
        east_own[i, LEV:PAD, :] = none
        rows_out[CELL_AT[i]] = cells[i].astype(BF16)
        rows_out[EAST_AT[i]] = east_own[i].astype(BF16)
        rows_out[NORTH_AT[i]] = north_own[i].astype(BF16)
    pl.semaphore_wait(barrier, 8)
    copies = [halo(rows_out.at[4:12], halo_w, 0, to_e), halo(rows_out.at[0:7], halo_e, 1, to_w)]
    spread_tiles(0)
    spread_ring(0)
    sources = jnp.concatenate([rows_out[n] for n in range(3 * CX)], axis=1)
    sources = jnp.concatenate([sources, jnp.zeros((CY - PAD, 3 * CX * CY), BF16)], axis=0)
    edges_out[...] = dot(pick_out[...], sources, ((1,), (1,))).astype(BF16)
    to_east, to_west = slice(LATS, LATS + CORNER), slice(LATS + CORNER, EDGE)
    for side, targets in enumerate(((to_n, to_ne, to_nw), (to_s, to_se, to_sw))):
        for n, some in enumerate((slice(0, LATS), to_east, to_west)):
            mine_at = edges_out.at[EDGE * side + some.start : EDGE * side + some.stop]
            there_at = halo_edges.at[EDGE * side + some.start : EDGE * side + some.stop]
            copies.append(halo(mine_at, there_at, 2 + 3 * side + n, targets[n]))

    lane_in = lax.broadcasted_iota(jnp.int32, (CY, CY), 0)
    lane_out = lax.broadcasted_iota(jnp.int32, (CY, CY), 1)
    shift = jnp.where(lane_in >= CY - REACH, lane_out - 2 * (lane_in - (CY - REACH)) + REACH, -999)
    shift = jnp.where(lane_in < REACH, lane_out - 2 * (lane_in + REACH), shift)
    shift = jnp.where(shift >= CY, shift - CY, shift)
    for n in range(WIDE):
        pick_rows[CY * n : CY * (n + 1), :] = jnp.where(shift == STRIP * n, 1.0, 0.0).astype(BF16)
    item = lax.broadcasted_iota(jnp.int32, (LATS, 3 * CY), 0)
    lane_out = lax.broadcasted_iota(jnp.int32, (LATS, 3 * CY), 1)
    shift = lane_out - (CY * (item // 16) + STRIP * (REACH + (item // 4) % 4) + 2 * (item % 4))
    shift = jnp.where(item % 4 < REACH, shift, -999)
    pick_edges[0:LATS, :] = jnp.where(shift == 0, 1.0, 0.0).astype(BF16)
    pick_edges[EDGE : EDGE + LATS, :] = jnp.where(shift == REACH, 1.0, 0.0).astype(BF16)
    item = lax.broadcasted_iota(jnp.int32, (CORNER, 3 * CY), 0)
    lane_out = lax.broadcasted_iota(jnp.int32, (CORNER, 3 * CY), 1)
    shift = lane_out - (CY * (item // 4) + STRIP * ((item // 2) % 2) + 2 * (item % 2))
    shift = jnp.where(item < 12, shift, -999)
    for n, (first, beside) in enumerate(((1, 2), (WIDE - REACH, 2), (1, REACH), (WIDE - REACH, REACH))):
        at = EDGE * (n // 2) + LATS + CORNER * (n % 2)
        pick_edges[at : at + CORNER, :] = jnp.where(shift == STRIP * first + beside, 1.0, 0.0).astype(BF16)

    masks = [level[0:LEV, :] < depth[i] for i in range(CX)]
    for i in range(CX):
        at = slice(CY * i, CY * (i + 1))
        feat[LEV : 2 * LEV, at] = jnp.where(masks[i], east_own[i, 0:LEV, :], 0.0)
        feat[2 * LEV : 3 * LEV, at] = jnp.where(masks[i], north_own[i, 0:LEV, :], 0.0)
    last = lax.broadcasted_iota(jnp.int32, (ROWS - 3 * LEV, CELLS), 0)
    feat[3 * LEV : ROWS, :] = jnp.where(last < 2, 1.0, 0.0)
    pl.semaphore_wait(known_tiles.at[0], 2)
    spread_tiles(1)
    pl.semaphore_wait(known_ring.at[0], 2)
    spread_ring(1)
    for load in loads[4:]:
        load.wait()
    wanted[0:LEV] = target_ref[...].astype(F32)
    edge = 3 * LEV // 16 * 16
    weights[0:edge, :] = w1_ref[0:edge, :]
    bias = b1_ref[...]
    coarse = bias.astype(BF16).astype(F32)
    row = lax.broadcasted_iota(jnp.int32, (ROWS - edge, HID), 0) + edge
    final = jnp.where(row == 3 * LEV - 1, w1_ref[3 * LEV - 1 : 3 * LEV, :].astype(F32), 0.0)
    final = jnp.where(row == 3 * LEV, coarse, final)
    final = jnp.where(row == 3 * LEV + 1, bias - coarse, final)
    weights[edge:ROWS, :] = final.astype(BF16)

    pl.semaphore_wait(known_tiles.at[1], 2)
    spread_tiles(2)
    for copy in copies:
        copy.wait_recv()

    cell_rows = [halo_w[0], halo_w[1], halo_w[3]] + [rows_out[n] for n in CELL_AT] + [halo_e[3], halo_e[4], halo_e[5]]
    east_rows = [halo_w[2], halo_w[4], halo_w[5]] + [rows_out[n] for n in EAST_AT] + [halo_e[2], halo_e[6]]
    north_rows = [halo_w[6], halo_w[7]] + [rows_out[n] for n in NORTH_AT] + [halo_e[0], halo_e[1]]
    beyond = dot(halo_edges[...], pick_edges[...], ((0,), (0,)))[0:PAD, :]

    def strip_of(some, first, f):
        own = dot(
            jnp.concatenate(some, axis=1), pick_rows[CY * first : CY * (first + len(some)), :], ((1,), (0,))
        )
        return own + beyond[:, CY * f : CY * (f + 1)]

    def turn(value, by):
        by = by % CY
        return pltpu.roll(value, by, 1) if by else value

    strip = strip_of(cell_rows, 0, 0)
    deep_here = jnp.broadcast_to(strip[LEV : LEV + 1, :], (PAD, CY))
    near_e, far_e = faces(level < jnp.minimum(deep_here, turn(deep_here, -STRIP)), strip_of(east_rows, 0, 1))
    at_south = jnp.logical_and(lane % STRIP == 2 * (REACH - 1), p == 0)
    at_north = jnp.logical_and(lane % STRIP == 2 * (REACH - 1) - REACH, p == TILES - 1)
    shut = jnp.logical_or(at_south, at_north)
    opened = jnp.logical_and(level < jnp.minimum(deep_here, turn(deep_here, -2)), jnp.logical_not(shut))
    strip_near, strip_far = faces(opened, strip_of(north_rows, 1, 2))
    near_w, far_w = turn(near_e, STRIP), turn(far_e, STRIP)
    near_s, far_s = turn(strip_near, 2), turn(strip_far, 2)
    strip_coef = (1.0 + far_w - near_e + far_s - strip_near, near_w, far_e, near_s, strip_far)
    strips_at = [strip]
    for step in range(STEPS - 1):
        keep, near_w, far_e, near_s, far_n = strip_coef
        strip = (
            keep * strip + near_w * turn(strip, STRIP) - far_e * turn(strip, -STRIP)
            + near_s * turn(strip, 2) - far_n * turn(strip, -2)
        )
        strips_at.append(strip)

    now = [
        cells[n - REACH] if REACH <= n < REACH + CX else cell_rows[n].astype(F32) for n in range(WIDE)
    ]
    deep = [jnp.broadcast_to(value[LEV : LEV + 1, :], (PAD, CY)) for value in now]
    east_faces = []
    for n in range(WIDE - 1):
        speed = east_own[n - REACH] if REACH <= n < REACH + CX else east_rows[n].astype(F32)
        east_faces.append(faces(level < jnp.minimum(deep[n], deep[n + 1]), speed))
    coef = [None] * WIDE
    for n in range(1, WIDE - 1):
        speed = north_own[n - REACH] if REACH <= n < REACH + CX else north_rows[n - 1].astype(F32)
        near_n, far_n = faces(level < jnp.minimum(deep[n], turn(deep[n], -1)), speed)
        edge_at = -(STRIP * n + 2)
        near_n = jnp.where(lane == CY - 1, turn(strip_near, edge_at), near_n)
        far_n = jnp.where(lane == CY - 1, turn(strip_far, edge_at), far_n)
        beyond_at = -(STRIP * n + 2 * (REACH - 1))
        near_s = jnp.where(lane == 0, turn(strip_near, beyond_at), turn(near_n, 1))
        far_s = jnp.where(lane == 0, turn(strip_far, beyond_at), turn(far_n, 1))
        near_w, far_w = east_faces[n - 1]
        near_e, far_e = east_faces[n]
        coef[n] = (1.0 + far_w - near_e + far_s - near_n, near_w, far_e, near_s, far_n)
    for step in range(STEPS):
        after = list(now)
        for n in range(step + 1, WIDE - 1 - step):
            keep, near_w, far_e, near_s, far_n = coef[n]
            past = turn(strips_at[step], -(STRIP * n + 2 * (REACH - 1)))
            south = jnp.where(lane == 0, past, turn(now[n], 1))
            north = jnp.where(lane == CY - 1, past, turn(now[n], -1))
            after[n] = (
                keep * now[n] + near_w * now[n - 1] - far_e * now[n + 1] + near_s * south - far_n * north
            )
        now = after
    for i in range(CX):
        cells[i] = now[REACH + i]
    pl.semaphore_wait(known_tiles.at[2], 2)
    spread_tiles(3)
    for i in range(CX):
        at = slice(CY * i, CY * (i + 1))
        feat[0:LEV, at] = jnp.where(masks[i], cells[i, 0:LEV, :], 0.0)
    inputs = feat[...].astype(BF16)

    acc = None
    for b in range(HID // BLK):
        at = slice(b * BLK, (b + 1) * BLK)
        before = dot(weights[:, at], inputs, ((0,), (0,)))
        stash = before.astype(BF16).astype(F32)
        gate = 0.5 * jnp.tanh(0.5 * stash) + 0.5
        act = (stash * gate).astype(BF16)
        hidden[at, :] = act
        slope[at, :] = gate * (1.0 + stash * (1.0 - gate))
        part = dot(w2_ref[:, at], act, ((1,), (0,)))
        acc = part if acc is None else acc + part
    pl.semaphore_wait(known_ring.at[1], 2)
    spread_ring(2)
    eye = lax.broadcasted_iota(jnp.int32, (LEV, LEV), 0) == lax.broadcasted_iota(jnp.int32, (LEV, LEV), 1)
    bias2 = jnp.sum(jnp.where(eye, b2_ref[...], 0.0), axis=1, keepdims=True)
    output = acc + bias2
    total[...] = jnp.zeros((PAD, CELLS), F32)
    for i in range(CX):
        at = slice(CY * i, CY * (i + 1))
        tendency = jnp.where(masks[i], output[:, at], 0.0).astype(BF16).astype(F32)
        goal = jnp.where(masks[i], wanted[0:LEV, i, :], 0.0)
        misfit = tendency - goal
        total[0:LEV, at] = misfit * (1.0 / COLUMNS)
        fresh[i, 0:LEV, :] = cells[i, 0:LEV, :] + tendency
        misfits[i, 0:LEV, :] = misfit
    d_out = total[...].astype(BF16)
    ones = jnp.ones((16, CELLS), BF16)
    bias_grad = dot(ones, d_out, ((1,), (1,)))
    spread = lax.broadcasted_iota(jnp.int32, (PAD, CY), 0) == LEV
    per = BLK // CY
    to_sibling = []
    for b in range(HID // BLK):
        at = slice(b * BLK, (b + 1) * BLK)
        d_hidden = dot(w2_ref[:, at], d_out[0:LEV, :], ((0,), (0,)))
        d_before = (d_hidden * slope[at, :]).astype(BF16)
        g1 = dot(inputs, d_before, ((1,), (1,)))
        g2 = dot(d_out, hidden[at, :], ((1,), (1,)))
        for t in range(per):
            lanes = slice(t * CY, (t + 1) * CY)
            tile = b * per + t
            for g in range(3):
                chunks[g % 2, 2 * tile + g // 2] = g1[PAD * g : PAD * (g + 1), lanes]
            last_part = g2[:, lanes]
            if tile == 0:
                row = jnp.concatenate([bias_grad[0:1, :], jnp.zeros((1, CY - PAD), F32)], axis=1)
                last_part = jnp.where(spread, row, last_part)
            chunks[1, 2 * tile + 1] = last_part
        some = pl.ds(2 * per * b, 2 * per)
        copy = remote(chunks.at[1 - core, some], core_in.at[some], core_send.at[b], core_recv.at[b], sibling)
        copy.start()
        to_sibling.append(copy)
    row = lax.broadcasted_iota(jnp.int32, (PAD, CY), 0)
    bias_row = 3 * LEV - 2 * PAD + core * (LEV - (3 * LEV - 2 * PAD))
    for b in range(HID // BLK):
        to_sibling[b].wait_recv()
        some = pl.ds(2 * per * b, 2 * per)
        both = chunks[core, some] + core_in[some]
        for j in range(2 * per):
            value = both[j]
            sent = value
            if j % 2:
                low = value - value.astype(BF16).astype(F32)
                sent = jnp.where(row == bias_row + 1, pltpu.roll(low, 1, 0), value)
            sending[2 * per * b + j] = sent.astype(BF16)

    pl.semaphore_wait(known_tiles.at[3], 2)

    for n, (dx, dy) in enumerate(STEPS_XY):
        c, target = other_chip(dx, dy)
        remote(sending.at[c], landed.at[n], send_sems.at[0], recv_sems.at[0], target).start()
    for i in range(CX):
        staged[0:LEV, i, :] = fresh[i, 0:LEV, :]
        wanted[0:LEV, i, :] = misfits[i, 0:LEV, :]
    tracer_out[...] = staged[0:LEV]
    misfit_out[...] = wanted[0:LEV].astype(BF16)
    has_bias = lax.rem(chip, 2) == 1
    amount = chunks[core, chip] + core_in[chip]
    amount = jnp.where(jnp.logical_and(row == bias_row + 1, has_bias), 0.0, amount)
    whole(landed, 0).wait_recv()
    for k in range(CHIPS - 1):
        amount = amount + landed[k].astype(F32)
    mine[...] = amount
    part = PAD // NZ
    for k in range(NZ):
        strips[k] = mine[part * k : part * (k + 1), :]

    pl.semaphore_wait(known_ring.at[2], 2)
    for n, k in enumerate(STEPS_Z):
        w, target = ring(k)
        remote(strips.at[w], strips_in.at[n], send_sems.at[1], recv_sems.at[1], target).start()
    whole(strips_in, 1).wait_recv()
    strip = strips[z]
    for n in range(NZ - 1):
        strip = strip + strips_in[n]
    strips_all[z] = strip
    for k in STEPS_Z:
        _, target = ring(k)
        remote(strips_all.at[z], strips_all.at[z], send_sems.at[2], recv_sems.at[2], target).start()
    whole(strips_in, 2).wait_recv()
    for k in range(NZ):
        mine[part * k : part * (k + 1), :] = strips_all[k]
    value = mine[...]
    both = jnp.where(jnp.logical_and(row == bias_row, has_bias), pltpu.roll(value, PAD - 1, 0), 0.0) + value
    low = both - both.astype(BF16).astype(F32)
    both = jnp.where(jnp.logical_and(row == bias_row + 1, has_bias), pltpu.roll(low, 1, 0), both)
    chunk[...] = both.astype(BF16)
    gathered[core, 0] = chunk[...]
    forwards = []
    for dx in (2, 1, 3, 0):
        for dy in (2, 1, 3, 0):
            if dx or dy:
                _, target = other_chip(dx, dy)
                slot = gathered.at[core, 4 * dx + dy]
                remote(chunk, slot, gather_send.at[dx], gather_recv.at[dx], target).start()
    for dx in (2, 1, 3, 0):
        some = gathered.at[core, 4 * dx + (dx == 0) : 4 * dx + 4]
        remote(some, some, gather_send.at[dx], gather_recv.at[dx], sibling).wait_recv()
        some = gathered.at[core, 4 * dx : 4 * dx + 4]
        forwards.append(remote(some, some, forward_send.at[dx], forward_recv.at[dx], sibling))
        forwards[-1].start()

    def unpack(half):
        rest = 3 * LEV - 2 * PAD
        y = lax.div(m, 2)
        for t in range(HID // CY):
            lanes = slice(t * CY, (t + 1) * CY)
            from_x = lax.rem(x + 4 - t // 2, 4) * 4
            first = from_x + lax.rem(y + 4 - 2 * (t % 2), 4)
            second = from_x + lax.rem(y + 3 - 2 * (t % 2), 4)
            w1_out[PAD * half : PAD * (half + 1), lanes] = gathered[half, first].astype(F32)
            value = gathered[half, second].astype(F32)
            if half == 0:
                w1_out[2 * PAD : 3 * LEV, lanes] = value[0:rest, :]
                b1_out[:, lanes] = value[rest : rest + 1, :] + value[rest + 1 : rest + 2, :]
            else:
                w2_out[:, lanes] = value[0:LEV, :]
                if t == 0:
                    b2_out[...] = value[LEV : LEV + 1, 0:LEV] + value[LEV + 1 : LEV + 2, 0:LEV]

    for half in range(2):
        pl.when(core == half)(functools.partial(unpack, half))
    for copy in copies + to_sibling:
        copy.wait_send()
    whole(landed, 0).wait_send()
    whole(strips_in, 1).wait_send()
    whole(strips_in, 2).wait_send()
    for dx in (2, 1, 3, 0):
        some = gathered.at[core, 4 * dx + (dx == 0) : 4 * dx + 4]
        remote(some, some, gather_send.at[dx], gather_recv.at[dx], sibling).wait_send()
    for forward in forwards:
        forward.wait()
    for half in range(2):
        pl.when(core != half)(functools.partial(unpack, half))


def main(*operands):
    vmem = pl.BlockSpec(memory_space=pltpu.VMEM)
    hbm = pl.BlockSpec(memory_space=pltpu.HBM)
    part = PAD // NZ
    halves = HID // BLK
    return pl.pallas_call(
        main_kernel,
        out_shape=(
            jax.ShapeDtypeStruct((LEV, CX, CY), F32),
            jax.ShapeDtypeStruct((LEV, CX, CY), BF16),
            jax.ShapeDtypeStruct((3 * LEV, HID), F32),
            jax.ShapeDtypeStruct((1, HID), F32),
            jax.ShapeDtypeStruct((LEV, HID), F32),
            jax.ShapeDtypeStruct((1, LEV), F32),
        ),
        in_specs=[hbm] * 9,
        out_specs=(vmem,) * 6,
        scratch_shapes=[pltpu.VMEM((PAD, CX, CY), F32)] * 3
        + [pltpu.VMEM(a.shape, a.dtype) for a in operands[3:]]
        + [
            pltpu.VMEM((CX, PAD, CY), F32),
            pltpu.VMEM((CX, PAD, CY), F32),
            pltpu.VMEM((CX, PAD, CY), F32),
            pltpu.VMEM((3 * CX, PAD, CY), BF16),
            pltpu.VMEM((2 * EDGE, CY), BF16),
            pltpu.VMEM((8, PAD, CY), BF16),
            pltpu.VMEM((7, PAD, CY), BF16),
            pltpu.VMEM((2 * EDGE, CY), BF16),
            pltpu.VMEM((2 * EDGE, 3 * CX * CY), BF16),
            pltpu.VMEM((WIDE * CY, CY), BF16),
            pltpu.VMEM((2 * EDGE, 3 * CY), BF16),
            pltpu.VMEM((PAD, CX, CY), F32),
            pltpu.VMEM((CX, PAD, CY), F32),
            pltpu.VMEM((CX, PAD, CY), F32),
            pltpu.VMEM((2, CHIPS, PAD, CY), BF16),
            pltpu.VMEM((ROWS, CELLS), F32),
            pltpu.VMEM((ROWS, HID), BF16),
            pltpu.VMEM((HID, CELLS), BF16),
            pltpu.VMEM((HID, CELLS), F32),
            pltpu.VMEM((PAD, CELLS), F32),
            pltpu.VMEM((PAD, CX, CY), F32),
            pltpu.VMEM((2, CHIPS, PAD, CY), F32),
            pltpu.VMEM((CHIPS, PAD, CY), F32),
            pltpu.VMEM((CHIPS, PAD, CY), BF16),
            pltpu.VMEM((CHIPS - 1, PAD, CY), BF16),
            pltpu.VMEM((PAD, CY), F32),
            pltpu.VMEM((NZ, part, CY), F32),
            pltpu.VMEM((NZ - 1, part, CY), F32),
            pltpu.VMEM((NZ, part, CY), F32),
            pltpu.VMEM((PAD, CY), BF16),
            pltpu.SemaphoreType.DMA((len(operands),)),
            pltpu.SemaphoreType.DMA((8,)),
            pltpu.SemaphoreType.DMA((8,)),
            pltpu.SemaphoreType.DMA((halves,)),
            pltpu.SemaphoreType.DMA((halves,)),
            pltpu.SemaphoreType.DMA((3,)),
            pltpu.SemaphoreType.DMA((3,)),
            pltpu.SemaphoreType.DMA((4,)),
            pltpu.SemaphoreType.DMA((4,)),
            pltpu.SemaphoreType.DMA((4,)),
            pltpu.SemaphoreType.DMA((4,)),
            pltpu.SemaphoreType.REGULAR((4,)),
            pltpu.SemaphoreType.REGULAR((3,)),
        ],
        compiler_params=pltpu.CompilerParams(
            collective_id=0, has_side_effects=True, vmem_limit_bytes=VMEM_LIMIT
        ),
        name="main",
    )(*(pltpu.with_memory_space_constraint(a, pltpu.HBM) for a in operands))


def store_kernel(*refs):
    count = len(refs) // 2
    copies = [pltpu.make_async_copy(refs[i], refs[count + i], refs[-1].at[i]) for i in (2, 4, 0, 1, 3, 5)]
    for copy in copies:
        copy.start()
    for copy in copies:
        copy.wait()


def store(*results):
    vmem = pl.BlockSpec(memory_space=pltpu.VMEM)
    hbm = pl.BlockSpec(memory_space=pltpu.HBM)
    return pl.pallas_call(
        store_kernel,
        out_shape=tuple(jax.ShapeDtypeStruct(a.shape, a.dtype) for a in results),
        in_specs=[vmem] * len(results),
        out_specs=(hbm,) * len(results),
        scratch_shapes=[pltpu.SemaphoreType.DMA((len(results),))],
        compiler_params=pltpu.CompilerParams(vmem_limit_bytes=16 * 1024 * 1024),
        name="store",
    )(*results)


def on_device(tracer, east, north, target, depth, slots, w1, b1, w2, b2):
    results = main(tracer, east, north, target, depth, w1, b1.reshape(1, HID), w2.T, b2.reshape(1, LEV))
    tracer_out, misfit_out, grad_w1, grad_b1, grad_w2, grad_b2 = store(*results)
    return tracer_out, misfit_out, grad_w1, grad_b1.reshape(HID), grad_w2.T, grad_b2.reshape(LEV)


def solution(mesh):
    grid = P(None, "ocx", ("ocy", "ml"))
    return jax.shard_map(
        on_device,
        mesh=mesh,
        in_specs=(grid, grid, grid, grid, P("ocx", ("ocy", "ml")), P("ocx", ("ocy", "ml"), None, None), P(), P(), P(), P()),
        out_specs=(grid, grid, P(), P(), P(), P()),
        check_vma=False,
    )
```

```python
import functools

import jax
import jax.numpy as jnp
from jax import lax
from jax.experimental import pallas as pl
from jax.experimental.pallas import tpu as pltpu
from jax.sharding import PartitionSpec as P

MESH = pl.DeviceIdType.MESH
KAPPA = 0.1
STEPS = 3
LEV = 75
PAD = 80
CX = 4
CY = 128
CELLS = CX * CY
HID = 1024
ROWS = 240
TILES = 32
NZ = 16
CHIPS = 16
COLUMNS = 262144
REACH = 3
WIDE = CX + 2 * REACH
STRIP = 4 * REACH
LATS = 16 * 3
CORNER = 16
EDGE = LATS + 2 * CORNER
NORTH_AT = (0, 1, 10, 11)
EAST_AT = (2, 6, 8, 9)
CELL_AT = (3, 4, 5, 7)
BLK = 256
STEPS_XY = tuple((dx, dy) for dx in (2, 1, 3, 0) for dy in (2, 1, 3, 0) if dx or dy)
STEPS_Z = (8, 7, 9, 6, 10, 5, 11, 4, 12, 3, 13, 2, 14, 1, 15)
F32 = jnp.float32
BF16 = jnp.bfloat16
VMEM_LIMIT = 40 * 1024 * 1024


def place(p):
    return lax.div(p, 8), lax.rem(p, 8)


def faces(opened, speed):
    near = jnp.where(opened, jnp.maximum(speed, 0.0) + KAPPA, 0.0)
    far = jnp.where(opened, jnp.minimum(speed, 0.0) - KAPPA, 0.0)
    return near, far


def dot(a, b, dims):
    return lax.dot_general(a, b, (dims, ((), ())), preferred_element_type=F32)


def main_kernel(
    tracer_hbm, east_hbm, north_hbm, target_hbm, depth_hbm, w1_hbm, b1_hbm, w2_hbm, b2_hbm,
    tracer_out, misfit_out, w1_out, b1_out, w2_out, b2_out,
    tracer_ref, east_ref, north_ref, target_ref, depth_ref, w1_ref, b1_ref, w2_ref, b2_ref,
    cells, north_own, east_own, rows_out, edges_out, halo_w, halo_e, halo_edges, pick_out, pick_rows, pick_edges,
    staged, fresh, misfits, gathered, feat, weights, hidden, slope, total, wanted, chunks, core_in, sending, landed,
    mine, strips, strips_in, strips_all, chunk,
    load_sems, halo_send, halo_recv, core_send, core_recv, send_sems, recv_sems, scatter_recv,
    gather_send, gather_recv, forward_send, forward_recv, known_tiles, known_ring,
):
    z, x, m = lax.axis_index("ocx"), lax.axis_index("ocy"), lax.axis_index("ml")
    core = lax.rem(m, 2)
    chip = x * 4 + lax.div(m, 2)
    p = x * 8 + m
    sibling = (z, x, m + 1 - 2 * core)

    def other_chip(dx, dy):
        to_x, to_m = lax.rem(x + dx, 4), lax.rem(m + 2 * dy, 8)
        return to_x * 4 + lax.div(to_m, 2), (z, to_x, to_m)

    def ring(k):
        w = lax.rem(z + k, NZ)
        return w, (w, x, m)

    def tile(k):
        return (z, *place(lax.rem(p + k, TILES)))

    to_e, to_w = ring(1)[1], ring(NZ - 1)[1]
    to_n, to_s = tile(1), tile(TILES - 1)

    pairs = (
        (depth_hbm, depth_ref), (tracer_hbm, tracer_ref.at[0:LEV]), (north_hbm, north_ref.at[0:LEV]), (east_hbm, east_ref.at[0:LEV]),
        (target_hbm, target_ref), (w1_hbm, w1_ref), (b1_hbm, b1_ref), (w2_hbm, w2_ref), (b2_hbm, b2_ref),
    )
    loads = [pltpu.make_async_copy(src, dst, load_sems.at[i]) for i, (src, dst) in enumerate(pairs)]
    for load in loads[:4]:
        load.start()

    barrier = pltpu.get_barrier_semaphore()

    def signal(target):
        pl.semaphore_signal(barrier, inc=1, device_id=target, device_id_type=MESH)

    def diagonal(dz, k):
        return (lax.rem(z + dz, NZ), *tile(k)[1:])

    to_ne, to_nw = diagonal(1, 1), diagonal(NZ - 1, 1)
    to_se, to_sw = diagonal(1, TILES - 1), diagonal(NZ - 1, TILES - 1)
    for target in (to_e, to_w, to_n, to_s, to_ne, to_nw, to_se, to_sw):
        signal(target)
    for load in loads[4:]:
        load.start()

    def spread_word(known, number, ahead, behind):
        for target in (ahead, behind):
            pl.semaphore_signal(known.at[number], inc=1, device_id=target, device_id_type=MESH)

    def spread_tiles(number):
        spread_word(known_tiles, number, tile(1 << number), tile(TILES - (1 << number)))

    def spread_ring(number):
        spread_word(known_ring, number, ring(1 << number)[1], ring(NZ - (1 << number))[1])

    def remote(src, dst, send_sem, recv_sem, target):
        return pltpu.make_async_remote_copy(
            src_ref=src, dst_ref=dst, send_sem=send_sem, recv_sem=recv_sem,
            device_id=target, device_id_type=MESH,
        )

    def whole(ref, number):
        return remote(ref, ref, send_sems.at[number], recv_sems.at[number], sibling)

    def halo(src, dst, number, target):
        copy = remote(src, dst, halo_send.at[number], halo_recv.at[number], target)
        copy.start()
        return copy

    item = lax.broadcasted_iota(jnp.int32, (2 * EDGE, CY), 0)
    lane_in = lax.broadcasted_iota(jnp.int32, (2 * EDGE, CY), 1)
    southern = item >= EDGE
    item = jnp.where(southern, item - EDGE, item)
    nth = jnp.where(southern, lane_in, lane_in - (CY - REACH))
    key = jnp.where(jnp.logical_and(nth >= 0, nth < REACH), item - nth, -999)
    nth = jnp.where(southern, nth, nth - 1)
    corner_key = jnp.where(jnp.logical_and(nth >= 0, nth < 2), item - nth, -999)
    for f, order in enumerate((CELL_AT, EAST_AT, NORTH_AT)):
        for i in range(CX):
            at = slice(CY * order[i], CY * (order[i] + 1))
            first = LATS + 4 * f + (2 * (i - 2) if i >= 2 else CORNER + 2 * i)
            hit = jnp.logical_or(key == 16 * f + 4 * i, corner_key == first)
            pick_out[:, at] = jnp.where(hit, 1.0, 0.0).astype(BF16)

    level = lax.broadcasted_iota(jnp.int32, (PAD, CY), 0).astype(F32)
    lane = lax.broadcasted_iota(jnp.int32, (PAD, CY), 1)
    tail = lax.broadcasted_iota(jnp.int32, (PAD - LEV, CY), 0)
    none = jnp.zeros((PAD - LEV, CY), F32)
    for load in loads[:4]:
        load.wait()
    depth = [depth_ref[i : i + 1, :].astype(F32) for i in range(CX)]
    for i in range(CX):
        cells[i, 0:LEV, :] = tracer_ref[0:LEV, i, :]
        cells[i, LEV:PAD, :] = jnp.where(tail == 0, depth[i], 0.0)
        north_own[i, 0:LEV, :] = north_ref[0:LEV, i, :]
        north_own[i, LEV:PAD, :] = none
        east_own[i, 0:LEV, :] = east_ref[0:LEV, i, :]
        east_own[i, LEV:PAD, :] = none
        rows_out[CELL_AT[i]] = cells[i].astype(BF16)
        rows_out[EAST_AT[i]] = east_own[i].astype(BF16)
        rows_out[NORTH_AT[i]] = north_own[i].astype(BF16)
    pl.semaphore_wait(barrier, 8)
    copies = [halo(rows_out.at[4:12], halo_w, 0, to_e), halo(rows_out.at[0:7], halo_e, 1, to_w)]
    spread_tiles(0)
    spread_ring(0)
    sources = jnp.concatenate([rows_out[n] for n in range(3 * CX)], axis=1)
    sources = jnp.concatenate([sources, jnp.zeros((CY - PAD, 3 * CX * CY), BF16)], axis=0)
    edges_out[...] = dot(pick_out[...], sources, ((1,), (1,))).astype(BF16)
    to_east, to_west = slice(LATS, LATS + CORNER), slice(LATS + CORNER, EDGE)
    for side, targets in enumerate(((to_n, to_ne, to_nw), (to_s, to_se, to_sw))):
        for n, some in enumerate((slice(0, LATS), to_east, to_west)):
            mine_at = edges_out.at[EDGE * side + some.start : EDGE * side + some.stop]
            there_at = halo_edges.at[EDGE * side + some.start : EDGE * side + some.stop]
            copies.append(halo(mine_at, there_at, 2 + 3 * side + n, targets[n]))

    lane_in = lax.broadcasted_iota(jnp.int32, (CY, CY), 0)
    lane_out = lax.broadcasted_iota(jnp.int32, (CY, CY), 1)
    shift = jnp.where(lane_in >= CY - REACH, lane_out - 2 * (lane_in - (CY - REACH)) + REACH, -999)
    shift = jnp.where(lane_in < REACH, lane_out - 2 * (lane_in + REACH), shift)
    shift = jnp.where(shift >= CY, shift - CY, shift)
    for n in range(WIDE):
        pick_rows[CY * n : CY * (n + 1), :] = jnp.where(shift == STRIP * n, 1.0, 0.0).astype(BF16)
    item = lax.broadcasted_iota(jnp.int32, (LATS, 3 * CY), 0)
    lane_out = lax.broadcasted_iota(jnp.int32, (LATS, 3 * CY), 1)
    shift = lane_out - (CY * (item // 16) + STRIP * (REACH + (item // 4) % 4) + 2 * (item % 4))
    shift = jnp.where(item % 4 < REACH, shift, -999)
    pick_edges[0:LATS, :] = jnp.where(shift == 0, 1.0, 0.0).astype(BF16)
    pick_edges[EDGE : EDGE + LATS, :] = jnp.where(shift == REACH, 1.0, 0.0).astype(BF16)
    item = lax.broadcasted_iota(jnp.int32, (CORNER, 3 * CY), 0)
    lane_out = lax.broadcasted_iota(jnp.int32, (CORNER, 3 * CY), 1)
    shift = lane_out - (CY * (item // 4) + STRIP * ((item // 2) % 2) + 2 * (item % 2))
    shift = jnp.where(item < 12, shift, -999)
    for n, (first, beside) in enumerate(((1, 2), (WIDE - REACH, 2), (1, REACH), (WIDE - REACH, REACH))):
        at = EDGE * (n // 2) + LATS + CORNER * (n % 2)
        pick_edges[at : at + CORNER, :] = jnp.where(shift == STRIP * first + beside, 1.0, 0.0).astype(BF16)

    masks = [level[0:LEV, :] < depth[i] for i in range(CX)]
    for i in range(CX):
        at = slice(CY * i, CY * (i + 1))
        feat[LEV : 2 * LEV, at] = jnp.where(masks[i], east_own[i, 0:LEV, :], 0.0)
        feat[2 * LEV : 3 * LEV, at] = jnp.where(masks[i], north_own[i, 0:LEV, :], 0.0)
    last = lax.broadcasted_iota(jnp.int32, (ROWS - 3 * LEV, CELLS), 0)
    feat[3 * LEV : ROWS, :] = jnp.where(last < 2, 1.0, 0.0)
    pl.semaphore_wait(known_tiles.at[0], 2)
    spread_tiles(1)
    pl.semaphore_wait(known_ring.at[0], 2)
    spread_ring(1)
    for load in loads[4:]:
        load.wait()
    wanted[0:LEV] = target_ref[...].astype(F32)
    edge = 3 * LEV // 16 * 16
    weights[0:edge, :] = w1_ref[0:edge, :]
    bias = b1_ref[...]
    coarse = bias.astype(BF16).astype(F32)
    row = lax.broadcasted_iota(jnp.int32, (ROWS - edge, HID), 0) + edge
    final = jnp.where(row == 3 * LEV - 1, w1_ref[3 * LEV - 1 : 3 * LEV, :].astype(F32), 0.0)
    final = jnp.where(row == 3 * LEV, coarse, final)
    final = jnp.where(row == 3 * LEV + 1, bias - coarse, final)
    weights[edge:ROWS, :] = final.astype(BF16)

    pl.semaphore_wait(known_tiles.at[1], 2)
    spread_tiles(2)
    for copy in copies:
        copy.wait_recv()

    cell_rows = [halo_w[0], halo_w[1], halo_w[3]] + [rows_out[n] for n in CELL_AT] + [halo_e[3], halo_e[4], halo_e[5]]
    east_rows = [halo_w[2], halo_w[4], halo_w[5]] + [rows_out[n] for n in EAST_AT] + [halo_e[2], halo_e[6]]
    north_rows = [halo_w[6], halo_w[7]] + [rows_out[n] for n in NORTH_AT] + [halo_e[0], halo_e[1]]
    beyond = dot(halo_edges[...], pick_edges[...], ((0,), (0,)))[0:PAD, :]

    def strip_of(some, first, f):
        own = dot(
            jnp.concatenate(some, axis=1), pick_rows[CY * first : CY * (first + len(some)), :], ((1,), (0,))
        )
        return own + beyond[:, CY * f : CY * (f + 1)]

    def turn(value, by):
        by = by % CY
        return pltpu.roll(value, by, 1) if by else value

    strip = strip_of(cell_rows, 0, 0)
    deep_here = jnp.broadcast_to(strip[LEV : LEV + 1, :], (PAD, CY))
    near_e, far_e = faces(level < jnp.minimum(deep_here, turn(deep_here, -STRIP)), strip_of(east_rows, 0, 1))
    at_south = jnp.logical_and(lane % STRIP == 2 * (REACH - 1), p == 0)
    at_north = jnp.logical_and(lane % STRIP == 2 * (REACH - 1) - REACH, p == TILES - 1)
    shut = jnp.logical_or(at_south, at_north)
    opened = jnp.logical_and(level < jnp.minimum(deep_here, turn(deep_here, -2)), jnp.logical_not(shut))
    strip_near, strip_far = faces(opened, strip_of(north_rows, 1, 2))
    near_w, far_w = turn(near_e, STRIP), turn(far_e, STRIP)
    near_s, far_s = turn(strip_near, 2), turn(strip_far, 2)
    strip_coef = (1.0 + far_w - near_e + far_s - strip_near, near_w, far_e, near_s, strip_far)
    strips_at = [strip]
    for step in range(STEPS - 1):
        keep, near_w, far_e, near_s, far_n = strip_coef
        strip = (
            keep * strip + near_w * turn(strip, STRIP) - far_e * turn(strip, -STRIP)
            + near_s * turn(strip, 2) - far_n * turn(strip, -2)
        )
        strips_at.append(strip)

    now = [
        cells[n - REACH] if REACH <= n < REACH + CX else cell_rows[n].astype(F32) for n in range(WIDE)
    ]
    deep = [jnp.broadcast_to(value[LEV : LEV + 1, :], (PAD, CY)) for value in now]
    east_faces = []
    for n in range(WIDE - 1):
        speed = east_own[n - REACH] if REACH <= n < REACH + CX else east_rows[n].astype(F32)
        east_faces.append(faces(level < jnp.minimum(deep[n], deep[n + 1]), speed))
    coef = [None] * WIDE
    for n in range(1, WIDE - 1):
        speed = north_own[n - REACH] if REACH <= n < REACH + CX else north_rows[n - 1].astype(F32)
        near_n, far_n = faces(level < jnp.minimum(deep[n], turn(deep[n], -1)), speed)
        edge_at = -(STRIP * n + 2)
        near_n = jnp.where(lane == CY - 1, turn(strip_near, edge_at), near_n)
        far_n = jnp.where(lane == CY - 1, turn(strip_far, edge_at), far_n)
        beyond_at = -(STRIP * n + 2 * (REACH - 1))
        near_s = jnp.where(lane == 0, turn(strip_near, beyond_at), turn(near_n, 1))
        far_s = jnp.where(lane == 0, turn(strip_far, beyond_at), turn(far_n, 1))
        near_w, far_w = east_faces[n - 1]
        near_e, far_e = east_faces[n]
        coef[n] = (1.0 + far_w - near_e + far_s - near_n, near_w, far_e, near_s, far_n)
    for step in range(STEPS):
        after = list(now)
        for n in range(step + 1, WIDE - 1 - step):
            keep, near_w, far_e, near_s, far_n = coef[n]
            past = turn(strips_at[step], -(STRIP * n + 2 * (REACH - 1)))
            south = jnp.where(lane == 0, past, turn(now[n], 1))
            north = jnp.where(lane == CY - 1, past, turn(now[n], -1))
            after[n] = (
                keep * now[n] + near_w * now[n - 1] - far_e * now[n + 1] + near_s * south - far_n * north
            )
        now = after
    for i in range(CX):
        cells[i] = now[REACH + i]
    pl.semaphore_wait(known_tiles.at[2], 2)
    spread_tiles(3)
    for i in range(CX):
        at = slice(CY * i, CY * (i + 1))
        feat[0:LEV, at] = jnp.where(masks[i], cells[i, 0:LEV, :], 0.0)
    inputs = feat[...].astype(BF16)

    acc = None
    for b in range(HID // BLK):
        at = slice(b * BLK, (b + 1) * BLK)
        before = dot(weights[:, at], inputs, ((0,), (0,)))
        stash = before.astype(BF16).astype(F32)
        gate = 0.5 * jnp.tanh(0.5 * stash) + 0.5
        act = (stash * gate).astype(BF16)
        hidden[at, :] = act
        slope[at, :] = gate * (1.0 + stash * (1.0 - gate))
        part = dot(w2_ref[:, at], act, ((1,), (0,)))
        acc = part if acc is None else acc + part
    pl.semaphore_wait(known_ring.at[1], 2)
    spread_ring(2)
    eye = lax.broadcasted_iota(jnp.int32, (LEV, LEV), 0) == lax.broadcasted_iota(jnp.int32, (LEV, LEV), 1)
    bias2 = jnp.sum(jnp.where(eye, b2_ref[...], 0.0), axis=1, keepdims=True)
    output = acc + bias2
    total[...] = jnp.zeros((PAD, CELLS), F32)
    for i in range(CX):
        at = slice(CY * i, CY * (i + 1))
        tendency = jnp.where(masks[i], output[:, at], 0.0).astype(BF16).astype(F32)
        goal = jnp.where(masks[i], wanted[0:LEV, i, :], 0.0)
        misfit = tendency - goal
        total[0:LEV, at] = misfit * (1.0 / COLUMNS)
        fresh[i, 0:LEV, :] = cells[i, 0:LEV, :] + tendency
        misfits[i, 0:LEV, :] = misfit
    d_out = total[...].astype(BF16)
    ones = jnp.ones((16, CELLS), BF16)
    bias_grad = dot(ones, d_out, ((1,), (1,)))
    spread = lax.broadcasted_iota(jnp.int32, (PAD, CY), 0) == LEV
    per = BLK // CY
    to_sibling = []
    for b in range(HID // BLK):
        at = slice(b * BLK, (b + 1) * BLK)
        d_hidden = dot(w2_ref[:, at], d_out[0:LEV, :], ((0,), (0,)))
        d_before = (d_hidden * slope[at, :]).astype(BF16)
        g1 = dot(inputs, d_before, ((1,), (1,)))
        g2 = dot(d_out, hidden[at, :], ((1,), (1,)))
        for t in range(per):
            lanes = slice(t * CY, (t + 1) * CY)
            tile = b * per + t
            for g in range(3):
                chunks[g % 2, 2 * tile + g // 2] = g1[PAD * g : PAD * (g + 1), lanes]
            last_part = g2[:, lanes]
            if tile == 0:
                row = jnp.concatenate([bias_grad[0:1, :], jnp.zeros((1, CY - PAD), F32)], axis=1)
                last_part = jnp.where(spread, row, last_part)
            chunks[1, 2 * tile + 1] = last_part
        some = pl.ds(2 * per * b, 2 * per)
        copy = remote(chunks.at[1 - core, some], core_in.at[some], core_send.at[b], core_recv.at[b], sibling)
        copy.start()
        to_sibling.append(copy)
    row = lax.broadcasted_iota(jnp.int32, (PAD, CY), 0)
    bias_row = 3 * LEV - 2 * PAD + core * (LEV - (3 * LEV - 2 * PAD))
    for b in range(HID // BLK):
        to_sibling[b].wait_recv()
        some = pl.ds(2 * per * b, 2 * per)
        both = chunks[core, some] + core_in[some]
        for j in range(2 * per):
            value = both[j]
            sent = value
            if j % 2:
                low = value - value.astype(BF16).astype(F32)
                sent = jnp.where(row == bias_row + 1, pltpu.roll(low, 1, 0), value)
            sending[2 * per * b + j] = sent.astype(BF16)

    pl.semaphore_wait(known_tiles.at[3], 2)

    for n, (dx, dy) in enumerate(STEPS_XY):
        c, target = other_chip(dx, dy)
        remote(sending.at[c], landed.at[n], send_sems.at[0], scatter_recv.at[n // 4], target).start()
    for i in range(CX):
        staged[0:LEV, i, :] = fresh[i, 0:LEV, :]
        wanted[0:LEV, i, :] = misfits[i, 0:LEV, :]
    tracer_out[...] = staged[0:LEV]
    misfit_out[...] = wanted[0:LEV].astype(BF16)
    has_bias = lax.rem(chip, 2) == 1
    amount = chunks[core, chip] + core_in[chip]
    amount = jnp.where(jnp.logical_and(row == bias_row + 1, has_bias), 0.0, amount)
    for group in range(4):
        some = landed.at[4 * group : min(4 * group + 4, CHIPS - 1)]
        remote(some, some, send_sems.at[0], scatter_recv.at[group], sibling).wait_recv()
        for k in range(4 * group, min(4 * group + 4, CHIPS - 1)):
            amount = amount + landed[k].astype(F32)
    mine[...] = amount
    part = PAD // NZ
    for k in range(NZ):
        strips[k] = mine[part * k : part * (k + 1), :]

    pl.semaphore_wait(known_ring.at[2], 2)
    for n, k in enumerate(STEPS_Z):
        w, target = ring(k)
        remote(strips.at[w], strips_in.at[n], send_sems.at[1], recv_sems.at[1], target).start()
    whole(strips_in, 1).wait_recv()
    strip = strips[z]
    for n in range(NZ - 1):
        strip = strip + strips_in[n]
    strips_all[z] = strip
    for k in STEPS_Z:
        _, target = ring(k)
        remote(strips_all.at[z], strips_all.at[z], send_sems.at[2], recv_sems.at[2], target).start()
    whole(strips_in, 2).wait_recv()
    for k in range(NZ):
        mine[part * k : part * (k + 1), :] = strips_all[k]
    value = mine[...]
    both = jnp.where(jnp.logical_and(row == bias_row, has_bias), pltpu.roll(value, PAD - 1, 0), 0.0) + value
    low = both - both.astype(BF16).astype(F32)
    both = jnp.where(jnp.logical_and(row == bias_row + 1, has_bias), pltpu.roll(low, 1, 0), both)
    chunk[...] = both.astype(BF16)
    gathered[core, 0] = chunk[...]
    forwards = []
    for dx in (2, 1, 3, 0):
        for dy in (2, 1, 3, 0):
            if dx or dy:
                _, target = other_chip(dx, dy)
                slot = gathered.at[core, 4 * dx + dy]
                remote(chunk, slot, gather_send.at[dx], gather_recv.at[dx], target).start()
    for dx in (2, 1, 3, 0):
        some = gathered.at[core, 4 * dx + (dx == 0) : 4 * dx + 4]
        remote(some, some, gather_send.at[dx], gather_recv.at[dx], sibling).wait_recv()
        some = gathered.at[core, 4 * dx : 4 * dx + 4]
        forwards.append(remote(some, some, forward_send.at[dx], forward_recv.at[dx], sibling))
        forwards[-1].start()

    def unpack(half):
        rest = 3 * LEV - 2 * PAD
        y = lax.div(m, 2)
        for t in range(HID // CY):
            lanes = slice(t * CY, (t + 1) * CY)
            from_x = lax.rem(x + 4 - t // 2, 4) * 4
            first = from_x + lax.rem(y + 4 - 2 * (t % 2), 4)
            second = from_x + lax.rem(y + 3 - 2 * (t % 2), 4)
            w1_out[PAD * half : PAD * (half + 1), lanes] = gathered[half, first].astype(F32)
            value = gathered[half, second].astype(F32)
            if half == 0:
                w1_out[2 * PAD : 3 * LEV, lanes] = value[0:rest, :]
                b1_out[:, lanes] = value[rest : rest + 1, :] + value[rest + 1 : rest + 2, :]
            else:
                w2_out[:, lanes] = value[0:LEV, :]
                if t == 0:
                    b2_out[...] = value[LEV : LEV + 1, 0:LEV] + value[LEV + 1 : LEV + 2, 0:LEV]

    for half in range(2):
        pl.when(core == half)(functools.partial(unpack, half))
    for copy in copies + to_sibling:
        copy.wait_send()
    whole(landed, 0).wait_send()
    whole(strips_in, 1).wait_send()
    whole(strips_in, 2).wait_send()
    for dx in (2, 1, 3, 0):
        some = gathered.at[core, 4 * dx + (dx == 0) : 4 * dx + 4]
        remote(some, some, gather_send.at[dx], gather_recv.at[dx], sibling).wait_send()
    for forward in forwards:
        forward.wait()
    for half in range(2):
        pl.when(core != half)(functools.partial(unpack, half))


def main(*operands):
    vmem = pl.BlockSpec(memory_space=pltpu.VMEM)
    hbm = pl.BlockSpec(memory_space=pltpu.HBM)
    part = PAD // NZ
    halves = HID // BLK
    return pl.pallas_call(
        main_kernel,
        out_shape=(
            jax.ShapeDtypeStruct((LEV, CX, CY), F32),
            jax.ShapeDtypeStruct((LEV, CX, CY), BF16),
            jax.ShapeDtypeStruct((3 * LEV, HID), F32),
            jax.ShapeDtypeStruct((1, HID), F32),
            jax.ShapeDtypeStruct((LEV, HID), F32),
            jax.ShapeDtypeStruct((1, LEV), F32),
        ),
        in_specs=[hbm] * 9,
        out_specs=(vmem,) * 6,
        scratch_shapes=[pltpu.VMEM((PAD, CX, CY), F32)] * 3
        + [pltpu.VMEM(a.shape, a.dtype) for a in operands[3:]]
        + [
            pltpu.VMEM((CX, PAD, CY), F32),
            pltpu.VMEM((CX, PAD, CY), F32),
            pltpu.VMEM((CX, PAD, CY), F32),
            pltpu.VMEM((3 * CX, PAD, CY), BF16),
            pltpu.VMEM((2 * EDGE, CY), BF16),
            pltpu.VMEM((8, PAD, CY), BF16),
            pltpu.VMEM((7, PAD, CY), BF16),
            pltpu.VMEM((2 * EDGE, CY), BF16),
            pltpu.VMEM((2 * EDGE, 3 * CX * CY), BF16),
            pltpu.VMEM((WIDE * CY, CY), BF16),
            pltpu.VMEM((2 * EDGE, 3 * CY), BF16),
            pltpu.VMEM((PAD, CX, CY), F32),
            pltpu.VMEM((CX, PAD, CY), F32),
            pltpu.VMEM((CX, PAD, CY), F32),
            pltpu.VMEM((2, CHIPS, PAD, CY), BF16),
            pltpu.VMEM((ROWS, CELLS), F32),
            pltpu.VMEM((ROWS, HID), BF16),
            pltpu.VMEM((HID, CELLS), BF16),
            pltpu.VMEM((HID, CELLS), F32),
            pltpu.VMEM((PAD, CELLS), F32),
            pltpu.VMEM((PAD, CX, CY), F32),
            pltpu.VMEM((2, CHIPS, PAD, CY), F32),
            pltpu.VMEM((CHIPS, PAD, CY), F32),
            pltpu.VMEM((CHIPS, PAD, CY), BF16),
            pltpu.VMEM((CHIPS - 1, PAD, CY), BF16),
            pltpu.VMEM((PAD, CY), F32),
            pltpu.VMEM((NZ, part, CY), F32),
            pltpu.VMEM((NZ - 1, part, CY), F32),
            pltpu.VMEM((NZ, part, CY), F32),
            pltpu.VMEM((PAD, CY), BF16),
            pltpu.SemaphoreType.DMA((len(operands),)),
            pltpu.SemaphoreType.DMA((8,)),
            pltpu.SemaphoreType.DMA((8,)),
            pltpu.SemaphoreType.DMA((halves,)),
            pltpu.SemaphoreType.DMA((halves,)),
            pltpu.SemaphoreType.DMA((3,)),
            pltpu.SemaphoreType.DMA((3,)),
            pltpu.SemaphoreType.DMA((4,)),
            pltpu.SemaphoreType.DMA((4,)),
            pltpu.SemaphoreType.DMA((4,)),
            pltpu.SemaphoreType.DMA((4,)),
            pltpu.SemaphoreType.DMA((4,)),
            pltpu.SemaphoreType.REGULAR((4,)),
            pltpu.SemaphoreType.REGULAR((3,)),
        ],
        compiler_params=pltpu.CompilerParams(
            collective_id=0, has_side_effects=True, vmem_limit_bytes=VMEM_LIMIT
        ),
        name="main",
    )(*(pltpu.with_memory_space_constraint(a, pltpu.HBM) for a in operands))


def store_kernel(*refs):
    count = len(refs) // 2
    copies = [pltpu.make_async_copy(refs[i], refs[count + i], refs[-1].at[i]) for i in (2, 4, 0, 1, 3, 5)]
    for copy in copies:
        copy.start()
    for copy in copies:
        copy.wait()


def store(*results):
    vmem = pl.BlockSpec(memory_space=pltpu.VMEM)
    hbm = pl.BlockSpec(memory_space=pltpu.HBM)
    return pl.pallas_call(
        store_kernel,
        out_shape=tuple(jax.ShapeDtypeStruct(a.shape, a.dtype) for a in results),
        in_specs=[vmem] * len(results),
        out_specs=(hbm,) * len(results),
        scratch_shapes=[pltpu.SemaphoreType.DMA((len(results),))],
        compiler_params=pltpu.CompilerParams(vmem_limit_bytes=16 * 1024 * 1024),
        name="store",
    )(*results)


def on_device(tracer, east, north, target, depth, slots, w1, b1, w2, b2):
    results = main(tracer, east, north, target, depth, w1, b1.reshape(1, HID), w2.T, b2.reshape(1, LEV))
    tracer_out, misfit_out, grad_w1, grad_b1, grad_w2, grad_b2 = store(*results)
    return tracer_out, misfit_out, grad_w1, grad_b1.reshape(HID), grad_w2.T, grad_b2.reshape(LEV)


def solution(mesh):
    grid = P(None, "ocx", ("ocy", "ml"))
    return jax.shard_map(
        on_device,
        mesh=mesh,
        in_specs=(grid, grid, grid, grid, P("ocx", ("ocy", "ml")), P("ocx", ("ocy", "ml"), None, None), P(), P(), P(), P()),
        out_specs=(grid, grid, P(), P(), P(), P()),
        check_vma=False,
    )
```
